32 devices in a mesh: dp: 4 (over y, core), mp: 8 (over z, x).
Axes of the slice: x: 2, y: 2, z: 4, core: 2. Of those that a mesh axis runs over, the one named last changes fastest.
Arguments:
- skip_stream_arriving: float32 [1024, 2304], P('dp', 'mp'), may hold values from -170 to 170
- chosen_specialists: int32 [1024, 2], P('dp'), may hold values from 0 to 3, all different within a row; in each aligned block of 256 rows (0 to 255, 256 to 511, ...) at most 160 rows name the same one
- sequence_piece_tallies: int32 [4, 4], P('dp'), may hold values from 1 to 128, 256 in all within a row
- premix_rmsnorm_gain: float32 [2304], P('mp'), may hold values from 0.1 to 1.9
- dispatcher_weights: bfloat16 [2304, 4], replicated, may hold values from -0.125 to 0.125
- specialist_switch_weights: bfloat16 [4, 2304, 5760], P(None, 'dp', 'mp'), may hold values from -0.125 to 0.125
- specialist_expand_weights: bfloat16 [4, 2304, 5760], P(None, 'dp', 'mp'), may hold values from -0.125 to 0.125
- specialist_contract_weights: bfloat16 [4, 5760, 2304], P(None, 'mp', 'dp'), may hold values from -0.109375 to 0.109375
- terminal_rmsnorm_gain: float32 [2304], replicated, may hold values from 0.1 to 1.9
- lexicon_projector_weights: bfloat16 [2304, 16384], P(None, ('dp', 'mp')), may hold values from -12 to 12
- softness_per_sequence: float32 [16], replicated, may hold values from 0.02 to 1.5
Outputs:
- new_hidden: float32 [1024, 2304], P('dp', 'mp')
- logprobs: float32 [16, 16384], P(None, ('dp', 'mp'))
The draws below stay inside these ranges and needn't reach their ends.
Inputs may be any that keep to these rules, and one draw needn't show every extreme that they name: `chosen_specialists`: in the 256 rows of each data group no expert is named by more than 160 rows, a bound that some block reaches. `sequence_piece_tallies`: each row sums to 256; its largest entry is 128.
All inputs are finite; a program needn't handle non-finite values.
Results may differ from the reference program's by a relative error of at most 0.0014.
Values may be sent and summed in bfloat16 or wider, within the bound.
No kernel may reach another device: no remote copies, remote signals or barrier semaphores. Data moves between devices by JAX's collectives and lax.ppermute only.
A program may use at most 128 MiB of HBM per device.

```python
import math
import jax
import jax.numpy as jnp
import numpy as np
from jax import lax

EMBED_DIMENSION = 2304
FF = 5760
EXPERTS = 4
TOP = 2
TOK_GRP = 256
CAP = 160
REQ_GRP = 4
TOKENS = 1024
REQS = 16
VOCAB = 16384
N_DP = 4
N_MP = 8


def draw_skip_stream_arriving(key, part):
    base_key, scale_key = jax.random.split(key, 2)
    spread = jnp.exp(jax.random.uniform(scale_key, (EMBED_DIMENSION,), jnp.float32, -1.15, 1.15))
    rising = 0.5 + jnp.arange(EMBED_DIMENSION, dtype=jnp.float32) / EMBED_DIMENSION
    values = jnp.clip(jax.random.normal(base_key, (TOKENS, EMBED_DIMENSION), jnp.float32), -6.0, 6.0)
    return values * spread * rising


def draw_lexicon_projector_weights(key, part):
    base_key, scale_key = jax.random.split(key, 2)
    column_scale = jnp.exp(jax.random.uniform(scale_key, (1, VOCAB), jnp.float32, 0.0, 2.3))
    values = jnp.clip(jax.random.normal(base_key, (EMBED_DIMENSION, VOCAB), jnp.float32), -6.0, 6.0)
    return (0.2 * values * column_scale).astype(jnp.bfloat16)


def draw_softness_per_sequence(key, part):
    return jnp.exp(jax.random.uniform(key, (REQS,), jnp.float32, -0.69, 0.405))


def spiked(array, stream_key, source, target, parts, factor):
    def block_of(axis_at):
        return (jnp.arange(array.shape[axis_at]) // (array.shape[axis_at] // parts)).reshape((-1,) + (1,) * (array.ndim - 1 - axis_at))

    first = jax.random.permutation(stream_key, parts)[block_of(target)]
    other_side = (block_of(target) + parts // 2) % parts
    return jnp.where((block_of(source) == first) | (block_of(source) == other_side), factor * array, array)


def steps_of(stream_key, shape, cuts, least, top_value):
    factor_of, own = 1.0, jax.random.fold_in(stream_key, 6)
    for axis_at, parts in cuts:
        draws = jnp.exp(jax.random.uniform(jax.random.fold_in(own, axis_at), (parts,), jnp.float32, least / len(cuts), top_value / len(cuts)))
        factor_of = factor_of * jnp.repeat(draws, shape[axis_at] // parts).reshape([-1 if axis == axis_at else 1 for axis in range(len(shape))])
    return factor_of


def length_profile(amount, total, bound, skew):
    loads = [(1 << 20) // math.isqrt(standing ** skew) + 1 for standing in range(2, amount + 1)]
    surplus, holding = total - bound - (amount - 1), [1] * (amount - 1)
    while surplus > 0:
        free = [i for i in range(amount - 1) if holding[i] < bound]
        whole, left = sum([loads[i] for i in free]), surplus
        for i in free:
            extra = min(bound - holding[i], max(1, left * loads[i] // whole), surplus)
            holding[i] = holding[i] + extra
            surplus = surplus - extra
    return np.array([bound] + holding)


def ragged(stream_key, number_of, total, most, lean):
    if number_of == 2:
        one = jax.random.randint(stream_key, (), max(1, total - most), min(most, total - 1) + 1)
        return jnp.stack([one, total - one])
    sizes = jnp.asarray(length_profile(number_of, total, most, lean), jnp.int32)
    twos = (number_of - 1) // 2
    donor, sink = sizes[1:1 + 2 * twos:2], sizes[2:2 + 2 * twos:2]
    room = jnp.minimum(donor - 1, most - sink)
    passed = jax.random.randint(jax.random.fold_in(stream_key, 1), (twos,), 0, 1 << 20) % (room + 1)
    sizes = sizes.at[1:1 + 2 * twos:2].set(donor - passed).at[2:2 + 2 * twos:2].set(sink + passed)
    return sizes[jax.random.permutation(jax.random.fold_in(stream_key, 2), number_of)]


def deal_out(stream_key, own, number, rows, amount, top, reach, slope):
    order = jax.random.permutation(stream_key, amount)
    packed, usual = shares(amount, rows * top, reach, slope, True), shares(amount, rows * top, reach, slope, False)
    places = jnp.arange(amount)

    def named(tallies, turn):
        used = int((tallies > 0).sum())
        fixed = max(1, used // 4)
        passed = fixed + (places - fixed + turn * (used - fixed)) % max(1, amount - fixed)
        return jnp.zeros((amount,), jnp.int32).at[order[jnp.where(places < fixed, places, passed)]].set(jnp.asarray(tallies, jnp.int32))

    tallies = jnp.where(number % 4 == 0, named(packed, number // 4), named(usual, number - number // 4 - 1))
    mixed = jax.random.permutation(jax.random.fold_in(own, 3), amount)
    giver, sink = mixed[0:amount // 2 * 2:2], mixed[1:amount // 2 * 2:2]
    room = jnp.minimum(tallies[giver] - 1, reach - tallies[sink]) // 2
    room = jnp.where((giver == order[0]) | (sink == order[0]) | (tallies[sink] == 0), 0, jnp.maximum(room, 0))
    passed = jax.random.randint(jax.random.fold_in(own, 4), (amount // 2,), 0, 1 << 20) % (room + 1)
    tallies = tallies.at[giver].add(-passed).at[sink].add(passed)
    items = jnp.searchsorted(jnp.cumsum(tallies), jnp.arange(rows * top), side="right").astype(jnp.int32)
    grid = items.reshape(top, rows).T
    grid = grid[jax.random.permutation(jax.random.fold_in(own, 1), rows)]
    turn = jax.random.randint(jax.random.fold_in(own, 2), (rows, 1), 0, top)
    return jnp.take_along_axis(grid, (jnp.arange(top)[None, :] + turn) % top, axis=1)


def shares(count, total, reach, slope, full):
    portions = [(1 << 20) // math.isqrt(grade ** slope) + 1 for grade in range(1, count + 1)]
    largest = reach if full else min(reach, max(-(-total // count), total * portions[0] // sum(portions)))
    least = 1 if total - largest >= count - 1 else 0
    counts, surplus = [largest] + [least] * (count - 1), total - largest - least * (count - 1)
    while surplus > 0:
        movable = [i for i in range(1, count) if counts[i] < largest] or [i for i in range(1, count) if counts[i] < reach]
        mass, budget = sum([portions[i] for i in movable]), surplus
        for i in movable:
            extra = min(reach - counts[i], max(1, budget * portions[i] // mass), surplus)
            counts[i] = counts[i] + extra
            surplus = surplus - extra
    return np.array(counts)


def bell_draw(own_key, extent, scale, most, pieces=(), held_as=jnp.bfloat16):
    loudness = steps_of(own_key, extent, pieces, -0.22, 0.18) if pieces else 1.0
    values = jax.random.normal(own_key, extent, jnp.float32) * scale * loudness
    return jnp.minimum(jnp.maximum(values, -most), most).astype(held_as)


def noise_with(key, shape, scale, most, cuts, heavy, held_as=jnp.bfloat16):
    values = scale * jax.random.normal(key, shape, jnp.float32)
    if cuts:
        values = values * steps_of(key, shape, cuts, -0.22, 0.18)
    return jnp.clip(spiked(values, jax.random.fold_in(key, 3), *heavy), -most, most).astype(held_as)


def setup_inputs(seed: int = 0) -> dict:
    streams_of = jax.random.split(jax.random.key(seed), 12)
    skip_stream_arriving = draw_skip_stream_arriving(jax.random.fold_in(streams_of[11], 71), 0)
    chosen_specialists_keys = jax.random.split(jax.random.fold_in(streams_of[1], 1), TOKENS // TOK_GRP)
    chosen_specialists_turns = jax.random.permutation(jax.random.fold_in(streams_of[1], 3), TOKENS // TOK_GRP)
    chosen_specialists = jax.vmap(lambda own, number: deal_out(jax.random.fold_in(streams_of[1], 2), own, number, TOK_GRP, EXPERTS, TOP, CAP, 2))(chosen_specialists_keys, chosen_specialists_turns).reshape((TOKENS, TOP))
    sequence_piece_tallies = jax.vmap(lambda own: ragged(own, REQ_GRP, TOK_GRP, TOK_GRP // 2, 2))(jax.random.split(streams_of[2], N_DP)).reshape((N_DP, REQ_GRP)).astype(jnp.int32)
    premix_rmsnorm_gain = jnp.clip(1.0 + 0.18 * jax.random.normal(streams_of[3], (EMBED_DIMENSION,), jnp.float32), 0.1, 1.9)
    dispatcher_weights = bell_draw(streams_of[4], (EMBED_DIMENSION, EXPERTS), EMBED_DIMENSION ** -0.5, 0.125)
    specialist_switch_weights = bell_draw(streams_of[5], (EXPERTS, EMBED_DIMENSION, FF), EMBED_DIMENSION ** -0.5, 0.125, ((1, 4), (2, 8)))
    specialist_expand_weights = bell_draw(streams_of[6], (EXPERTS, EMBED_DIMENSION, FF), EMBED_DIMENSION ** -0.5, 0.125, ((1, 4), (2, 8)))
    specialist_contract_weights = noise_with(streams_of[7], (EXPERTS, FF, EMBED_DIMENSION), FF ** -0.5, 0.109375, ((1, 8), (2, 4)), (1, 2, 8, 2.0))
    terminal_rmsnorm_gain = jnp.clip(1.0 + 0.18 * jax.random.normal(streams_of[8], (EMBED_DIMENSION,), jnp.float32), 0.1, 1.9)
    lexicon_projector_weights = draw_lexicon_projector_weights(jax.random.fold_in(streams_of[11], 71), 0)
    softness_per_sequence = draw_softness_per_sequence(jax.random.fold_in(streams_of[11], 71), 0)
    return dict(skip_stream_arriving=skip_stream_arriving, chosen_specialists=chosen_specialists, sequence_piece_tallies=sequence_piece_tallies, premix_rmsnorm_gain=premix_rmsnorm_gain, dispatcher_weights=dispatcher_weights, specialist_switch_weights=specialist_switch_weights, specialist_expand_weights=specialist_expand_weights, specialist_contract_weights=specialist_contract_weights, terminal_rmsnorm_gain=terminal_rmsnorm_gain, lexicon_projector_weights=lexicon_projector_weights, softness_per_sequence=softness_per_sequence)


branch_scale = 1.4 / math.sqrt(40.0)
epsilon = 1e-05

def slot_tables(routes_grp, expert, capacity):
    count = routes_grp.shape[0]
    hit = jnp.any(routes_grp == expert, axis=1)
    second = (routes_grp[:, 1] == expert).astype(jnp.int32)
    order = jnp.cumsum(hit.astype(jnp.int32), dtype=jnp.int32) - 1
    target = jnp.where(hit, order, capacity).astype(jnp.int32)
    tokens = jnp.arange(count, dtype=jnp.int32)
    slot_rows = jnp.zeros((capacity,), jnp.int32).at[target].set(tokens, mode='drop')
    live = jnp.zeros((capacity,), jnp.float32).at[target].set(1.0, mode='drop')
    which = jnp.zeros((capacity,), jnp.int32).at[target].set(second, mode='drop')
    return (slot_rows, live, which)

def group_branch(hidden_grp, routes_grp, premix_rmsnorm_gain, dispatcher_weights, specialist_switch_weights, specialist_expand_weights, specialist_contract_weights):
    mean_sq = lax.optimization_barrier(jnp.mean(hidden_grp * hidden_grp, axis=1, keepdims=True))
    normed = (hidden_grp * lax.rsqrt(mean_sq + epsilon) * premix_rmsnorm_gain).astype(jnp.bfloat16)
    router = jnp.dot(normed, dispatcher_weights, preferred_element_type=jnp.float32)
    mixing = jax.nn.softmax(jnp.take_along_axis(router, routes_grp, axis=1), axis=1)
    block = FF // N_MP
    partial_value = jnp.zeros((N_MP, TOK_GRP, EMBED_DIMENSION), jnp.float32)
    for expert in range(EXPERTS):
        slot_rows, live, which = slot_tables(routes_grp, expert, CAP)
        inputs = normed[slot_rows]
        gate = jnp.dot(inputs, specialist_switch_weights[expert], preferred_element_type=jnp.float32)
        up_part = jnp.dot(inputs, specialist_expand_weights[expert], preferred_element_type=jnp.float32)
        act = (jax.nn.silu(gate) * up_part).astype(jnp.bfloat16)
        blocks = act.astype(jnp.float32).reshape(CAP, N_MP, block)
        down_blocks = specialist_contract_weights[expert].astype(jnp.float32).reshape(N_MP, block, EMBED_DIMENSION)
        outputs = jnp.einsum('cjf,jfd->jcd', blocks, down_blocks)
        weight = mixing[slot_rows, which] * live
        partial_value = partial_value.at[:, slot_rows].add(outputs * weight[None, :, None])
    rounded = lax.optimization_barrier(partial_value.astype(jnp.bfloat16)).astype(jnp.float32)
    return lax.optimization_barrier(jnp.sum(rounded, axis=0))

def reference(skip_stream_arriving, chosen_specialists, sequence_piece_tallies, premix_rmsnorm_gain, dispatcher_weights, specialist_switch_weights, specialist_expand_weights, specialist_contract_weights, terminal_rmsnorm_gain, lexicon_projector_weights, softness_per_sequence):

    def one_group(pair):
        return group_branch(pair[0], pair[1], premix_rmsnorm_gain, dispatcher_weights, specialist_switch_weights, specialist_expand_weights, specialist_contract_weights)
    branch = lax.map(one_group, (skip_stream_arriving.reshape(N_DP, TOK_GRP, EMBED_DIMENSION), chosen_specialists.reshape(N_DP, TOK_GRP, TOP)))
    new_hidden = skip_stream_arriving + branch_scale * branch.reshape(TOKENS, EMBED_DIMENSION)
    offsets = (jnp.arange(N_DP, dtype=jnp.int32) * TOK_GRP)[:, None]
    ends_index = (jnp.cumsum(sequence_piece_tallies, axis=1, dtype=jnp.int32) - 1 + offsets).reshape(-1).astype(jnp.int32)
    ends = new_hidden[ends_index]
    end_sq = lax.optimization_barrier(jnp.mean(ends * ends, axis=1, keepdims=True))
    lexicon_projector_feed = (ends * lax.rsqrt(end_sq + epsilon) * terminal_rmsnorm_gain).astype(jnp.bfloat16)
    lexicon_logit_values = jnp.dot(lexicon_projector_feed, lexicon_projector_weights, preferred_element_type=jnp.float32) / (EMBED_DIMENSION / 256.0 * softness_per_sequence[:, None])
    largest = lax.optimization_barrier(jnp.max(lexicon_logit_values, axis=1, keepdims=True))
    total_exp = lax.optimization_barrier(jnp.sum(jnp.exp(lexicon_logit_values - largest), axis=1, keepdims=True))
    logprobs = lexicon_logit_values - largest - jnp.log(total_exp)
    return (new_hidden, logprobs)
```

```python
import math

import jax
import jax.numpy as jnp
from jax import lax
from jax.experimental import pallas as pl
from jax.experimental.pallas import tpu as pltpu
from jax.sharding import PartitionSpec as P

WIDTH = 2304
META = 16
branch_scale = 1.4 / math.sqrt(40.0)
epsilon = 1e-05
f32, bf16 = jnp.float32, jnp.bfloat16

VMEM = pl.BlockSpec(memory_space=pltpu.VMEM)
SMEM = pl.BlockSpec(memory_space=pltpu.SMEM)


def split3(v):
    hi = lax.reduce_precision(v, 8, 7)
    mid = lax.reduce_precision(v - hi, 8, 7)
    return hi, mid, v - hi - mid


def route_rows(core, meta):
    first, second = meta[0:1].astype(f32), meta[1:2].astype(f32)
    zero = core == 0
    return jnp.where(zero, first, second), jnp.where(zero, second, first)


def hi_lo(m):
    hi = m.astype(bf16)
    lo = (m - hi.astype(f32)).astype(bf16)
    return jnp.concatenate([hi.astype(f32), lo.astype(f32)], axis=0).astype(bf16)


def partial_kernel(scal, *refs):
    *blocks, wr, wg, wu, own, send, xs = refs
    near = blocks[0]
    n = pl.program_id(0)
    core, side = scal[0], scal[1]
    experts, tile, _ = wg.shape
    block = near.shape[0] - META
    hidden = (own.shape[0] - META) // 2

    @pl.when(n == 0)
    def _():
        for i, ref in enumerate(blocks):
            xs[pl.ds(pl.multiple_of((side ^ i) * block, 16), block)] = ref[0:block]
        router = jnp.dot(wr[...], xs[...], preferred_element_type=f32)
        sq = jnp.zeros((1, near.shape[1]), f32)
        for ref in blocks:
            for row in (4, 3, 2):
                sq = sq + ref[block + row : block + row + 1].astype(f32)
        m = jnp.concatenate([sq, router[0:7]], axis=0)
        own[2 * hidden : 2 * hidden + 8] = m
        own[2 * hidden + 8 : 2 * hidden + 16] = jnp.zeros_like(m)
        send[2 * hidden :] = hi_lo(m)

    mine, other = route_rows(core, near[block:])
    x = xs[...]
    for which, w in ((0, wg), (1, wu)):
        a = b = None
        for e in range(experts):
            d = jnp.dot(w[e], x, preferred_element_type=f32)
            a = d if a is None else jnp.where(mine == e, d, a)
            b = d if b is None else jnp.where(other == e, d, b)
        at = pl.ds(pl.multiple_of(which * hidden + n * tile, 16), tile)
        own[at] = a
        send[at] = b.astype(bf16)


def half_kernel(scal, own, recv, keep, send):
    y = scal[0]
    rows = own.shape[0] - META
    half = keep.shape[1]

    def halves(v):
        lo, hi = v[:, :half], v[:, half:]
        return jnp.where(y == 0, lo, hi), jnp.where(y == 0, hi, lo)

    step = rows // 10
    for at in range(0, rows, step):
        a, b = halves(own[at : at + step] + recv[at : at + step].astype(f32))
        keep[at : at + step] = a
        send[at : at + step] = b.astype(bf16)
    r = recv[rows:].astype(f32)
    a, b = halves(own[rows : rows + 8] + r[0:8] + r[8:16])
    keep[rows : rows + 8] = a
    keep[rows + 8 :] = jnp.zeros_like(a)
    send[rows:] = hi_lo(b)


def act_kernel(scal, keep, recv, meta, act):
    core, y = scal[0], scal[1]
    hidden, half = act.shape
    experts = 4
    mine, other = route_rows(core, meta[...])
    pick = lambda v: jnp.where(y == 0, v[:, :half], v[:, half:])
    mine, other = pick(mine), pick(other)
    r = recv[2 * hidden :].astype(f32)
    m = keep[2 * hidden : 2 * hidden + 8] + r[0:8] + r[8:16]
    scale = lax.rsqrt(m[0:1] / WIDTH + epsilon)
    la = lb = jnp.zeros_like(scale)
    for e in range(experts):
        logit = m[1 + e : 2 + e] * scale
        la = jnp.where(mine == e, logit, la)
        lb = jnp.where(other == e, logit, lb)
    mix = 1.0 / (1.0 + jnp.exp(lb - la))
    step = hidden // 5
    for at in range(0, hidden, step):
        g = (keep[at : at + step] + recv[at : at + step].astype(f32)) * scale
        up = hidden + at
        u = (keep[up : up + step] + recv[up : up + step].astype(f32)) * (scale * mix)
        act[at : at + step] = (g / (1.0 + jnp.exp(-g)) * u).astype(bf16)


def down_kernel(scal, a_near, a_far, b_near, b_far, meta, wd, out, ends, acc):
    e = pl.program_id(0)
    core, y, group = scal[0], scal[1], scal[2]
    mine, other = route_rows(core, meta[...])

    def whole(near, far):
        return jnp.concatenate(
            [jnp.where(y == 0, near[...], far[...]), jnp.where(y == 0, far[...], near[...])], axis=1
        )

    ef = e.astype(f32)
    ma = jnp.where(mine == ef, 1.0, 0.0).astype(bf16)
    mb = jnp.where(other == ef, 1.0, 0.0).astype(bf16)
    a = whole(a_near, a_far) * ma + whole(b_near, b_far) * mb
    d = jnp.dot(wd[0], a, preferred_element_type=f32)

    @pl.when(e == 0)
    def _():
        acc[...] = d

    @pl.when(e > 0)
    def _():
        acc[...] += d

    @pl.when(e == pl.num_programs(0) - 1)
    def _():
        o = acc[...].astype(bf16)
        out[...] = o
        rows = ends.shape[0]
        mark = meta[5:6].astype(f32)
        at = lax.broadcasted_iota(jnp.int32, (rows, mark.shape[1]), 0)
        want = (at - group * 4 + 1).astype(f32)
        sel = jnp.where((mark == want) & (want > 0.5) & (want < 4.5), 1.0, 0.0).astype(bf16)
        ends[...] = lax.dot_general(
            sel, o, (((1,), (1,)), ((), ())), preferred_element_type=f32
        ).astype(bf16)


def params(mib=24):
    return pltpu.CompilerParams(vmem_limit_bytes=mib * 2**20)


def partial_call(scal, blocks, wr, wg, wu):
    experts, hidden, depth = wg.shape
    rows, tokens = blocks[0].shape
    tile = hidden // 5
    full = lambda *shape: pl.BlockSpec(shape, lambda n: (0,) * len(shape))
    out_rows = 2 * hidden + META
    return pl.pallas_call(
        partial_kernel,
        grid=(hidden // tile,),
        in_specs=[
            SMEM,
            *[full(rows, tokens)] * len(blocks),
            full(*wr.shape),
            pl.BlockSpec((experts, tile, depth), lambda n: (0, n, 0)),
            pl.BlockSpec((experts, tile, depth), lambda n: (0, n, 0)),
        ],
        out_specs=[full(out_rows, tokens), full(out_rows, tokens)],
        out_shape=[
            jax.ShapeDtypeStruct((out_rows, tokens), f32),
            jax.ShapeDtypeStruct((out_rows, tokens), bf16),
        ],
        scratch_shapes=[pltpu.VMEM((depth, tokens), bf16)],
        compiler_params=params(),
        cost_estimate=pl.CostEstimate(
            flops=4 * experts * hidden * depth * tokens,
            bytes_accessed=4 * experts * hidden * depth + 6 * out_rows * tokens,
            transcendentals=0,
        ),
        name="gate_up_partial",
    )(scal, *blocks, wr, wg, wu)


def half_call(scal, own, recv):
    rows, tokens = own.shape
    shape = (rows, tokens // 2)
    return pl.pallas_call(
        half_kernel,
        in_specs=[SMEM, VMEM, VMEM],
        out_specs=[VMEM, VMEM],
        out_shape=[jax.ShapeDtypeStruct(shape, f32), jax.ShapeDtypeStruct(shape, bf16)],
        compiler_params=params(),
        cost_estimate=pl.CostEstimate(
            flops=rows * tokens, bytes_accessed=9 * rows * tokens, transcendentals=0
        ),
        name="core_sum",
    )(scal, own, recv)


def act_call(scal, keep, recv, near):
    rows, half = keep.shape
    hidden = (rows - META) // 2
    at = (near.shape[0] - META) // META
    return pl.pallas_call(
        act_kernel,
        grid=(1,),
        in_specs=[
            SMEM,
            pl.BlockSpec(keep.shape, lambda n: (0, 0)),
            pl.BlockSpec(recv.shape, lambda n: (0, 0)),
            pl.BlockSpec((META, near.shape[1]), lambda n: (at, 0)),
        ],
        out_specs=pl.BlockSpec((hidden, half), lambda n: (0, 0)),
        out_shape=jax.ShapeDtypeStruct((hidden, half), bf16),
        compiler_params=params(),
        cost_estimate=pl.CostEstimate(
            flops=8 * hidden * half, bytes_accessed=7 * rows * half, transcendentals=hidden * half
        ),
        name="act",
    )(scal, keep, recv, near)


def down_call(scal, pieces, near, wd, rows):
    experts, width, hidden = wd.shape
    tokens = near.shape[1]
    at = (near.shape[0] - META) // META
    piece = pl.BlockSpec(pieces[0].shape, lambda n: (0, 0))
    return pl.pallas_call(
        down_kernel,
        grid=(experts,),
        in_specs=[
            SMEM,
            piece,
            piece,
            piece,
            piece,
            pl.BlockSpec((META, tokens), lambda n: (at, 0)),
            pl.BlockSpec((1, width, hidden), lambda n: (n, 0, 0)),
        ],
        out_specs=[
            pl.BlockSpec((width, tokens), lambda n: (0, 0)),
            pl.BlockSpec((rows, width), lambda n: (0, 0)),
        ],
        out_shape=[
            jax.ShapeDtypeStruct((width, tokens), bf16),
            jax.ShapeDtypeStruct((rows, width), bf16),
        ],
        scratch_shapes=[pltpu.VMEM((width, tokens), f32)],
        compiler_params=params(),
        cost_estimate=pl.CostEstimate(
            flops=2 * experts * width * hidden * tokens,
            bytes_accessed=2 * experts * width * hidden + 2 * width * tokens,
            transcendentals=0,
        ),
        name="down",
    )(scal, *pieces, near, wd)


def body(
    skip_stream_arriving,
    chosen_specialists,
    sequence_piece_tallies,
    premix_rmsnorm_gain,
    dispatcher_weights,
    specialist_switch_weights,
    specialist_expand_weights,
    specialist_contract_weights,
    terminal_rmsnorm_gain,
    lexicon_projector_weights,
    softness_per_sequence,
):
    tokens, block = skip_stream_arriving.shape
    dp, mp = lax.axis_size("dp"), lax.axis_size("mp")
    parts = 4
    spread, sides = dp // parts, mp // parts
    assert dp == parts * spread and mp == parts * sides and sides & (sides - 1) == 0
    me_dp, me_mp = lax.axis_index("dp"), lax.axis_index("mp")
    part, lane = me_dp // spread, me_dp % spread
    y, core = part // 2, part % 2
    z, x = me_mp // sides, me_mp % sides

    def send(value, to):
        pairs = []
        for q in range(parts):
            for r in range(spread):
                for zz in range(parts):
                    for xx in range(sides):
                        q2, z2, x2 = to(q, zz, xx)
                        source = (q * spread + r) * mp + zz * sides + xx
                        pairs.append((source, (q2 * spread + r) * mp + z2 * sides + x2))
        return lax.ppermute(value, ("dp", "mp"), pairs)

    other_core = lambda q, zz, xx: (q ^ 1, zz, xx)
    other_y = lambda q, zz, xx: (q ^ 2, zz, xx)
    home = lambda q, zz, xx: (zz, q, xx)

    xt = (skip_stream_arriving * premix_rmsnorm_gain).T.astype(bf16)
    squares = split3(jnp.sum(skip_stream_arriving * skip_stream_arriving, axis=1))
    ends_index = jnp.cumsum(sequence_piece_tallies[0], dtype=jnp.int32) - 1
    reqs = ends_index.shape[0]
    here = jnp.arange(tokens, dtype=jnp.int32)
    mark = jnp.sum(
        jnp.where(here[None, :] == ends_index[:, None], jnp.arange(1, reqs + 1, dtype=jnp.int32)[:, None], 0),
        axis=0,
    )
    rows = [chosen_specialists[:, 0], chosen_specialists[:, 1], *squares, mark]
    meta = jnp.stack([row.astype(bf16) for row in rows])
    sent = jnp.concatenate([xt, meta, jnp.zeros((META - len(rows), tokens), bf16)], axis=0)
    feeds = [[send(sent, lambda q, zz, xx, i=i: (zz, q, xx ^ i)) for i in range(sides)]]
    for s in range(1, parts):
        shift = lambda q, zz, xx, s=s: (q, (zz - s) % parts, xx)
        feeds.append([send(v, shift) for v in feeds[0]])

    wg, wu, wd = specialist_switch_weights, specialist_expand_weights, specialist_contract_weights
    if spread > 1:
        runs = [[q * spread + r for r in range(spread)] for q in range(parts)]
        wg = lax.all_gather(wg, "dp", axis=1, tiled=True, axis_index_groups=runs)
        wu = lax.all_gather(wu, "dp", axis=1, tiled=True, axis_index_groups=runs)
        wd = lax.all_gather(wd, "dp", axis=2, tiled=True, axis_index_groups=runs)
    depth = wg.shape[1]
    short = -wg.shape[2] % 80
    wg, wu, wd = (jnp.swapaxes(w, 1, 2) for w in (wg, wu, wd))
    if short:
        wg, wu = (jnp.pad(w, ((0, 0), (0, short), (0, 0))) for w in (wg, wu))
        wd = jnp.pad(wd, ((0, 0), (0, 0), (0, short)))
    wr = lax.dynamic_slice_in_dim(dispatcher_weights, part * depth, depth).T
    wr = jnp.pad(wr, ((0, 16 - wr.shape[0]), (0, 0)))

    ints = lambda *v: jnp.stack([jnp.asarray(i, jnp.int32) for i in v])
    outs, ends = [], []
    for s in range(parts):
        own, give = partial_call(ints(core, x), feeds[s], wr, wg, wu)
        keep, give = half_call(ints(y), own, send(give, other_core))
        act = act_call(ints(core, y), keep, send(give, other_y), feeds[s][0])
        act_y = send(act, other_y)
        pieces = (act, act_y, send(act, other_core), send(act_y, other_core))
        group = (z + s) % parts
        out, end = down_call(ints(core, y, group), pieces, feeds[s][0], wd, parts * reqs)
        outs.append(out)
        ends.append(end)

    end_rows = ends[0] + ends[1] + ends[2] + ends[3]
    skip_ends = jnp.concatenate(split3(skip_stream_arriving[ends_index]), axis=0).astype(bf16)
    skip_ends = jnp.pad(skip_ends, ((0, 0), (0, depth - block)))
    message = jnp.concatenate([end_rows, skip_ends], axis=0)
    count = dp * mp
    everyone = lambda v: lax.all_to_all(
        jnp.broadcast_to(v[None], (count,) + v.shape), ("dp", "mp"), 0, 0, tiled=True
    )
    got = everyone(message).reshape(parts, spread, mp, -1, depth).astype(f32)
    all_ends = jnp.sum(got[:, :, :, : parts * reqs], axis=2).reshape(parts, spread, parts, reqs, depth)
    all_ends = all_ends.transpose(2, 1, 3, 0, 4).reshape(dp * reqs, WIDTH)
    stream = got[:, :, :, parts * reqs :, :block].reshape(parts, spread, mp, 3, reqs, block)
    stream = jnp.sum(stream, axis=3).transpose(0, 1, 3, 2, 4).reshape(dp * reqs, WIDTH)
    all_ends = stream + branch_scale * all_ends
    mean = jnp.mean(all_ends * all_ends, axis=1, keepdims=True)
    feed = (all_ends * lax.rsqrt(mean + epsilon) * terminal_rmsnorm_gain).astype(bf16)
    logits = jnp.dot(feed, lexicon_projector_weights, preferred_element_type=f32) / (
        WIDTH / 256.0 * softness_per_sequence[:, None]
    )
    top = jnp.max(logits, axis=1)
    total = jnp.sum(jnp.exp(logits - top[:, None]), axis=1)
    pairs = everyone(jnp.stack([top, total]))
    largest = jnp.max(pairs[:, 0], axis=0)
    total = jnp.sum(pairs[:, 1] * jnp.exp(pairs[:, 0] - largest), axis=0)
    logprobs = logits - largest[:, None] - jnp.log(total)[:, None]

    branch = None
    for s in range(parts):
        blocks = outs[s].reshape(sides, block, tokens)
        part_of = lambda i: lax.dynamic_index_in_dim(blocks, x ^ i, 0, keepdims=False)
        share = part_of(0).astype(f32)
        for i in range(1, sides):
            share += send(part_of(i), lambda q, zz, xx, i=i: (q, zz, xx ^ i)).astype(f32)
        if s:
            back = lambda q, zz, xx, s=s: (q, (zz + s) % parts, xx)
            share = send(share.astype(bf16), back).astype(f32)
        branch = share if branch is None else branch + share
    new_hidden = skip_stream_arriving + branch_scale * send(branch, home).T
    return (new_hidden, logprobs)


def solution(mesh):
    return jax.shard_map(
        body,
        mesh=mesh,
        in_specs=(
            P("dp", "mp"),
            P("dp", None),
            P("dp", None),
            P("mp"),
            P(),
            P(None, "dp", "mp"),
            P(None, "dp", "mp"),
            P(None, "mp", "dp"),
            P(),
            P(None, ("dp", "mp")),
            P(),
        ),
        out_specs=(P("dp", "mp"), P(None, ("dp", "mp"))),
        check_vma=False,
    )
```

```python
import math

import jax
import jax.numpy as jnp
from jax import lax
from jax.experimental import pallas as pl
from jax.experimental.pallas import tpu as pltpu
from jax.sharding import PartitionSpec as P

WIDTH = 2304
META = 16
LANES = 128
branch_scale = 1.4 / math.sqrt(40.0)
epsilon = 1e-05
f32, bf16 = jnp.float32, jnp.bfloat16

VMEM = pl.BlockSpec(memory_space=pltpu.VMEM)
SMEM = pl.BlockSpec(memory_space=pltpu.SMEM)
ANY = pl.BlockSpec(memory_space=pl.ANY)


def up_to(n, step=LANES):
    return -(-n // step) * step


def params(mib=32):
    return pltpu.CompilerParams(vmem_limit_bytes=mib * 2**20)


def cost(flops, bytes_accessed):
    return pl.CostEstimate(flops=flops, bytes_accessed=bytes_accessed, transcendentals=0)


def shape(dims, dtype):
    return jax.ShapeDtypeStruct(dims, dtype)


def prep_kernel(tallies, x, gain, routes, out, ends, wide):
    tokens, block = x.shape
    lanes = wide.shape[1]
    v = x[...]
    squares = jnp.sum(v * v, axis=1, keepdims=True)
    r = routes[...].astype(f32)
    wide[:, 0:block] = v * gain[...]
    at = lax.broadcasted_iota(jnp.int32, (tokens, lanes - block), 1)
    wide[:, block:] = jnp.where(
        at == 0, r[:, 0:1], jnp.where(at == 1, r[:, 1:2], jnp.where(at == 2, squares, 0.0))
    )
    turned = wide[...].T
    out[0:block] = turned[0:block].astype(bf16)
    sq = turned[block + 2 : block + 3]
    hi = sq.astype(bf16).astype(f32)
    mid = (sq - hi).astype(bf16).astype(f32)
    here = lax.broadcasted_iota(jnp.int32, (1, tokens), 1)
    mark, end = jnp.zeros((1, tokens), f32), jnp.int32(-1)
    for q in range(ends.shape[0]):
        end = end + tallies[0, q]
        mark = jnp.where(here == end, q + 1.0, mark)
        ends[q : q + 1] = x[pl.ds(end, 1)]
    rows = [turned[block : block + 2], hi, mid, sq - hi - mid, mark]
    rows.append(jnp.zeros((META - 6, tokens), f32))
    out[block:] = jnp.concatenate(rows, axis=0).astype(bf16)


def prep_call(x, gain, routes, tallies):
    tokens, block = x.shape
    reqs = tallies.shape[1]
    return pl.pallas_call(
        prep_kernel,
        in_specs=[SMEM, VMEM, VMEM, VMEM],
        out_specs=[VMEM, VMEM],
        out_shape=[shape((block + META, tokens), bf16), shape((reqs, block), f32)],
        scratch_shapes=[pltpu.VMEM((tokens, up_to(block + META)), f32)],
        compiler_params=params(),
        cost_estimate=cost(4 * tokens * block, 6 * tokens * block),
        name="prep",
    )(tallies, x, gain[None], routes)


def partial_kernel(sides, held, scal, *refs):
    feeds, refs = refs[:held], refs[held:]
    wr0, wr1, wg, wu, rg, ru = refs[:6]
    own, give, meta, cols, xs, xt, acc = refs[-7:]
    e = pl.program_id(0)
    core, side, y = scal[0], scal[1], scal[2]
    depth, half = rg.shape[1], rg.shape[2]
    deep = up_to(depth)
    tokens = xt.shape[0]
    block = depth // sides

    @pl.when(e == 0)
    def _():
        xs[...] = jnp.zeros_like(xs)
        sq = jnp.zeros((1, tokens), f32)
        each = 2 * sides // held
        for n in range(2 * sides):
            ref, at = feeds[n // each], (n % each) * (block + META)
            which, i = n // sides, n % sides
            row = which * deep + (side ^ i) * block
            xs[pl.ds(pl.multiple_of(row, 16), block)] = ref[at : at + block]
            row = 2 * deep + META * n
            xs[row : row + META] = ref[at + block : at + block + META]
            for term in (4, 3, 2):
                sq = sq + ref[at + block + term : at + block + term + 1].astype(f32)
        router = jnp.dot(wr0[...], xs[0:depth], preferred_element_type=f32)
        router += jnp.dot(wr1[...], xs[deep : deep + depth], preferred_element_type=f32)
        meta[...] = jnp.concatenate([sq, router[0:7]], axis=0)
        xt[...] = xs[...].T
        cols[...] = xt[:, 2 * deep :]

    routes = xt[:, 2 * deep :].astype(f32)
    ef = e.astype(f32)
    for which, (w, r) in enumerate(((wg, rg), (wu, ru))):
        d = jnp.dot(xt[:, 0:depth], w[0], preferred_element_type=f32)
        d += jnp.dot(xt[:, deep : deep + depth], r[0], preferred_element_type=f32)
        at = which * half
        for k in range(2):
            take = (routes[:, k : k + 1] == ef) | (e == 0)
            acc[k, :, at : at + half] = jnp.where(take, d, acc[k, :, at : at + half])

    @pl.when(e == pl.num_programs(0) - 1)
    def _():
        th = tokens // 2
        for k in range(2):
            own[k] = acc[k, pl.ds(pl.multiple_of(y * th, th), th)]
            give[k] = acc[k, pl.ds(pl.multiple_of((1 - y) * th, th), th)].astype(bf16)


def partial_call(scal, sides, feeds, wr, weights, swapped, deps):
    experts, depth, half = swapped[0].shape
    rows, tokens = feeds[0].shape
    deep = up_to(depth)
    full = lambda v: pl.BlockSpec(v.shape, lambda n, s: (0,) * len(v.shape))
    mine = pl.BlockSpec((1, depth, half), lambda n, s: (n, 0, s[0]))
    theirs = pl.BlockSpec((1, depth, half), lambda n, s: (n, 0, 0))
    outs = [
        shape((2, tokens // 2, 2 * half), f32),
        shape((2, tokens // 2, 2 * half), bf16),
        shape((8, tokens), f32),
        shape((tokens, LANES), bf16),
    ]
    call = pl.pallas_call(
        lambda *refs: partial_kernel(sides, len(feeds), *refs),
        grid_spec=pltpu.PrefetchScalarGridSpec(
            num_scalar_prefetch=1,
            grid=(experts,),
            in_specs=[full(v) for v in feeds]
            + [full(v) for v in wr]
            + [mine, mine, theirs, theirs]
            + [ANY] * len(deps),
            out_specs=[full(v) for v in outs],
            scratch_shapes=[
                pltpu.VMEM((2 * deep + LANES, tokens), bf16),
                pltpu.VMEM((tokens, 2 * deep + LANES), bf16),
                pltpu.VMEM((2, tokens, 2 * half), f32),
            ],
        ),
        out_shape=outs,
        compiler_params=params(),
        cost_estimate=cost(
            8 * experts * depth * half * tokens, 8 * experts * depth * half + 12 * tokens * half
        ),
        name="gate_up_partial",
    )
    return call(scal, *feeds, *wr, *weights, *swapped, *deps)


def act_kernel(scal, own, recv, meta, meta_recv, cols, *refs):
    act, turned = refs[-2:]
    y = scal[0]
    _, th, half = act.shape
    m = meta[...] + meta_recv[...]
    turned[...] = jnp.concatenate([m, jnp.zeros((LANES - 8, m.shape[1]), f32)], axis=0).T
    here = pl.ds(pl.multiple_of(y * th, th), th)
    m = turned[here]
    routes = cols[here].astype(f32)
    scale = lax.rsqrt(m[:, 0:1] / WIDTH + epsilon)
    logits = []
    for k in range(2):
        logit = jnp.zeros_like(scale)
        for e in range(4):
            logit = jnp.where(routes[:, k : k + 1] == e, m[:, 1 + e : 2 + e], logit)
        logits.append(logit * scale)
    for k in range(2):
        mix = scale / (1.0 + jnp.exp(logits[1 - k] - logits[k]))
        g = (own[k, :, 0:half] + recv[k, :, 0:half].astype(f32)) * scale
        u = (own[k, :, half:] + recv[k, :, half:].astype(f32)) * mix
        act[k] = (g / (1.0 + jnp.exp(-g)) * u).astype(bf16)


def act_call(scal, own, recv, meta, meta_recv, cols, deps):
    _, th, wide = own.shape
    return pl.pallas_call(
        act_kernel,
        in_specs=[SMEM] + [VMEM] * 5 + [ANY] * len(deps),
        out_specs=VMEM,
        out_shape=shape((2, th, wide // 2), bf16),
        scratch_shapes=[pltpu.VMEM((meta.shape[1], LANES), f32)],
        compiler_params=params(),
        cost_estimate=cost(12 * th * wide, 14 * th * wide),
        name="act",
    )(scal, own, recv, meta, meta_recv, cols, *deps)


def down_kernel(sides, scal, a, a_y, b, b_y, cols, wd, *refs):
    outs = refs[-sides - 3 : -3]
    whole, acc, turned = refs[-3:]
    e = pl.program_id(0)
    core, side, y = scal[0], scal[1], scal[2]
    _, th, half = a.shape
    hidden, width = wd.shape[1:]
    block = width // sides

    @pl.when(e == 0)
    def _():
        for mine, other, first in ((a, b, y), (a_y, b_y, 1 - y)):
            rows = pl.ds(pl.multiple_of(first * th, th), th)
            for k in range(2):
                whole[k, rows, 0:half] = jnp.where(core == 0, mine[k], other[k])
                whole[k, rows, half:] = jnp.where(core == 0, other[k], mine[k])

    ef = e.astype(f32)
    routes = cols[...].astype(f32)
    masks = [jnp.where(routes[:, k : k + 1] == ef, 1.0, 0.0).astype(bf16) for k in range(2)]
    rows = whole[0, :, 0:hidden] * masks[0] + whole[1, :, 0:hidden] * masks[1]
    d = jnp.dot(rows, wd[0], preferred_element_type=f32)

    @pl.when(e == 0)
    def _():
        acc[...] = jnp.zeros_like(acc)
        acc[:, 0:width] = d

    @pl.when(e > 0)
    def _():
        acc[:, 0:width] += d

    @pl.when(e == pl.num_programs(0) - 1)
    def _():
        turned[...] = acc[...].T
        for i in range(sides):
            rows = pl.ds(pl.multiple_of((side ^ i) * block, 16), block)
            outs[i][...] = turned[rows].astype(bf16)


def down_call(scal, sides, pieces, cols, wd, deps):
    experts, hidden, width = wd.shape
    tokens = cols.shape[0]
    half = pieces[0].shape[2]
    full = lambda v: pl.BlockSpec(v.shape, lambda n: (0,) * len(v.shape))
    outs = [shape((width // sides, tokens), bf16)] * sides
    return pl.pallas_call(
        lambda *refs: down_kernel(sides, *refs),
        grid=(experts,),
        in_specs=[SMEM]
        + [full(v) for v in pieces]
        + [full(cols), pl.BlockSpec((1, hidden, width), lambda n: (n, 0, 0))]
        + [ANY] * len(deps),
        out_specs=[full(v) for v in outs],
        out_shape=outs,
        scratch_shapes=[
            pltpu.VMEM((2, tokens, 2 * half), bf16),
            pltpu.VMEM((tokens, up_to(width)), f32),
            pltpu.VMEM((up_to(width), tokens), f32),
        ],
        compiler_params=params(),
        cost_estimate=cost(
            2 * experts * width * hidden * tokens, 2 * experts * width * hidden + 2 * width * tokens
        ),
        name="down",
    )(scal, *pieces, cols, wd, *deps)


def total_kernel(meta, stream, *refs):
    parts, (total, message) = refs[:-2], refs[-2:]
    v = parts[0][...].astype(f32)
    for ref in parts[1:]:
        v = v + ref[...].astype(f32)
    total[...] = v
    reqs = stream.shape[0]
    mark = meta[5:6].astype(f32)
    row = lax.broadcasted_iota(jnp.int32, (8, mark.shape[1]), 0)
    pick = jnp.where(mark == (row + 1).astype(f32), 1.0, 0.0)
    ends = lax.dot_general(
        pick, v, (((1,), (1,)), ((), ())), precision=lax.Precision.HIGHEST, preferred_element_type=f32
    )
    ends = stream[...] + branch_scale * ends[0:reqs]
    message[...] = jnp.broadcast_to(ends[None], message.shape)


def total_call(feed, stream, parts, block, count):
    tokens = feed.shape[1]
    full = lambda v: pl.BlockSpec(v.shape, lambda n: (0,) * len(v.shape))
    outs = [shape((block, tokens), f32), shape((count, *stream.shape), f32)]
    return pl.pallas_call(
        total_kernel,
        grid=(1,),
        in_specs=[pl.BlockSpec((META, tokens), lambda n: (block // META, 0)), full(stream)]
        + [full(v) for v in parts],
        out_specs=[full(v) for v in outs],
        out_shape=outs,
        compiler_params=params(),
        cost_estimate=cost(16 * block * tokens, 14 * block * tokens),
        name="branch_total",
    )(feed, stream, *parts)


def head_kernel(order, got, gain, words, softness, logits, message, wide):
    blocks, block = gain.shape
    rows, columns = logits.shape
    ends, squares = [], 0.0
    for b in range(blocks):
        v = jnp.concatenate([got[i] for i in order[b]], axis=0)
        squares = squares + jnp.sum(v * v, axis=1, keepdims=True)
        ends.append(v)
    scale = lax.rsqrt(squares / WIDTH + epsilon)
    total = jnp.zeros((rows, columns), f32)
    for b in range(blocks):
        feed = (ends[b] * scale * gain[b : b + 1]).astype(bf16)
        total += jnp.dot(feed, words[b * block : (b + 1) * block], preferred_element_type=f32)
    total = total / (WIDTH / 256.0 * softness[...])
    logits[...] = total
    top = jnp.max(total, axis=1, keepdims=True)
    mass = jnp.sum(jnp.exp(total - top), axis=1, keepdims=True)
    wide[...] = jnp.zeros_like(wide)
    lane = lax.broadcasted_iota(jnp.int32, (rows, LANES), 1)
    wide[0:rows] = jnp.where(lane == 0, top, jnp.where(lane == 1, mass, 0.0))
    turned = wide[...].T
    message[...] = jnp.broadcast_to(turned[None, 0:2, 0:rows], message.shape)


def head_call(order, got, gain, words, softness):
    rows, columns = softness.shape[0], words.shape[1]
    return pl.pallas_call(
        lambda *refs: head_kernel(order, *refs),
        in_specs=[VMEM] * 4,
        out_specs=[VMEM, VMEM],
        out_shape=[shape((rows, columns), f32), shape((got.shape[0], 2, rows), f32)],
        scratch_shapes=[pltpu.VMEM((LANES, LANES), f32)],
        compiler_params=params(),
        cost_estimate=cost(2 * rows * WIDTH * columns, 2 * WIDTH * columns),
        name="head",
    )(got, gain, words, softness)


def body(
    skip_stream_arriving,
    chosen_specialists,
    sequence_piece_tallies,
    premix_rmsnorm_gain,
    dispatcher_weights,
    specialist_switch_weights,
    specialist_expand_weights,
    specialist_contract_weights,
    terminal_rmsnorm_gain,
    lexicon_projector_weights,
    softness_per_sequence,
):
    tokens, block = skip_stream_arriving.shape
    dp, mp = lax.axis_size("dp"), lax.axis_size("mp")
    count = dp * mp
    parts = 4
    spread, sides = dp // parts, mp // parts
    assert dp == parts * spread and mp == parts * sides and sides & (sides - 1) == 0
    part = lax.axis_index("dp") // spread
    y, core = part // 2, part % 2
    side = lax.axis_index("mp") % sides

    def send(value, to):
        pairs = []
        for q in range(parts):
            for r in range(spread):
                for z in range(parts):
                    for x in range(sides):
                        q2, z2, x2 = to(q, z, x)
                        source = (q * spread + r) * mp + z * sides + x
                        pairs.append((source, (q2 * spread + r) * mp + z2 * sides + x2))
        return lax.ppermute(value, ("dp", "mp"), pairs)

    other_core = lambda q, z, x: (q ^ 1, z, x)
    other_y = lambda q, z, x: (q ^ 2, z, x)
    home = lambda q, z, x: (z, q, x)

    sent, stream = prep_call(
        skip_stream_arriving, premix_rmsnorm_gain, chosen_specialists, sequence_piece_tallies
    )
    first = [
        send(sent, lambda q, z, x, c=c, i=i: (z ^ c, (q - 1) % parts, x ^ i))
        for c in range(2)
        for i in range(sides)
    ]
    wg, wu, wd = specialist_switch_weights, specialist_expand_weights, specialist_contract_weights
    if spread > 1:
        runs = [[q * spread + r for r in range(spread)] for q in range(parts)]
        wg = lax.all_gather(wg, "dp", axis=1, tiled=True, axis_index_groups=runs)
        wu = lax.all_gather(wu, "dp", axis=1, tiled=True, axis_index_groups=runs)
        wd = lax.all_gather(wd, "dp", axis=2, tiled=True, axis_index_groups=runs)
    depth, hidden = wg.shape[1], wg.shape[2]
    half = up_to(-(-hidden // 2))
    swap = lambda w: jnp.where(
        core == 0, jnp.pad(w[:, :, half:], ((0, 0), (0, 0), (0, 2 * half - hidden))), w[:, :, :half]
    )
    swapped = [send(swap(w), other_core) for w in (wg, wu)]
    wr = []
    for p in (part, part ^ 1):
        w = lax.dynamic_slice_in_dim(dispatcher_weights, p * depth, depth).T
        wr.append(jnp.pad(w, ((0, 16 - w.shape[0]), (0, 0))))

    feeds = [first]
    own = jnp.concatenate(first[:sides], axis=0)
    for s in range(1, parts):
        mine = send(own, lambda q, z, x, s=s: (q, (z - s) % parts, x))
        feeds.append([mine, send(mine, other_core)])
    stream = send(stream, home)

    scal = jnp.stack([core, side, y]).astype(jnp.int32)
    y_only = scal[2:3]
    partial, act, pieces, shares, back = {}, {}, {}, {}, {}

    def do_partial(s, *deps):
        own, give, meta, cols = partial_call(scal, sides, feeds[s], wr, (wg, wu), swapped, deps)
        partial[s] = (own, send(give, other_y), meta, send(meta, other_y), cols)
        return own

    def do_act(s, *deps):
        a = act_call(y_only, *partial[s], deps)
        a_y = send(a, other_y)
        pieces[s] = (a, a_y, send(a, other_core), send(a_y, other_core))
        return a

    def do_down(s, *deps):
        outs = down_call(scal, sides, pieces[s], partial[s][4], wd, deps)
        shares[s] = [outs[0]] + [
            send(outs[i], lambda q, z, x, i=i: (q, z, x ^ i)) for i in range(1, sides)
        ]
        if s < parts - 1:
            share = sum(v.astype(f32) for v in shares[s]).astype(bf16)
            shares[s] = share
            back[s] = send(share, lambda q, z, x, s=s: (q, (z + s + 1) % parts, x))
        return outs[0]

    p0 = do_partial(0)
    p1 = do_partial(1, p0)
    a0 = do_act(0, p1)
    p2 = do_partial(2, a0)
    a1 = do_act(1, p2)
    d0 = do_down(0, a1)
    p3 = do_partial(3, d0)
    a2 = do_act(2, p3)
    d1 = do_down(1, a2, shares[0])
    a3 = do_act(3, d1)
    d2 = do_down(2, a3, shares[1], back[0])
    do_down(3, d2, back[1])
    total, message = total_call(
        feeds[3][0], stream, [*shares[3], back[0], back[1], back[2]], block, count
    )

    everyone = lambda v: lax.all_to_all(v, ("dp", "mp"), 0, 0, tiled=True)
    got = everyone(message)
    branch = send(total, home)
    order = [
        [
            (q * spread + r) * mp + z * sides + x
            for z in range(parts)
            for r in range(spread)
        ]
        for q in range(parts)
        for x in range(sides)
    ]
    logits, pairs = head_call(
        order,
        got,
        terminal_rmsnorm_gain.reshape(mp, block),
        lexicon_projector_weights,
        softness_per_sequence[:, None],
    )
    pairs = everyone(pairs)
    new_hidden = skip_stream_arriving + branch_scale * branch.T
    largest = jnp.max(pairs[:, 0], axis=0)
    mass = jnp.sum(pairs[:, 1] * jnp.exp(pairs[:, 0] - largest), axis=0)
    logprobs = logits - largest[:, None] - jnp.log(mass)[:, None]
    return (new_hidden, logprobs)


def solution(mesh):
    return jax.shard_map(
        body,
        mesh=mesh,
        in_specs=(
            P("dp", "mp"),
            P("dp", None),
            P("dp", None),
            P("mp"),
            P(),
            P(None, "dp", "mp"),
            P(None, "dp", "mp"),
            P(None, "mp", "dp"),
            P(),
            P(None, ("dp", "mp")),
            P(),
        ),
        out_specs=(P("dp", "mp"), P(None, ("dp", "mp"))),
        check_vma=False,
    )
```

```python
import math

import jax
import jax.numpy as jnp
from jax import lax
from jax.experimental import pallas as pl
from jax.experimental.pallas import tpu as pltpu
from jax.sharding import PartitionSpec as P

WIDTH = 2304
META = 16
LANES = 128
branch_scale = 1.4 / math.sqrt(40.0)
epsilon = 1e-05
f32, bf16 = jnp.float32, jnp.bfloat16

VMEM = pl.BlockSpec(memory_space=pltpu.VMEM)
SMEM = pl.BlockSpec(memory_space=pltpu.SMEM)
ANY = pl.BlockSpec(memory_space=pl.ANY)


def up_to(n, step=LANES):
    return -(-n // step) * step


def params(mib=32):
    return pltpu.CompilerParams(vmem_limit_bytes=mib * 2**20)


def cost(flops, bytes_accessed):
    return pl.CostEstimate(flops=flops, bytes_accessed=bytes_accessed, transcendentals=0)


def shape(dims, dtype):
    return jax.ShapeDtypeStruct(dims, dtype)


def prep_kernel(tallies, x, gain, routes, out, ends):
    block, tokens = x.shape
    v = x[...]
    out[0:block] = (v * gain[...]).astype(bf16)
    sq = jnp.sum(v * v, axis=0, keepdims=True)
    hi = sq.astype(bf16).astype(f32)
    mid = (sq - hi).astype(bf16).astype(f32)
    here = lax.broadcasted_iota(jnp.int32, (1, tokens), 1)
    mark, end = jnp.zeros((1, tokens), f32), jnp.int32(-1)
    for q in range(ends.shape[0]):
        end = end + tallies[0, q]
        mark = jnp.where(here == end, q + 1.0, mark)
    rows = [routes[...].astype(f32), hi, mid, sq - hi - mid, mark]
    rows.append(jnp.zeros((META - 6, tokens), f32))
    out[block:] = jnp.concatenate(rows, axis=0).astype(bf16)
    ends[...] = columns_at(mark, v)[0 : ends.shape[0]]


def columns_at(mark, v):
    row = lax.broadcasted_iota(jnp.int32, (8, mark.shape[1]), 0)
    pick = jnp.where(mark == (row + 1).astype(f32), 1.0, 0.0)
    return lax.dot_general(
        pick, v, (((1,), (1,)), ((), ())), precision=lax.Precision.HIGHEST, preferred_element_type=f32
    )


def prep_call(x, gain, routes, tallies):
    block, tokens = x.shape
    reqs = tallies.shape[1]
    return pl.pallas_call(
        prep_kernel,
        in_specs=[SMEM, VMEM, VMEM, VMEM],
        out_specs=[VMEM, VMEM],
        out_shape=[shape((block + META, tokens), bf16), shape((reqs, block), f32)],
        compiler_params=params(),
        cost_estimate=cost(4 * tokens * block, 6 * tokens * block),
        name="prep",
    )(tallies, x, gain, routes)


def swap_kernel(scal, wg, wu, dep, out):
    half = wg.shape[2]
    out[:, :, 0:half] = wg[...]
    out[:, :, half:] = wu[...]


def swap_call(scal, wg, wu, half, dep):
    experts, depth, _ = wg.shape
    theirs = pl.BlockSpec((1, depth, half), lambda n, s: (n, 0, 1 - s[0]))
    return pl.pallas_call(
        swap_kernel,
        grid_spec=pltpu.PrefetchScalarGridSpec(
            num_scalar_prefetch=1,
            grid=(experts,),
            in_specs=[theirs, theirs, ANY],
            out_specs=pl.BlockSpec((1, depth, 2 * half), lambda n, s: (n, 0, 0)),
        ),
        out_shape=shape((experts, depth, 2 * half), bf16),
        compiler_params=params(),
        cost_estimate=cost(0, 8 * experts * depth * half),
        name="swap_halves",
    )(scal, wg, wu, dep)


def join_call(blocks):
    rows, tokens = blocks[0].shape

    def join_kernel(*refs):
        for i, ref in enumerate(refs[:-1]):
            refs[-1][i * rows : (i + 1) * rows] = ref[...]

    return pl.pallas_call(
        join_kernel,
        in_specs=[VMEM] * len(blocks),
        out_specs=VMEM,
        out_shape=shape((len(blocks) * rows, tokens), bf16),
        compiler_params=params(),
        cost_estimate=cost(0, 4 * len(blocks) * rows * tokens),
        name="join",
    )(*blocks)


def partial_kernel(sides, scal, *refs):
    feeds, refs = refs[:2], refs[2:]
    wr0, wr1, wg, wu, theirs = refs[:5]
    own, give, meta, cols, xs, xt, acc = refs[-7:]
    e = pl.program_id(0)
    core, side, y = scal[0], scal[1], scal[2]
    depth, half = wg.shape[1], wg.shape[2]
    deep = up_to(depth)
    tokens = xt.shape[0]
    block = depth // sides
    th = tokens // 2

    @pl.when(e == 0)
    def _():
        xs[depth:deep] = jnp.zeros((deep - depth, tokens), bf16)
        xs[deep + depth : 2 * deep] = jnp.zeros((deep - depth, tokens), bf16)
        xs[2 * deep :] = jnp.zeros((LANES, tokens), bf16)
        sq = jnp.zeros((1, tokens), f32)
        for which in range(2):
            ref = feeds[which]
            for i in range(sides):
                at = i * (block + META)
                row = which * deep + (side ^ i) * block
                xs[pl.ds(pl.multiple_of(row, 16), block)] = ref[at : at + block]
                for term in (4, 3, 2):
                    sq = sq + ref[at + block + term : at + block + term + 1].astype(f32)
        xs[2 * deep : 2 * deep + META] = feeds[0][block : block + META]
        router = jnp.dot(wr0[...], xs[0:depth], preferred_element_type=f32)
        router += jnp.dot(wr1[...], xs[deep : deep + depth], preferred_element_type=f32)
        m = jnp.concatenate([sq, router[0:7]], axis=0)
        near = jnp.where(y == 0, m[:, 0:th], m[:, th:])
        far = jnp.where(y == 0, m[:, th:], m[:, 0:th])
        meta[...] = near
        hi = far.astype(bf16).astype(f32)
        give[2 * th :] = jnp.zeros((META, 2 * half), bf16)
        give[2 * th :, 0:th] = jnp.concatenate([hi, far - hi], axis=0).astype(bf16)
        xt[...] = xs[...].T
        cols[...] = xt[:, 2 * deep :]

    routes = xt[:, 2 * deep :].astype(f32)
    ef = e.astype(f32)
    for which, w in enumerate((wg, wu)):
        at = which * half
        d = jnp.dot(xt[:, 0:depth], w[0], preferred_element_type=f32)
        d += jnp.dot(
            xt[:, deep : deep + depth], theirs[0, :, at : at + half], preferred_element_type=f32
        )
        for k in range(2):
            take = (routes[:, k : k + 1] == ef) | (e == 0)
            acc[k, :, at : at + half] = jnp.where(take, d, acc[k, :, at : at + half])

    @pl.when(e == pl.num_programs(0) - 1)
    def _():
        for k in range(2):
            own[k] = acc[k, pl.ds(pl.multiple_of(y * th, th), th)]
            give[k * th : (k + 1) * th] = acc[k, pl.ds(pl.multiple_of((1 - y) * th, th), th)].astype(bf16)


def partial_call(scal, sides, feeds, wr, weights, swapped, deps):
    experts, depth, wide = swapped.shape
    half = wide // 2
    tokens = feeds[0].shape[1]
    deep = up_to(depth)
    full = lambda v: pl.BlockSpec(v.shape, lambda n, s: (0,) * len(v.shape))
    mine = pl.BlockSpec((1, depth, half), lambda n, s: (n, 0, s[0]))
    theirs = pl.BlockSpec((1, depth, wide), lambda n, s: (n, 0, 0))
    outs = [
        shape((2, tokens // 2, wide), f32),
        shape((tokens + META, wide), bf16),
        shape((8, tokens // 2), f32),
        shape((tokens, LANES), bf16),
    ]
    call = pl.pallas_call(
        lambda *refs: partial_kernel(sides, *refs),
        grid_spec=pltpu.PrefetchScalarGridSpec(
            num_scalar_prefetch=1,
            grid=(experts,),
            in_specs=[full(v) for v in feeds]
            + [full(v) for v in wr]
            + [mine, mine, theirs]
            + [ANY] * len(deps),
            out_specs=[full(v) for v in outs],
            scratch_shapes=[
                pltpu.VMEM((2 * deep + LANES, tokens), bf16),
                pltpu.VMEM((tokens, 2 * deep + LANES), bf16),
                pltpu.VMEM((2, tokens, wide), f32),
            ],
        ),
        out_shape=outs,
        compiler_params=params(),
        cost_estimate=cost(
            8 * experts * depth * half * tokens, 8 * experts * depth * half + 12 * tokens * half
        ),
        name="gate_up_partial",
    )
    return call(scal, *feeds, *wr, *weights, swapped, *deps)


def act_kernel(scal, own, recv, meta, cols, *refs):
    act, turned = refs[-2:]
    y = scal[0]
    _, th, half = act.shape
    got = recv[2 * th :, 0:th].astype(f32)
    m = meta[...] + got[0:8] + got[8:16]
    turned[...] = jnp.concatenate([m, jnp.zeros((LANES - 8, th), f32)], axis=0).T
    m = turned[...]
    routes = cols[pl.ds(pl.multiple_of(y * th, th), th)].astype(f32)
    scale = lax.rsqrt(m[:, 0:1] / WIDTH + epsilon)
    logits = []
    for k in range(2):
        logit = jnp.zeros_like(scale)
        for e in range(4):
            logit = jnp.where(routes[:, k : k + 1] == e, m[:, 1 + e : 2 + e], logit)
        logits.append(logit * scale)
    for k in range(2):
        mix = scale / (1.0 + jnp.exp(logits[1 - k] - logits[k]))
        at = slice(k * th, (k + 1) * th)
        g = (own[k, :, 0:half] + recv[at, 0:half].astype(f32)) * scale
        u = (own[k, :, half:] + recv[at, half:].astype(f32)) * mix
        act[k] = (g / (1.0 + jnp.exp(-g)) * u).astype(bf16)


def act_call(scal, own, recv, meta, cols, deps):
    _, th, wide = own.shape
    return pl.pallas_call(
        act_kernel,
        in_specs=[SMEM] + [VMEM] * 4 + [ANY] * len(deps),
        out_specs=VMEM,
        out_shape=shape((2, th, wide // 2), bf16),
        scratch_shapes=[pltpu.VMEM((th, LANES), f32)],
        compiler_params=params(),
        cost_estimate=cost(12 * th * wide, 14 * th * wide),
        name="act",
    )(scal, own, recv, meta, cols, *deps)


def down_kernel(sides, scal, a, a_y, b, b_y, cols, wd, *refs):
    outs = refs[-sides - 2 : -2]
    whole, acc = refs[-2:]
    e = pl.program_id(0)
    core, side, y = scal[0], scal[1], scal[2]
    _, th, half = a.shape
    width, hidden = wd.shape[1:]
    block = width // sides

    @pl.when(e == 0)
    def _():
        for mine, other, first in ((a, b, y), (a_y, b_y, 1 - y)):
            rows = pl.ds(pl.multiple_of(first * th, th), th)
            for k in range(2):
                whole[k, rows, 0:half] = jnp.where(core == 0, mine[k], other[k])
                whole[k, rows, half:] = jnp.where(core == 0, other[k], mine[k])

    ef = e.astype(f32)
    routes = cols[...].astype(f32)
    masks = [jnp.where(routes[:, k : k + 1] == ef, 1.0, 0.0).astype(bf16) for k in range(2)]
    rows = whole[0, :, 0:hidden] * masks[0] + whole[1, :, 0:hidden] * masks[1]
    d = lax.dot_general(wd[0], rows, (((1,), (1,)), ((), ())), preferred_element_type=f32)

    @pl.when(e == 0)
    def _():
        acc[...] = d

    @pl.when(e > 0)
    def _():
        acc[...] += d

    @pl.when(e == pl.num_programs(0) - 1)
    def _():
        for i in range(sides):
            rows = pl.ds(pl.multiple_of((side ^ i) * block, 16), block)
            outs[i][...] = acc[rows].astype(bf16)


def down_call(scal, sides, pieces, cols, wd, deps):
    experts, width, hidden = wd.shape
    tokens = cols.shape[0]
    half = pieces[0].shape[2]
    full = lambda v: pl.BlockSpec(v.shape, lambda n: (0,) * len(v.shape))
    outs = [shape((width // sides, tokens), bf16)] * sides
    return pl.pallas_call(
        lambda *refs: down_kernel(sides, *refs),
        grid=(experts,),
        in_specs=[SMEM]
        + [full(v) for v in pieces]
        + [full(cols), pl.BlockSpec((1, width, hidden), lambda n: (n, 0, 0))]
        + [ANY] * len(deps),
        out_specs=[full(v) for v in outs],
        out_shape=outs,
        scratch_shapes=[
            pltpu.VMEM((2, tokens, 2 * half), bf16),
            pltpu.VMEM((width, tokens), f32),
        ],
        compiler_params=params(),
        cost_estimate=cost(
            2 * experts * width * hidden * tokens, 2 * experts * width * hidden + 2 * width * tokens
        ),
        name="down",
    )(scal, *pieces, cols, wd, *deps)


def total_kernel(meta, stream, *refs):
    parts, (total, message) = refs[:-2], refs[-2:]
    v = parts[0][...].astype(f32)
    for ref in parts[1:]:
        v = v + ref[...].astype(f32)
    total[...] = v
    reqs = stream.shape[0]
    ends = columns_at(meta[5:6].astype(f32), v)
    ends = stream[...] + branch_scale * ends[0:reqs]
    message[...] = jnp.broadcast_to(ends[None], message.shape)


def total_call(feed, stream, parts, block, count):
    tokens = feed.shape[1]
    full = lambda v: pl.BlockSpec(v.shape, lambda n: (0,) * len(v.shape))
    outs = [shape((block, tokens), f32), shape((count, *stream.shape), f32)]
    return pl.pallas_call(
        total_kernel,
        grid=(1,),
        in_specs=[pl.BlockSpec((META, tokens), lambda n: (block // META, 0)), full(stream)]
        + [full(v) for v in parts],
        out_specs=[full(v) for v in outs],
        out_shape=outs,
        compiler_params=params(),
        cost_estimate=cost(16 * block * tokens, 14 * block * tokens),
        name="branch_total",
    )(feed, stream, *parts)


def head_kernel(order, got, gain, words, softness, logits, message, wide):
    blocks, block = gain.shape
    rows, columns = logits.shape
    ends, squares = [], 0.0
    for b in range(blocks):
        v = jnp.concatenate([got[i] for i in order[b]], axis=0)
        squares = squares + jnp.sum(v * v, axis=1, keepdims=True)
        ends.append(v)
    scale = lax.rsqrt(squares / WIDTH + epsilon)
    total = jnp.zeros((rows, columns), f32)
    for b in range(blocks):
        feed = (ends[b] * scale * gain[b : b + 1]).astype(bf16)
        total += jnp.dot(feed, words[b * block : (b + 1) * block], preferred_element_type=f32)
    total = total / (WIDTH / 256.0 * softness[...])
    logits[...] = total
    top = jnp.max(total, axis=1, keepdims=True)
    mass = jnp.sum(jnp.exp(total - top), axis=1, keepdims=True)
    wide[...] = jnp.zeros_like(wide)
    lane = lax.broadcasted_iota(jnp.int32, (rows, LANES), 1)
    wide[0:rows] = jnp.where(lane == 0, top, jnp.where(lane == 1, mass, 0.0))
    turned = wide[...].T
    message[...] = jnp.broadcast_to(turned[None, 0:2, 0:rows], message.shape)


def head_call(order, got, gain, words, softness):
    rows, columns = softness.shape[0], words.shape[1]
    return pl.pallas_call(
        lambda *refs: head_kernel(order, *refs),
        in_specs=[VMEM] * 4,
        out_specs=[VMEM, VMEM],
        out_shape=[shape((rows, columns), f32), shape((got.shape[0], 2, rows), f32)],
        scratch_shapes=[pltpu.VMEM((LANES, LANES), f32)],
        compiler_params=params(),
        cost_estimate=cost(2 * rows * WIDTH * columns, 2 * WIDTH * columns),
        name="head",
    )(got, gain, words, softness)


def body(
    skip_stream_arriving,
    chosen_specialists,
    sequence_piece_tallies,
    premix_rmsnorm_gain,
    dispatcher_weights,
    specialist_switch_weights,
    specialist_expand_weights,
    specialist_contract_weights,
    terminal_rmsnorm_gain,
    lexicon_projector_weights,
    softness_per_sequence,
):
    tokens, block = skip_stream_arriving.shape
    dp, mp = lax.axis_size("dp"), lax.axis_size("mp")
    count = dp * mp
    parts = 4
    spread, sides = dp // parts, mp // parts
    assert dp == parts * spread and mp == parts * sides and sides & (sides - 1) == 0
    part = lax.axis_index("dp") // spread
    y, core = part // 2, part % 2
    side = lax.axis_index("mp") % sides

    def send(value, to):
        pairs = []
        for q in range(parts):
            for r in range(spread):
                for z in range(parts):
                    for x in range(sides):
                        q2, z2, x2 = to(q, z, x)
                        source = (q * spread + r) * mp + z * sides + x
                        pairs.append((source, (q2 * spread + r) * mp + z2 * sides + x2))
        return lax.ppermute(value, ("dp", "mp"), pairs)

    other_core = lambda q, z, x: (q ^ 1, z, x)
    other_y = lambda q, z, x: (q ^ 2, z, x)
    home = lambda q, z, x: (z, q, x)

    scal = jnp.stack([core, side, y]).astype(jnp.int32)
    sent, stream = prep_call(
        skip_stream_arriving.T, premix_rmsnorm_gain[:, None], chosen_specialists.T, sequence_piece_tallies
    )
    first = [send(sent, lambda q, z, x, i=i: (z, (q - 1) % parts, x ^ i)) for i in range(sides)]
    wg, wu, wd = specialist_switch_weights, specialist_expand_weights, specialist_contract_weights
    if spread > 1:
        runs = [[q * spread + r for r in range(spread)] for q in range(parts)]
        wg = lax.all_gather(wg, "dp", axis=1, tiled=True, axis_index_groups=runs)
        wu = lax.all_gather(wu, "dp", axis=1, tiled=True, axis_index_groups=runs)
        wd = lax.all_gather(wd, "dp", axis=2, tiled=True, axis_index_groups=runs)
    wd = jnp.swapaxes(wd, 1, 2)
    depth, hidden = wg.shape[1], wg.shape[2]
    half = up_to(-(-hidden // 2))
    swapped = send(swap_call(scal, wg, wu, half, sent), other_core)
    wr = []
    padded = jnp.pad(dispatcher_weights.T, ((0, 16 - dispatcher_weights.shape[1]), (0, 0)))
    for p in (part, part ^ 1):
        wr.append(lax.dynamic_slice_in_dim(padded, p * depth, depth, axis=1))

    pair = join_call(first)
    feeds = [[pair, send(pair, other_core)]]
    for s in range(1, parts):
        mine = send(pair, lambda q, z, x, s=s: (q, (z - s) % parts, x))
        feeds.append([mine, send(mine, other_core)])
    stream = send(stream, home)

    y_only = scal[2:3]
    partial, act, pieces, shares, back = {}, {}, {}, {}, {}

    def do_partial(s, *deps):
        own, give, meta, cols = partial_call(scal, sides, feeds[s], wr, (wg, wu), swapped, deps)
        partial[s] = (own, send(give, other_y), meta, cols)
        return own

    def do_act(s, *deps):
        a = act_call(y_only, *partial[s], deps)
        a_y = send(a, other_y)
        pieces[s] = (a, a_y, send(a, other_core), send(a_y, other_core))
        return a

    def do_down(s, *deps):
        outs = down_call(scal, sides, pieces[s], partial[s][3], wd, deps)
        shares[s] = [outs[0]] + [
            send(outs[i], lambda q, z, x, i=i: (q, z, x ^ i)) for i in range(1, sides)
        ]
        if s < parts - 1:
            share = sum(v.astype(f32) for v in shares[s]).astype(bf16)
            shares[s] = share
            back[s] = send(share, lambda q, z, x, s=s: (q, (z + s + 1) % parts, x))
        return outs[0]

    p0 = do_partial(0)
    p1 = do_partial(1, p0)
    a0 = do_act(0, p1)
    p2 = do_partial(2, a0)
    a1 = do_act(1, p2)
    d0 = do_down(0, a1)
    p3 = do_partial(3, d0)
    a2 = do_act(2, p3)
    d1 = do_down(1, a2, shares[0])
    a3 = do_act(3, d1)
    d2 = do_down(2, a3, shares[1], back[0])
    do_down(3, d2, back[1])
    total, message = total_call(
        feeds[3][0], stream, [*shares[3], back[0], back[1], back[2]], block, count
    )

    everyone = lambda v: lax.all_to_all(v, ("dp", "mp"), 0, 0, tiled=True)
    got = everyone(message)
    branch = send(total, home)
    order = [
        [
            (q * spread + r) * mp + z * sides + x
            for z in range(parts)
            for r in range(spread)
        ]
        for q in range(parts)
        for x in range(sides)
    ]
    logits, pairs = head_call(
        order,
        got,
        terminal_rmsnorm_gain.reshape(mp, block),
        lexicon_projector_weights,
        softness_per_sequence[:, None],
    )
    pairs = everyone(pairs)
    new_hidden = skip_stream_arriving + branch_scale * branch.T
    largest = jnp.max(pairs[:, 0], axis=0)
    mass = jnp.sum(pairs[:, 1] * jnp.exp(pairs[:, 0] - largest), axis=0)
    logprobs = logits - largest[:, None] - jnp.log(mass)[:, None]
    return (new_hidden, logprobs)


def solution(mesh):
    return jax.shard_map(
        body,
        mesh=mesh,
        in_specs=(
            P("dp", "mp"),
            P("dp", None),
            P("dp", None),
            P("mp"),
            P(),
            P(None, "dp", "mp"),
            P(None, "dp", "mp"),
            P(None, "mp", "dp"),
            P(),
            P(None, ("dp", "mp")),
            P(),
        ),
        out_specs=(P("dp", "mp"), P(None, ("dp", "mp"))),
        check_vma=False,
    )
```

```python
import math

import jax
import jax.numpy as jnp
from jax import lax
from jax.experimental import pallas as pl
from jax.experimental.pallas import tpu as pltpu
from jax.sharding import PartitionSpec as P

WIDTH = 2304
META = 16
LANES = 128
branch_scale = 1.4 / math.sqrt(40.0)
epsilon = 1e-05
f32, bf16 = jnp.float32, jnp.bfloat16

VMEM = pl.BlockSpec(memory_space=pltpu.VMEM)
SMEM = pl.BlockSpec(memory_space=pltpu.SMEM)
ANY = pl.BlockSpec(memory_space=pl.ANY)


def up_to(n, step=LANES):
    return -(-n // step) * step


def params(mib=60):
    return pltpu.CompilerParams(vmem_limit_bytes=mib * 2**20)


def cost(flops, bytes_accessed):
    return pl.CostEstimate(flops=flops, bytes_accessed=bytes_accessed, transcendentals=0)


def shape(dims, dtype):
    return jax.ShapeDtypeStruct(dims, dtype)


def prep_kernel(tallies, x, gain, routes, dep, out, ends):
    block, tokens = x.shape
    v = x[...]
    out[0:block] = (v * gain[...]).astype(bf16)
    sq = jnp.sum(v * v, axis=0, keepdims=True)
    hi = sq.astype(bf16).astype(f32)
    mid = (sq - hi).astype(bf16).astype(f32)
    here = lax.broadcasted_iota(jnp.int32, (1, tokens), 1)
    mark, end = jnp.zeros((1, tokens), f32), jnp.int32(-1)
    for q in range(ends.shape[0]):
        end = end + tallies[0, q]
        mark = jnp.where(here == end, q + 1.0, mark)
    rows = [routes[...].astype(f32), hi, mid, sq - hi - mid, mark]
    rows.append(jnp.zeros((META - 6, tokens), f32))
    out[block:] = jnp.concatenate(rows, axis=0).astype(bf16)
    ends[...] = columns_at(mark, v)[0 : ends.shape[0]]


def columns_at(mark, v):
    row = lax.broadcasted_iota(jnp.int32, (8, mark.shape[1]), 0)
    pick = jnp.where(mark == (row + 1).astype(f32), 1.0, 0.0)
    return lax.dot_general(
        pick, v, (((1,), (1,)), ((), ())), precision=lax.Precision.HIGHEST, preferred_element_type=f32
    )


def prep_call(x, gain, routes, tallies, dep):
    block, tokens = x.shape
    reqs = tallies.shape[1]
    return pl.pallas_call(
        prep_kernel,
        in_specs=[SMEM, VMEM, VMEM, VMEM, ANY],
        out_specs=[VMEM, VMEM],
        out_shape=[shape((block + META, tokens), bf16), shape((reqs, block), f32)],
        compiler_params=params(),
        cost_estimate=cost(4 * tokens * block, 6 * tokens * block),
        name="prep",
    )(tallies, x, gain, routes, dep)


def pack_kernel(scal, wg, wu, *refs):
    out = refs[-1]
    half = wg.shape[2]
    out[:, :, 0:half] = wg[...]
    out[:, :, half:] = wu[...]


def pack_call(scal, wg, wu, half, mine, deps):
    experts, depth, _ = wg.shape
    part = pl.BlockSpec((1, depth, half), lambda n, s: (n, 0, s[0] if mine else 1 - s[0]))
    return pl.pallas_call(
        pack_kernel,
        grid_spec=pltpu.PrefetchScalarGridSpec(
            num_scalar_prefetch=1,
            grid=(experts,),
            in_specs=[part, part] + [ANY] * len(deps),
            out_specs=pl.BlockSpec((1, depth, 2 * half), lambda n, s: (n, 0, 0)),
        ),
        out_shape=shape((experts, depth, 2 * half), bf16),
        compiler_params=params(),
        cost_estimate=cost(0, 8 * experts * depth * half),
        name="pack_mine" if mine else "pack_other",
    )(scal, wg, wu, *deps)


def join_call(blocks):
    rows, tokens = blocks[0].shape

    def join_kernel(*refs):
        for i, ref in enumerate(refs[:-1]):
            refs[-1][i * rows : (i + 1) * rows] = ref[...]

    return pl.pallas_call(
        join_kernel,
        in_specs=[VMEM] * len(blocks),
        out_specs=VMEM,
        out_shape=shape((len(blocks) * rows, tokens), bf16),
        compiler_params=params(),
        cost_estimate=cost(0, 4 * len(blocks) * rows * tokens),
        name="join",
    )(*blocks)


def partial_kernel(sides, scal, *refs):
    feeds, refs = refs[:2], refs[2:]
    wr0, wr1, mine, theirs = refs[:4]
    own, give, meta, cols, xs, xt, acc = refs[-7:]
    e = pl.program_id(0)
    core, side, y = scal[0], scal[1], scal[2]
    depth, wide = mine.shape[1:]
    deep = up_to(depth)
    tokens = xt.shape[0]
    block = depth // sides
    th = tokens // 2

    @pl.when(e == 0)
    def _():
        xs[depth:deep] = jnp.zeros((deep - depth, tokens), bf16)
        xs[deep + depth : 2 * deep] = jnp.zeros((deep - depth, tokens), bf16)
        xs[2 * deep :] = jnp.zeros((LANES, tokens), bf16)
        sq = jnp.zeros((1, tokens), f32)
        for which in range(2):
            ref = feeds[which]
            for i in range(sides):
                at = i * (block + META)
                row = which * deep + (side ^ i) * block
                xs[pl.ds(pl.multiple_of(row, 16), block)] = ref[at : at + block]
                for term in (4, 3, 2):
                    sq = sq + ref[at + block + term : at + block + term + 1].astype(f32)
        xs[2 * deep : 2 * deep + META] = feeds[0][block : block + META]
        router = jnp.dot(wr0[...], xs[0:depth], preferred_element_type=f32)
        router += jnp.dot(wr1[...], xs[deep : deep + depth], preferred_element_type=f32)
        m = jnp.concatenate([sq, router[0:7]], axis=0)
        near = jnp.where(y == 0, m[:, 0:th], m[:, th:])
        far = jnp.where(y == 0, m[:, th:], m[:, 0:th])
        meta[...] = near
        hi = far.astype(bf16).astype(f32)
        give[2 * th :] = jnp.zeros((META, wide), bf16)
        give[2 * th :, 0:th] = jnp.concatenate([hi, far - hi], axis=0).astype(bf16)
        xt[...] = xs[...].T
        cols[...] = xt[:, 2 * deep :]

    routes = xt[:, 2 * deep :].astype(f32)
    ef = e.astype(f32)
    step = 256
    for at in range(0, wide, step):
        to = slice(at, at + step)
        d = jnp.dot(xt[:, 0:depth], mine[0, :, to], preferred_element_type=f32)
        d += jnp.dot(xt[:, deep : deep + depth], theirs[0, :, to], preferred_element_type=f32)
        for k in range(2):
            take = (routes[:, k : k + 1] == ef) | (e == 0)
            acc[k, :, to] = jnp.where(take, d, acc[k, :, to])

    @pl.when(e == pl.num_programs(0) - 1)
    def _():
        for k in range(2):
            own[k] = acc[k, pl.ds(pl.multiple_of(y * th, th), th)]
            give[k * th : (k + 1) * th] = acc[k, pl.ds(pl.multiple_of((1 - y) * th, th), th)].astype(bf16)


def partial_call(scal, sides, feeds, wr, weights, deps):
    experts, depth, wide = weights[0].shape
    half = wide // 2
    tokens = feeds[0].shape[1]
    deep = up_to(depth)
    full = lambda v: pl.BlockSpec(v.shape, lambda n, s: (0,) * len(v.shape))
    part = pl.BlockSpec((1, depth, wide), lambda n, s: (n, 0, 0))
    outs = [
        shape((2, tokens // 2, wide), f32),
        shape((tokens + META, wide), bf16),
        shape((8, tokens // 2), f32),
        shape((tokens, LANES), bf16),
    ]
    call = pl.pallas_call(
        lambda *refs: partial_kernel(sides, *refs),
        grid_spec=pltpu.PrefetchScalarGridSpec(
            num_scalar_prefetch=1,
            grid=(experts,),
            in_specs=[full(v) for v in feeds]
            + [full(v) for v in wr]
            + [part, part]
            + [ANY] * len(deps),
            out_specs=[full(v) for v in outs],
            scratch_shapes=[
                pltpu.VMEM((2 * deep + LANES, tokens), bf16),
                pltpu.VMEM((tokens, 2 * deep + LANES), bf16),
                pltpu.VMEM((2, tokens, wide), f32),
            ],
        ),
        out_shape=outs,
        compiler_params=params(),
        cost_estimate=cost(
            8 * experts * depth * half * tokens, 8 * experts * depth * half + 12 * tokens * half
        ),
        name="gate_up_partial",
    )
    return call(scal, *feeds, *wr, *weights, *deps)


def act_kernel(scal, own, recv, meta, cols, *refs):
    act, turned = refs[-2:]
    y = scal[0]
    _, th, half = act.shape
    got = recv[2 * th :, 0:th].astype(f32)
    m = meta[...] + got[0:8] + got[8:16]
    turned[...] = jnp.concatenate([m, jnp.zeros((LANES - 8, th), f32)], axis=0).T
    m = turned[...]
    routes = cols[pl.ds(pl.multiple_of(y * th, th), th)].astype(f32)
    scale = lax.rsqrt(m[:, 0:1] / WIDTH + epsilon)
    logits = []
    for k in range(2):
        logit = jnp.zeros_like(scale)
        for e in range(4):
            logit = jnp.where(routes[:, k : k + 1] == e, m[:, 1 + e : 2 + e], logit)
        logits.append(logit * scale)
    for k in range(2):
        mix = scale / (1.0 + jnp.exp(logits[1 - k] - logits[k]))
        at = slice(k * th, (k + 1) * th)
        g = (own[k, :, 0:half] + recv[at, 0:half].astype(f32)) * scale
        u = (own[k, :, half:] + recv[at, half:].astype(f32)) * mix
        act[k] = (g / (1.0 + jnp.exp(-g)) * u).astype(bf16)


def act_call(scal, own, recv, meta, cols, deps):
    _, th, wide = own.shape
    return pl.pallas_call(
        act_kernel,
        in_specs=[SMEM] + [VMEM] * 4 + [ANY] * len(deps),
        out_specs=VMEM,
        out_shape=shape((2, th, wide // 2), bf16),
        scratch_shapes=[pltpu.VMEM((th, LANES), f32)],
        compiler_params=params(),
        cost_estimate=cost(12 * th * wide, 14 * th * wide),
        name="act",
    )(scal, own, recv, meta, cols, *deps)


def down_kernel(sides, scal, a, a_y, b, b_y, cols, wd, *refs):
    outs = refs[-sides - 2 : -2]
    whole, acc = refs[-2:]
    e = pl.program_id(0)
    core, side, y = scal[0], scal[1], scal[2]
    _, th, half = a.shape
    width, hidden = wd.shape[1:]
    block = width // sides

    @pl.when(e == 0)
    def _():
        for mine, other, first in ((a, b, y), (a_y, b_y, 1 - y)):
            rows = pl.ds(pl.multiple_of(first * th, th), th)
            for k in range(2):
                whole[k, rows, 0:half] = jnp.where(core == 0, mine[k], other[k])
                whole[k, rows, half:] = jnp.where(core == 0, other[k], mine[k])

    ef = e.astype(f32)
    routes = cols[...].astype(f32)
    masks = [jnp.where(routes[:, k : k + 1] == ef, 1.0, 0.0).astype(bf16) for k in range(2)]
    rows = whole[0, :, 0:hidden] * masks[0] + whole[1, :, 0:hidden] * masks[1]
    d = lax.dot_general(wd[0], rows, (((1,), (1,)), ((), ())), preferred_element_type=f32)

    @pl.when(e == 0)
    def _():
        acc[...] = d

    @pl.when(e > 0)
    def _():
        acc[...] += d

    @pl.when(e == pl.num_programs(0) - 1)
    def _():
        for i in range(sides):
            rows = pl.ds(pl.multiple_of((side ^ i) * block, 16), block)
            outs[i][...] = acc[rows].astype(bf16)


def down_call(scal, sides, pieces, cols, wd, deps):
    experts, width, hidden = wd.shape
    tokens = cols.shape[0]
    half = pieces[0].shape[2]
    full = lambda v: pl.BlockSpec(v.shape, lambda n: (0,) * len(v.shape))
    outs = [shape((width // sides, tokens), bf16)] * sides
    return pl.pallas_call(
        lambda *refs: down_kernel(sides, *refs),
        grid=(experts,),
        in_specs=[SMEM]
        + [full(v) for v in pieces]
        + [full(cols), pl.BlockSpec((1, width, hidden), lambda n: (n, 0, 0))]
        + [ANY] * len(deps),
        out_specs=[full(v) for v in outs],
        out_shape=outs,
        scratch_shapes=[
            pltpu.VMEM((2, tokens, 2 * half), bf16),
            pltpu.VMEM((width, tokens), f32),
        ],
        compiler_params=params(),
        cost_estimate=cost(
            2 * experts * width * hidden * tokens, 2 * experts * width * hidden + 2 * width * tokens
        ),
        name="down",
    )(scal, *pieces, cols, wd, *deps)


def total_kernel(meta, stream, *refs):
    parts, (total, message) = refs[:-2], refs[-2:]
    v = parts[0][...].astype(f32)
    for ref in parts[1:]:
        v = v + ref[...].astype(f32)
    total[...] = v
    reqs = stream.shape[0]
    ends = columns_at(meta[5:6].astype(f32), v)
    ends = stream[...] + branch_scale * ends[0:reqs]
    message[...] = jnp.broadcast_to(ends[None], message.shape)


def total_call(feed, stream, parts, block, count):
    tokens = feed.shape[1]
    full = lambda v: pl.BlockSpec(v.shape, lambda n: (0,) * len(v.shape))
    outs = [shape((block, tokens), f32), shape((count, *stream.shape), f32)]
    return pl.pallas_call(
        total_kernel,
        grid=(1,),
        in_specs=[pl.BlockSpec((META, tokens), lambda n: (block // META, 0)), full(stream)]
        + [full(v) for v in parts],
        out_specs=[full(v) for v in outs],
        out_shape=outs,
        compiler_params=params(),
        cost_estimate=cost(16 * block * tokens, 14 * block * tokens),
        name="branch_total",
    )(feed, stream, *parts)


def head_kernel(order, got, gain, words, softness, logits, message, wide):
    blocks, block = gain.shape
    rows, columns = logits.shape
    ends, squares = [], 0.0
    for b in range(blocks):
        v = jnp.concatenate([got[i] for i in order[b]], axis=0)
        squares = squares + jnp.sum(v * v, axis=1, keepdims=True)
        ends.append(v)
    scale = lax.rsqrt(squares / WIDTH + epsilon)
    total = jnp.zeros((rows, columns), f32)
    for b in range(blocks):
        feed = (ends[b] * scale * gain[b : b + 1]).astype(bf16)
        total += jnp.dot(feed, words[b * block : (b + 1) * block], preferred_element_type=f32)
    total = total / (WIDTH / 256.0 * softness[...])
    logits[...] = total
    top = jnp.max(total, axis=1, keepdims=True)
    mass = jnp.sum(jnp.exp(total - top), axis=1, keepdims=True)
    wide[...] = jnp.zeros_like(wide)
    lane = lax.broadcasted_iota(jnp.int32, (rows, LANES), 1)
    wide[0:rows] = jnp.where(lane == 0, top, jnp.where(lane == 1, mass, 0.0))
    turned = wide[...].T
    message[...] = jnp.broadcast_to(turned[None, 0:2, 0:rows], message.shape)


def head_call(order, got, gain, words, softness):
    rows, columns = softness.shape[0], words.shape[1]
    return pl.pallas_call(
        lambda *refs: head_kernel(order, *refs),
        in_specs=[VMEM] * 4,
        out_specs=[VMEM, VMEM],
        out_shape=[shape((rows, columns), f32), shape((got.shape[0], 2, rows), f32)],
        scratch_shapes=[pltpu.VMEM((LANES, LANES), f32)],
        compiler_params=params(),
        cost_estimate=cost(2 * rows * WIDTH * columns, 2 * WIDTH * columns),
        name="head",
    )(got, gain, words, softness)


def body(
    skip_stream_arriving,
    chosen_specialists,
    sequence_piece_tallies,
    premix_rmsnorm_gain,
    dispatcher_weights,
    specialist_switch_weights,
    specialist_expand_weights,
    specialist_contract_weights,
    terminal_rmsnorm_gain,
    lexicon_projector_weights,
    softness_per_sequence,
):
    tokens, block = skip_stream_arriving.shape
    dp, mp = lax.axis_size("dp"), lax.axis_size("mp")
    count = dp * mp
    parts = 4
    spread, sides = dp // parts, mp // parts
    assert dp == parts * spread and mp == parts * sides and sides & (sides - 1) == 0
    part = lax.axis_index("dp") // spread
    y, core = part // 2, part % 2
    side = lax.axis_index("mp") % sides

    def send(value, to):
        pairs = []
        for q in range(parts):
            for r in range(spread):
                for z in range(parts):
                    for x in range(sides):
                        q2, z2, x2 = to(q, z, x)
                        source = (q * spread + r) * mp + z * sides + x
                        pairs.append((source, (q2 * spread + r) * mp + z2 * sides + x2))
        return lax.ppermute(value, ("dp", "mp"), pairs)

    other_core = lambda q, z, x: (q ^ 1, z, x)
    other_y = lambda q, z, x: (q ^ 2, z, x)
    home = lambda q, z, x: (z, q, x)

    scal = jnp.stack([core, side, y]).astype(jnp.int32)
    wg, wu, wd = specialist_switch_weights, specialist_expand_weights, specialist_contract_weights
    if spread > 1:
        runs = [[q * spread + r for r in range(spread)] for q in range(parts)]
        wg = lax.all_gather(wg, "dp", axis=1, tiled=True, axis_index_groups=runs)
        wu = lax.all_gather(wu, "dp", axis=1, tiled=True, axis_index_groups=runs)
        wd = lax.all_gather(wd, "dp", axis=2, tiled=True, axis_index_groups=runs)
    wd = jnp.swapaxes(wd, 1, 2)
    depth, hidden = wg.shape[1], wg.shape[2]
    half = up_to(-(-hidden // 2))
    given = pack_call(scal, wg, wu, half, False, ())
    sent, stream = prep_call(
        skip_stream_arriving.T,
        premix_rmsnorm_gain[:, None],
        chosen_specialists.T,
        sequence_piece_tallies,
        given,
    )
    first = [send(sent, lambda q, z, x, i=i: (z, (q - 1) % parts, x ^ i)) for i in range(sides)]
    weights = (pack_call(scal, wg, wu, half, True, (sent,)), send(given, other_core))
    wr = []
    padded = jnp.pad(dispatcher_weights.T, ((0, 16 - dispatcher_weights.shape[1]), (0, 0)))
    for p in (part, part ^ 1):
        wr.append(lax.dynamic_slice_in_dim(padded, p * depth, depth, axis=1))

    pair = join_call(first)
    feeds = [[pair, send(pair, other_core)]]
    for s in range(1, parts):
        mine = send(pair, lambda q, z, x, s=s: (q, (z - s) % parts, x))
        feeds.append([mine, send(mine, other_core)])
    stream = send(stream, home)

    y_only = scal[2:3]
    partial, act, pieces, shares, back = {}, {}, {}, {}, {}

    def do_partial(s, *deps):
        own, give, meta, cols = partial_call(scal, sides, feeds[s], wr, weights, deps)
        partial[s] = (own, send(give, other_y), meta, cols)
        return own

    def do_act(s, *deps):
        a = act_call(y_only, *partial[s], deps)
        a_y = send(a, other_y)
        pieces[s] = (a, a_y, send(a, other_core), send(a_y, other_core))
        return a

    def do_down(s, *deps):
        outs = down_call(scal, sides, pieces[s], partial[s][3], wd, deps)
        shares[s] = [outs[0]] + [
            send(outs[i], lambda q, z, x, i=i: (q, z, x ^ i)) for i in range(1, sides)
        ]
        if s < parts - 1:
            share = sum(v.astype(f32) for v in shares[s]).astype(bf16)
            shares[s] = share
            back[s] = send(share, lambda q, z, x, s=s: (q, (z + s + 1) % parts, x))
        return outs[0]

    p0 = do_partial(0)
    p1 = do_partial(1, p0)
    a0 = do_act(0, p1)
    p2 = do_partial(2, a0)
    a1 = do_act(1, p2)
    p3 = do_partial(3, a1)
    a2 = do_act(2, p3)
    d0 = do_down(0, a2)
    a3 = do_act(3, d0)
    d1 = do_down(1, a3)
    d2 = do_down(2, d1, shares[0])
    do_down(3, d2, shares[1])
    total, message = total_call(
        feeds[3][0], stream, [*shares[3], back[0], back[1], back[2]], block, count
    )

    everyone = lambda v: lax.all_to_all(v, ("dp", "mp"), 0, 0, tiled=True)
    got = everyone(message)
    branch = send(total, home)
    order = [
        [
            (q * spread + r) * mp + z * sides + x
            for z in range(parts)
            for r in range(spread)
        ]
        for q in range(parts)
        for x in range(sides)
    ]
    logits, pairs = head_call(
        order,
        got,
        terminal_rmsnorm_gain.reshape(mp, block),
        lexicon_projector_weights,
        softness_per_sequence[:, None],
    )
    pairs = everyone(pairs)
    new_hidden = skip_stream_arriving + branch_scale * branch.T
    largest = jnp.max(pairs[:, 0], axis=0)
    mass = jnp.sum(pairs[:, 1] * jnp.exp(pairs[:, 0] - largest), axis=0)
    logprobs = logits - largest[:, None] - jnp.log(mass)[:, None]
    return (new_hidden, logprobs)


def solution(mesh):
    return jax.shard_map(
        body,
        mesh=mesh,
        in_specs=(
            P("dp", "mp"),
            P("dp", None),
            P("dp", None),
            P("mp"),
            P(),
            P(None, "dp", "mp"),
            P(None, "dp", "mp"),
            P(None, "mp", "dp"),
            P(),
            P(None, ("dp", "mp")),
            P(),
        ),
        out_specs=(P("dp", "mp"), P(None, ("dp", "mp"))),
        check_vma=False,
    )
```

```python
import math

import jax
import jax.numpy as jnp
from jax import lax
from jax.experimental import pallas as pl
from jax.experimental.pallas import tpu as pltpu
from jax.sharding import PartitionSpec as P

WIDTH = 2304
META = 16
LANES = 128
branch_scale = 1.4 / math.sqrt(40.0)
epsilon = 1e-05
f32, bf16 = jnp.float32, jnp.bfloat16

VMEM = pl.BlockSpec(memory_space=pltpu.VMEM)
SMEM = pl.BlockSpec(memory_space=pltpu.SMEM)
ANY = pl.BlockSpec(memory_space=pl.ANY)


def up_to(n, step=LANES):
    return -(-n // step) * step


def params(mib=16):
    return pltpu.CompilerParams(vmem_limit_bytes=mib * 2**20)


def cost(flops, bytes_accessed):
    return pl.CostEstimate(flops=flops, bytes_accessed=bytes_accessed, transcendentals=0)


def shape(dims, dtype):
    return jax.ShapeDtypeStruct(dims, dtype)


def prep_kernel(tallies, x, gain, routes, out, ends):
    block, tokens = x.shape
    v = x[...]
    wide = up_to(block)
    g = jnp.concatenate([gain[...], jnp.zeros((1, wide - block), f32)], axis=1)
    g = jnp.broadcast_to(g, (LANES, wide)).T[0:block, 0:1]
    out[0:block] = (v * g).astype(bf16)
    sq = jnp.sum(v * v, axis=0, keepdims=True)
    hi = sq.astype(bf16).astype(f32)
    mid = (sq - hi).astype(bf16).astype(f32)
    here = lax.broadcasted_iota(jnp.int32, (1, tokens), 1)
    mark, end = jnp.zeros((1, tokens), f32), jnp.int32(-1)
    for q in range(ends.shape[0]):
        end = end + tallies[0, q]
        mark = jnp.where(here == end, q + 1.0, mark)
    rows = [routes[...].astype(f32), hi, mid, sq - hi - mid, mark]
    rows.append(jnp.zeros((META - 6, tokens), f32))
    out[block:] = jnp.concatenate(rows, axis=0).astype(bf16)
    ends[...] = columns_at(mark, v)[0 : ends.shape[0]]


def columns_at(mark, v):
    row = lax.broadcasted_iota(jnp.int32, (8, mark.shape[1]), 0)
    pick = jnp.where(mark == (row + 1).astype(f32), 1.0, 0.0)
    return lax.dot_general(
        pick, v, (((1,), (1,)), ((), ())), precision=lax.Precision.HIGHEST, preferred_element_type=f32
    )


def whole_spec(v):
    return pl.BlockSpec(v.shape, lambda *_: (0,) * len(v.shape))


def prep_call(x, gain, routes, tallies):
    block, tokens = x.shape
    reqs = tallies.shape[1]
    outs = [shape((block + META, tokens), bf16), shape((reqs, block), f32)]
    return pl.pallas_call(
        prep_kernel,
        grid=(1,),
        in_specs=[SMEM] + [whole_spec(v) for v in (x, gain, routes)],
        out_specs=[whole_spec(v) for v in outs],
        out_shape=outs,
        compiler_params=params(),
        cost_estimate=cost(4 * tokens * block, 6 * tokens * block),
        name="prep",
    )(tallies, x, gain, routes)


def join_call(blocks):
    rows, tokens = blocks[0].shape

    def join_kernel(*refs):
        for i, ref in enumerate(refs[:-1]):
            refs[-1][i * rows : (i + 1) * rows] = ref[...]

    return pl.pallas_call(
        join_kernel,
        in_specs=[VMEM] * len(blocks),
        out_specs=VMEM,
        out_shape=shape((len(blocks) * rows, tokens), bf16),
        compiler_params=params(),
        cost_estimate=cost(0, 4 * len(blocks) * rows * tokens),
        name="join",
    )(*blocks)


EXTRA = 5


def spread_lanes(v, base):
    lane = lax.broadcasted_iota(jnp.int32, v.shape, 1)
    hi = v.astype(bf16).astype(f32)
    return jnp.where(lane < base, v, jnp.where(lane < base + EXTRA, hi, v - hi)).astype(bf16)


def joined_lanes(v, base):
    lane = lax.broadcasted_iota(jnp.int32, v.shape, 1)
    left, right = pltpu.roll(v, LANES - EXTRA, 1), pltpu.roll(v, EXTRA, 1)
    return v + jnp.where(lane < base, 0.0, jnp.where(lane < base + EXTRA, left, right))


def slot_columns(core, cols):
    first, second = cols[:, 0:1].astype(f32), cols[:, 1:2].astype(f32)
    zero = core == 0
    return jnp.where(zero, first, second), jnp.where(zero, second, first)


def partial_kernel(sides, held, scal, *refs):
    feeds, (wr, wg, wu), (own, give, cols, xs, xt, acc, extra) = refs[:held], refs[held : held + 3], refs[-7:]
    e = pl.program_id(0)
    core, side = scal[0], scal[1]
    depth, hidden = wg.shape[1:]
    deep, half = up_to(depth), up_to(hidden)
    base = hidden % LANES
    tokens = feeds[0].shape[1]
    block = depth // sides
    last = slice(2 * half - LANES, 2 * half)

    @pl.when(e == 0)
    def _():
        xs[depth:] = jnp.zeros((deep + LANES - depth, xs.shape[1]), bf16)
        for n, ref in enumerate(feeds):
            to = slice(n * tokens, (n + 1) * tokens)
            for i in range(sides):
                at = i * (block + META)
                xs[pl.ds(pl.multiple_of((side ^ i) * block, 16), block), to] = ref[at : at + block]
                xs[deep + i * META : deep + (i + 1) * META, to] = ref[at + block : at + block + META]
        xt[...] = xs[...].T
        more = xt[:, deep:]
        cols[...] = more
        more = more.astype(f32)
        sq = jnp.zeros((more.shape[0], 1), f32)
        for i in range(sides):
            for term in (4, 3, 2):
                sq = sq + more[:, i * META + term : i * META + term + 1]
        router = lax.dot_general(
            xt[:, 0:depth], wr[...], (((1,), (1,)), ((), ())), preferred_element_type=f32
        )
        lane = lax.broadcasted_iota(jnp.int32, router.shape, 1)
        extra[...] = router + jnp.where((lane == base) | (lane == base + EXTRA), sq, 0.0)
        for ref in (own, acc):
            ref[:, half - LANES : half] = jnp.zeros((xt.shape[0], LANES), f32)
            ref[:, last] = jnp.zeros((xt.shape[0], LANES), f32)

    mine, other = slot_columns(core, xt[:, deep : deep + LANES])
    ef = e.astype(f32)
    take = [(v == ef) | (e == 0) for v in (mine, other)]
    for which, w in enumerate((wg, wu)):
        for at in range(0, hidden, 256):
            end = min(hidden, at + 256)
            d = jnp.dot(xt[:, 0:depth], w[0, :, at:end], preferred_element_type=f32)
            to = slice(which * half + at, which * half + end)
            for ref, pick in ((own, take[0]), (acc, take[1])):
                ref[:, to] = jnp.where(pick, d, ref[:, to])

    @pl.when(e == pl.num_programs(0) - 1)
    def _():
        lane = lax.broadcasted_iota(jnp.int32, extra.shape, 1)
        more = extra[...]
        own[:, last] = jnp.where(lane < base, own[:, last], more)
        give[:, 0 : last.start] = acc[:, 0 : last.start].astype(bf16)
        give[:, last] = spread_lanes(jnp.where(lane < base, acc[:, last], more), base)


def partial_call(scal, sides, feeds, wr, wg, wu, deps):
    experts, depth, hidden = wg.shape
    tokens = feeds[0].shape[1] * len(feeds)
    deep, wide = up_to(depth), 2 * up_to(hidden)
    part = pl.BlockSpec((1, depth, hidden), lambda n: (n, 0, 0))
    outs = [shape((tokens, wide), f32), shape((tokens, wide), bf16), shape((tokens, LANES), bf16)]
    return pl.pallas_call(
        lambda *refs: partial_kernel(sides, len(feeds), *refs),
        grid=(experts,),
        in_specs=[SMEM] + [whole_spec(v) for v in feeds] + [whole_spec(wr), part, part] + [ANY] * len(deps),
        out_specs=[whole_spec(v) for v in outs],
        out_shape=outs,
        scratch_shapes=[
            pltpu.VMEM((deep + LANES, tokens), bf16),
            pltpu.VMEM((tokens, deep + LANES), bf16),
            pltpu.VMEM((tokens, wide), f32),
            pltpu.VMEM((tokens, LANES), f32),
        ],
        compiler_params=params(32),
        cost_estimate=cost(
            4 * experts * depth * hidden * tokens, 4 * experts * depth * hidden + 6 * tokens * wide
        ),
        name="gate_up_partial",
    )(scal, *feeds, wr, wg, wu, *deps)


def sum_kernel(base, scal, own, recv, *refs):
    keep, send = refs[-2:]
    y = scal[2]
    th, wide = keep.shape
    main = wide - LANES
    for to, first in ((keep, y), (send, 1 - y)):
        rows = pl.ds(pl.multiple_of(first * th, th), th)
        to[:, 0:main] = (own[rows, 0:main] + recv[rows, 0:main].astype(f32)).astype(to.dtype)
        v = own[rows, main:] + joined_lanes(recv[rows, main:].astype(f32), base)
        to[:, main:] = v if to is keep else spread_lanes(v, base)


def sum_call(scal, base, own, recv, deps):
    tokens, wide = own.shape
    return pl.pallas_call(
        lambda *refs: sum_kernel(base, *refs),
        in_specs=[SMEM, VMEM, VMEM] + [ANY] * len(deps),
        out_specs=[VMEM, VMEM],
        out_shape=[shape((tokens // 2, wide), f32), shape((tokens // 2, wide), bf16)],
        compiler_params=params(),
        cost_estimate=cost(tokens * wide, 9 * tokens * wide),
        name="core_sum",
    )(scal, own, recv, *deps)


def act_kernel(base, scal, keep, recv, cols, *refs):
    act = refs[-1]
    core, y = scal[0], scal[2]
    th, half = act.shape
    main = 2 * half - LANES
    m = keep[:, main:] + joined_lanes(recv[:, main:].astype(f32), base)
    mine, other = slot_columns(core, cols[pl.ds(pl.multiple_of(y * th, th), th)])
    scale = lax.rsqrt(m[:, base : base + 1] / WIDTH + epsilon)
    la = lb = jnp.zeros_like(scale)
    for e in range(4):
        logit = m[:, base + 1 + e : base + 2 + e] * scale
        la = jnp.where(mine == e, logit, la)
        lb = jnp.where(other == e, logit, lb)
    mix = scale / (1.0 + jnp.exp(lb - la))
    g = (keep[:, 0:half] + recv[:, 0:half].astype(f32)) * scale
    u = (keep[:, half:] + recv[:, half:].astype(f32)) * mix
    act[...] = (g / (1.0 + jnp.exp(-g)) * u).astype(bf16)


def act_call(scal, base, keep, recv, cols, deps):
    th, wide = keep.shape
    return pl.pallas_call(
        lambda *refs: act_kernel(base, *refs),
        in_specs=[SMEM] + [VMEM] * 3 + [ANY] * len(deps),
        out_specs=VMEM,
        out_shape=shape((th, wide // 2), bf16),
        compiler_params=params(),
        cost_estimate=cost(6 * th * wide, 7 * th * wide),
        name="act",
    )(scal, keep, recv, cols, *deps)


def down_kernel(sides, scal, a, a_y, b, b_y, cols, wd, *refs):
    outs = refs[-sides - 2 : -2]
    whole, acc = refs[-2:]
    e = pl.program_id(0)
    core, side, y = scal[0], scal[1], scal[2]
    th = a.shape[0]
    width, hidden = wd.shape[1:]
    block = width // sides

    @pl.when(e == 0)
    def _():
        for k, near, far in ((0, a, a_y), (1, b, b_y)):
            whole[k, pl.ds(pl.multiple_of(y * th, th), th)] = near[...]
            whole[k, pl.ds(pl.multiple_of((1 - y) * th, th), th)] = far[...]

    ef = e.astype(f32)
    masks = [jnp.where(v == ef, 1.0, 0.0).astype(bf16) for v in slot_columns(core, cols[...])]
    rows = whole[0, :, 0:hidden] * masks[0] + whole[1, :, 0:hidden] * masks[1]
    d = lax.dot_general(wd[0], rows, (((1,), (1,)), ((), ())), preferred_element_type=f32)

    @pl.when(e == 0)
    def _():
        acc[...] = d

    @pl.when(e > 0)
    def _():
        acc[...] += d

    @pl.when(e == pl.num_programs(0) - 1)
    def _():
        for i in range(sides):
            rows = pl.ds(pl.multiple_of((side ^ i) * block, 16), block)
            outs[i][...] = acc[rows].astype(bf16)


def down_call(scal, sides, pieces, cols, wd, deps):
    experts, width, hidden = wd.shape
    tokens = cols.shape[0]
    outs = [shape((width // sides, tokens), bf16)] * sides
    return pl.pallas_call(
        lambda *refs: down_kernel(sides, *refs),
        grid=(experts,),
        in_specs=[SMEM]
        + [whole_spec(v) for v in pieces]
        + [whole_spec(cols), pl.BlockSpec((1, width, hidden), lambda n: (n, 0, 0))]
        + [ANY] * len(deps),
        out_specs=[whole_spec(v) for v in outs],
        out_shape=outs,
        scratch_shapes=[
            pltpu.VMEM((2, tokens, pieces[0].shape[1]), bf16),
            pltpu.VMEM((width, tokens), f32),
        ],
        compiler_params=params(20),
        cost_estimate=cost(
            2 * experts * width * hidden * tokens, 2 * experts * width * hidden + 2 * width * tokens
        ),
        name="down",
    )(scal, *pieces, cols, wd, *deps)


def total_kernel(meta, stream, *refs):
    parts, (total, message) = refs[:-2], refs[-2:]
    v = parts[0][...].astype(f32)
    for ref in parts[1:]:
        v = v + ref[...].astype(f32)
    total[...] = v
    reqs = stream.shape[0]
    ends = columns_at(meta[5:6].astype(f32), v)
    ends = stream[...] + branch_scale * ends[0:reqs]
    message[...] = jnp.broadcast_to(ends[None], message.shape)


def total_call(feed, stream, parts, block, count):
    tokens = feed.shape[1]
    full = lambda v: pl.BlockSpec(v.shape, lambda n: (0,) * len(v.shape))
    outs = [shape((block, tokens), f32), shape((count, *stream.shape), f32)]
    return pl.pallas_call(
        total_kernel,
        grid=(1,),
        in_specs=[pl.BlockSpec((META, tokens), lambda n: (block // META, 0)), full(stream)]
        + [full(v) for v in parts],
        out_specs=[full(v) for v in outs],
        out_shape=outs,
        compiler_params=params(),
        cost_estimate=cost(16 * block * tokens, 14 * block * tokens),
        name="branch_total",
    )(feed, stream, *parts)


def head_kernel(order, got, gain, words, softness, logits, message, wide):
    blocks, block = gain.shape
    rows, columns = logits.shape
    ends, squares = [], 0.0
    for b in range(blocks):
        v = jnp.concatenate([got[i] for i in order[b]], axis=0)
        squares = squares + jnp.sum(v * v, axis=1, keepdims=True)
        ends.append(v)
    scale = lax.rsqrt(squares / WIDTH + epsilon)
    total = jnp.zeros((rows, columns), f32)
    for b in range(blocks):
        feed = (ends[b] * scale * gain[b : b + 1]).astype(bf16)
        total += jnp.dot(feed, words[b * block : (b + 1) * block], preferred_element_type=f32)
    total = total / (WIDTH / 256.0 * softness[...])
    logits[...] = total
    top = jnp.max(total, axis=1, keepdims=True)
    mass = jnp.sum(jnp.exp(total - top), axis=1, keepdims=True)
    wide[...] = jnp.zeros_like(wide)
    lane = lax.broadcasted_iota(jnp.int32, (rows, LANES), 1)
    wide[0:rows] = jnp.where(lane == 0, top, jnp.where(lane == 1, mass, 0.0))
    turned = wide[...].T
    message[...] = jnp.broadcast_to(turned[None, 0:2, 0:rows], message.shape)


def head_call(order, got, gain, words, softness):
    rows, columns = softness.shape[0], words.shape[1]
    return pl.pallas_call(
        lambda *refs: head_kernel(order, *refs),
        in_specs=[VMEM] * 4,
        out_specs=[VMEM, VMEM],
        out_shape=[shape((rows, columns), f32), shape((got.shape[0], 2, rows), f32)],
        scratch_shapes=[pltpu.VMEM((LANES, LANES), f32)],
        compiler_params=params(),
        cost_estimate=cost(2 * rows * WIDTH * columns, 2 * WIDTH * columns),
        name="head",
    )(got, gain, words, softness)


def body(
    skip_stream_arriving,
    chosen_specialists,
    sequence_piece_tallies,
    premix_rmsnorm_gain,
    dispatcher_weights,
    specialist_switch_weights,
    specialist_expand_weights,
    specialist_contract_weights,
    terminal_rmsnorm_gain,
    lexicon_projector_weights,
    softness_per_sequence,
):
    tokens, block = skip_stream_arriving.shape
    dp, mp = lax.axis_size("dp"), lax.axis_size("mp")
    count = dp * mp
    parts = 4
    spread, sides = dp // parts, mp // parts
    assert dp == parts * spread and mp == parts * sides and sides & (sides - 1) == 0
    part = lax.axis_index("dp") // spread
    y, core = part // 2, part % 2
    side = lax.axis_index("mp") % sides

    def send(value, to):
        pairs = []
        for q in range(parts):
            for r in range(spread):
                for z in range(parts):
                    for x in range(sides):
                        q2, z2, x2 = to(q, z, x)
                        source = (q * spread + r) * mp + z * sides + x
                        pairs.append((source, (q2 * spread + r) * mp + z2 * sides + x2))
        return lax.ppermute(value, ("dp", "mp"), pairs)

    other_core = lambda q, z, x: (q ^ 1, z, x)
    other_y = lambda q, z, x: (q ^ 2, z, x)
    home = lambda q, z, x: (z, q, x)

    scal = jnp.stack([core, side, y]).astype(jnp.int32)
    sent, stream = prep_call(
        skip_stream_arriving.T, premix_rmsnorm_gain[None], chosen_specialists.T, sequence_piece_tallies
    )
    wg, wu, wd = specialist_switch_weights, specialist_expand_weights, specialist_contract_weights
    if spread > 1:
        runs = [[q * spread + r for r in range(spread)] for q in range(parts)]
        wg = lax.all_gather(wg, "dp", axis=1, tiled=True, axis_index_groups=runs)
        wu = lax.all_gather(wu, "dp", axis=1, tiled=True, axis_index_groups=runs)
        wd = lax.all_gather(wd, "dp", axis=2, tiled=True, axis_index_groups=runs)
    wd = jnp.swapaxes(wd, 1, 2)
    depth, hidden = wg.shape[1:]
    base = hidden % LANES
    wr = lax.dynamic_slice_in_dim(dispatcher_weights.T, part * depth, depth, axis=1)
    room = lambda at: jnp.pad(wr, ((at, LANES - at - wr.shape[0]), (0, 0)))
    wr = room(base + 1) + room(base + 1 + EXTRA)

    chunks = ((1,), (2, 3), (0,))
    first = [send(sent, lambda q, z, x, i=i: (z, (q - 1) % parts, x ^ i)) for i in range(sides)]
    pair = join_call(first)
    feeds = {1: pair}
    for group in (2, 3, 0):
        feeds[group] = send(pair, lambda q, z, x, group=group: (q, (z - group + 1) % parts, x))
    stream = send(stream, home)
    partial, kept, pieces, shares = {}, {}, {}, {}

    def do_partial(s, *deps):
        own, give, cols = partial_call(scal, sides, [feeds[g] for g in chunks[s]], wr, wg, wu, deps)
        partial[s] = (own, send(give, other_core), cols)
        return own

    def do_sum(s, *deps):
        own, recv, _ = partial[s]
        keep, give = sum_call(scal, base, own, recv, deps)
        kept[s] = (keep, send(give, other_y))
        return keep

    def do_act(s, *deps):
        a = act_call(scal, base, *kept[s], partial[s][2], deps)
        a_y = send(a, other_y)
        pieces[s] = (a, a_y, send(a, other_core), send(a_y, other_core))
        return a

    def do_down(s, *deps):
        outs = down_call(scal, sides, pieces[s], partial[s][2], wd, deps)
        got = [outs[0]] + [send(outs[i], lambda q, z, x, i=i: (q, z, x ^ i)) for i in range(1, sides)]
        for n, group in enumerate(chunks[s]):
            to = slice(n * tokens, (n + 1) * tokens)
            if group == 0:
                shares[0] = [v[:, to] for v in got]
            else:
                share = sum(v[:, to].astype(f32) for v in got).astype(bf16)
                back = lambda q, z, x, group=group: (q, (z + group) % parts, x)
                shares[group] = [send(share, back)]
        return outs[0]

    p0 = do_partial(0)
    s0 = do_sum(0)
    p1 = do_partial(1, s0)
    s1 = do_sum(1)
    a0 = do_act(0, s1)
    p2 = do_partial(2, a0)
    s2 = do_sum(2)
    d0 = do_down(0, s2)
    a1 = do_act(1, d0)
    a2 = do_act(2, a1)
    d1 = do_down(1, a2)
    do_down(2, d1)
    mine = [v for group in range(parts) for v in shares[group]]
    total, message = total_call(feeds[0], stream, mine, block, count)

    everyone = lambda v: lax.all_to_all(v, ("dp", "mp"), 0, 0, tiled=True)
    got = everyone(message)
    branch = send(total, home)
    order = [
        [
            (q * spread + r) * mp + z * sides + x
            for z in range(parts)
            for r in range(spread)
        ]
        for q in range(parts)
        for x in range(sides)
    ]
    logits, pairs = head_call(
        order,
        got,
        terminal_rmsnorm_gain.reshape(mp, block),
        lexicon_projector_weights,
        softness_per_sequence[:, None],
    )
    pairs = everyone(pairs)
    new_hidden = skip_stream_arriving + branch_scale * branch.T
    largest = jnp.max(pairs[:, 0], axis=0)
    mass = jnp.sum(pairs[:, 1] * jnp.exp(pairs[:, 0] - largest), axis=0)
    logprobs = logits - largest[:, None] - jnp.log(mass)[:, None]
    return (new_hidden, logprobs)


def solution(mesh):
    return jax.shard_map(
        body,
        mesh=mesh,
        in_specs=(
            P("dp", "mp"),
            P("dp", None),
            P("dp", None),
            P("mp"),
            P(),
            P(None, "dp", "mp"),
            P(None, "dp", "mp"),
            P(None, "mp", "dp"),
            P(),
            P(None, ("dp", "mp")),
            P(),
        ),
        out_specs=(P("dp", "mp"), P(None, ("dp", "mp"))),
        check_vma=False,
    )
```

```python
import math

import jax
import jax.numpy as jnp
from jax import lax
from jax.experimental import pallas as pl
from jax.experimental.pallas import tpu as pltpu
from jax.sharding import PartitionSpec as P

WIDTH = 2304
META = 16
LANES = 128
branch_scale = 1.4 / math.sqrt(40.0)
epsilon = 1e-05
f32, bf16 = jnp.float32, jnp.bfloat16

VMEM = pl.BlockSpec(memory_space=pltpu.VMEM)
SMEM = pl.BlockSpec(memory_space=pltpu.SMEM)
ANY = pl.BlockSpec(memory_space=pl.ANY)
HBM = pl.BlockSpec(memory_space=pltpu.HBM)


def up_to(n, step=LANES):
    return -(-n // step) * step


def params(mib=16):
    return pltpu.CompilerParams(vmem_limit_bytes=mib * 2**20)


HINT = pl.CostEstimate(flops=1, bytes_accessed=1024, transcendentals=0)


def shape(dims, dtype):
    return jax.ShapeDtypeStruct(dims, dtype)


def prep_kernel(tallies, x, gain, routes, out, ends):
    block, tokens = x.shape
    v = x[...]
    wide = up_to(block)
    g = jnp.concatenate([gain[...], jnp.zeros((1, wide - block), f32)], axis=1)
    g = jnp.broadcast_to(g, (LANES, wide)).T[0:block, 0:1]
    out[0:block] = (v * g).astype(bf16)
    sq = jnp.sum(v * v, axis=0, keepdims=True)
    hi = sq.astype(bf16).astype(f32)
    mid = (sq - hi).astype(bf16).astype(f32)
    here = lax.broadcasted_iota(jnp.int32, (1, tokens), 1)
    mark, end = jnp.zeros((1, tokens), f32), jnp.int32(-1)
    for q in range(ends.shape[0]):
        end = end + tallies[0, q]
        mark = jnp.where(here == end, q + 1.0, mark)
    rows = [routes[...].astype(f32), hi, mid, sq - hi - mid, mark]
    rows.append(jnp.zeros((META - 6, tokens), f32))
    out[block:] = jnp.concatenate(rows, axis=0).astype(bf16)
    ends[...] = columns_at(mark, v)[0 : ends.shape[0]]


def columns_at(mark, v):
    row = lax.broadcasted_iota(jnp.int32, (8, mark.shape[1]), 0)
    pick = jnp.where(mark == (row + 1).astype(f32), 1.0, 0.0)
    return lax.dot_general(
        pick, v, (((1,), (1,)), ((), ())), precision=lax.Precision.HIGHEST, preferred_element_type=f32
    )


def whole_spec(v):
    return pl.BlockSpec(v.shape, lambda *_: (0,) * len(v.shape))


def prep_call(x, gain, routes, tallies):
    block, tokens = x.shape
    reqs = tallies.shape[1]
    outs = [shape((block + META, tokens), bf16), shape((reqs, block), f32)]
    return pl.pallas_call(
        prep_kernel,
        grid=(1,),
        in_specs=[SMEM] + [whole_spec(v) for v in (x, gain, routes)],
        out_specs=[whole_spec(v) for v in outs],
        out_shape=outs,
        compiler_params=params(),
        cost_estimate=HINT,
        name="prep",
    )(tallies, x, gain, routes)


def join_call(blocks):
    rows, tokens = blocks[0].shape

    def join_kernel(*refs):
        for i, ref in enumerate(refs[:-1]):
            refs[-1][i * rows : (i + 1) * rows] = ref[...]

    return pl.pallas_call(
        join_kernel,
        in_specs=[VMEM] * len(blocks),
        out_specs=VMEM,
        out_shape=shape((len(blocks) * rows, tokens), bf16),
        compiler_params=params(),
        cost_estimate=HINT,
        name="join",
    )(*blocks)


EXTRA = 5


def spread_lanes(v, base):
    lane = lax.broadcasted_iota(jnp.int32, v.shape, 1)
    hi = v.astype(bf16).astype(f32)
    return jnp.where(lane < base, v, jnp.where(lane < base + EXTRA, hi, v - hi)).astype(bf16)


def joined_lanes(v, base):
    lane = lax.broadcasted_iota(jnp.int32, v.shape, 1)
    left, right = pltpu.roll(v, LANES - EXTRA, 1), pltpu.roll(v, EXTRA, 1)
    return v + jnp.where(lane < base, 0.0, jnp.where(lane < base + EXTRA, left, right))


def slot_columns(core, cols):
    first, second = cols[:, 0:1].astype(f32), cols[:, 1:2].astype(f32)
    zero = core == 0
    return jnp.where(zero, first, second), jnp.where(zero, second, first)


def partial_kernel(sides, held, scal, *refs):
    feeds, (wr, wg, wu) = refs[:held], refs[held : held + 3]
    own, give, cols, xs, xt, acc, extra, ring, sems = refs[-9:]
    e = pl.program_id(0)
    experts = wg.shape[0]

    def fetch(n, slot, which):
        return pltpu.make_async_copy((wg, wu)[which].at[n], ring.at[slot, which], sems.at[slot, which])

    @pl.when(e == 0)
    def _():
        for n in range(min(2, experts)):
            for which in range(2):
                fetch(n, n, which).start()

    core, side = scal[0], scal[1]
    depth, hidden = wg.shape[1:]
    deep, half = up_to(depth), up_to(hidden)
    base = hidden % LANES
    tokens = feeds[0].shape[1]
    block = depth // sides
    last = slice(2 * half - LANES, 2 * half)

    @pl.when(e == 0)
    def _():
        xs[depth:] = jnp.zeros((deep + LANES - depth, xs.shape[1]), bf16)
        for n, ref in enumerate(feeds):
            to = slice(n * tokens, (n + 1) * tokens)
            for i in range(sides):
                at = i * (block + META)
                xs[pl.ds(pl.multiple_of((side ^ i) * block, 16), block), to] = ref[at : at + block]
                xs[deep + i * META : deep + (i + 1) * META, to] = ref[at + block : at + block + META]
        xt[...] = xs[...].T
        more = xt[:, deep:]
        cols[...] = more
        more = more.astype(f32)
        sq = jnp.zeros((more.shape[0], 1), f32)
        for i in range(sides):
            for term in (4, 3, 2):
                sq = sq + more[:, i * META + term : i * META + term + 1]
        router = lax.dot_general(
            xt[:, 0:depth], wr[...], (((1,), (1,)), ((), ())), preferred_element_type=f32
        )
        lane = lax.broadcasted_iota(jnp.int32, router.shape, 1)
        extra[...] = router + jnp.where((lane == base) | (lane == base + EXTRA), sq, 0.0)
        for ref in (own, acc):
            ref[:, half - LANES : half] = jnp.zeros((xt.shape[0], LANES), f32)
            ref[:, last] = jnp.zeros((xt.shape[0], LANES), f32)

    mine, other = slot_columns(core, xt[:, deep : deep + LANES])
    ef = e.astype(f32)
    take = [(v == ef) | (e == 0) for v in (mine, other)]
    slot = e % 2
    for which in range(2):
        fetch(e, slot, which).wait()
        for at in range(0, hidden, 256):
            end = min(hidden, at + 256)
            d = jnp.dot(xt[:, 0:depth], ring[slot, which, :, at:end], preferred_element_type=f32)
            to = slice(which * half + at, which * half + end)
            for ref, pick in ((own, take[0]), (acc, take[1])):
                ref[:, to] = jnp.where(pick, d, ref[:, to])

    @pl.when(e + 2 < experts)
    def _():
        for which in range(2):
            fetch(e + 2, slot, which).start()

    @pl.when(e == experts - 1)
    def _():
        lane = lax.broadcasted_iota(jnp.int32, extra.shape, 1)
        more = extra[...]
        own[:, last] = jnp.where(lane < base, own[:, last], more)
        give[:, 0 : last.start] = acc[:, 0 : last.start].astype(bf16)
        give[:, last] = spread_lanes(jnp.where(lane < base, acc[:, last], more), base)


def partial_call(scal, sides, feeds, wr, wg, wu, deps):
    experts, depth, hidden = wg.shape
    tokens = feeds[0].shape[1] * len(feeds)
    deep, wide = up_to(depth), 2 * up_to(hidden)
    outs = [shape((tokens, wide), f32), shape((tokens, wide), bf16), shape((tokens, LANES), bf16)]
    return pl.pallas_call(
        lambda *refs: partial_kernel(sides, len(feeds), *refs),
        grid=(experts,),
        in_specs=[SMEM] + [whole_spec(v) for v in feeds] + [whole_spec(wr), HBM, HBM] + [ANY] * len(deps),
        out_specs=[whole_spec(v) for v in outs],
        out_shape=outs,
        scratch_shapes=[
            pltpu.VMEM((deep + LANES, tokens), bf16),
            pltpu.VMEM((tokens, deep + LANES), bf16),
            pltpu.VMEM((tokens, wide), f32),
            pltpu.VMEM((tokens, LANES), f32),
            pltpu.VMEM((2, 2, depth, hidden), bf16),
            pltpu.SemaphoreType.DMA((2, 2)),
        ],
        compiler_params=params(20),
        cost_estimate=HINT,
        name="gate_up_partial",
    )(scal, *feeds, wr, wg, wu, *deps)


def sum_kernel(base, scal, own, recv, *refs):
    keep, send = refs[-2:]
    y = scal[2]
    th, wide = keep.shape
    main = wide - LANES
    for to, first in ((keep, y), (send, 1 - y)):
        rows = pl.ds(pl.multiple_of(first * th, th), th)
        to[:, 0:main] = (own[rows, 0:main] + recv[rows, 0:main].astype(f32)).astype(to.dtype)
        v = own[rows, main:] + joined_lanes(recv[rows, main:].astype(f32), base)
        to[:, main:] = v if to is keep else spread_lanes(v, base)


def sum_call(scal, base, own, recv, deps):
    tokens, wide = own.shape
    return pl.pallas_call(
        lambda *refs: sum_kernel(base, *refs),
        in_specs=[SMEM, VMEM, VMEM] + [ANY] * len(deps),
        out_specs=[VMEM, VMEM],
        out_shape=[shape((tokens // 2, wide), f32), shape((tokens // 2, wide), bf16)],
        compiler_params=params(),
        cost_estimate=HINT,
        name="core_sum",
    )(scal, own, recv, *deps)


def act_kernel(base, scal, keep, recv, cols, *refs):
    act = refs[-1]
    core, y = scal[0], scal[2]
    th, half = act.shape
    main = 2 * half - LANES
    m = keep[:, main:] + joined_lanes(recv[:, main:].astype(f32), base)
    mine, other = slot_columns(core, cols[pl.ds(pl.multiple_of(y * th, th), th)])
    scale = lax.rsqrt(m[:, base : base + 1] / WIDTH + epsilon)
    la = lb = jnp.zeros_like(scale)
    for e in range(4):
        logit = m[:, base + 1 + e : base + 2 + e] * scale
        la = jnp.where(mine == e, logit, la)
        lb = jnp.where(other == e, logit, lb)
    mix = scale / (1.0 + jnp.exp(lb - la))
    g = (keep[:, 0:half] + recv[:, 0:half].astype(f32)) * scale
    u = (keep[:, half:] + recv[:, half:].astype(f32)) * mix
    act[...] = (g / (1.0 + jnp.exp(-g)) * u).astype(bf16)


def act_call(scal, base, keep, recv, cols, deps):
    th, wide = keep.shape
    return pl.pallas_call(
        lambda *refs: act_kernel(base, *refs),
        in_specs=[SMEM] + [VMEM] * 3 + [ANY] * len(deps),
        out_specs=VMEM,
        out_shape=shape((th, wide // 2), bf16),
        compiler_params=params(),
        cost_estimate=HINT,
        name="act",
    )(scal, keep, recv, cols, *deps)


def down_kernel(sides, scal, a, a_y, b, b_y, cols, wd, *refs):
    outs = refs[-sides - 2 : -2]
    whole, acc = refs[-2:]
    e = pl.program_id(0)
    core, side, y = scal[0], scal[1], scal[2]
    th = a.shape[0]
    width, hidden = wd.shape[1:]
    block = width // sides

    @pl.when(e == 0)
    def _():
        for k, near, far in ((0, a, a_y), (1, b, b_y)):
            whole[k, pl.ds(pl.multiple_of(y * th, th), th)] = near[...]
            whole[k, pl.ds(pl.multiple_of((1 - y) * th, th), th)] = far[...]

    ef = e.astype(f32)
    masks = [jnp.where(v == ef, 1.0, 0.0).astype(bf16) for v in slot_columns(core, cols[...])]
    rows = whole[0, :, 0:hidden] * masks[0] + whole[1, :, 0:hidden] * masks[1]
    d = lax.dot_general(wd[0], rows, (((1,), (1,)), ((), ())), preferred_element_type=f32)

    @pl.when(e == 0)
    def _():
        acc[...] = d

    @pl.when(e > 0)
    def _():
        acc[...] += d

    @pl.when(e == pl.num_programs(0) - 1)
    def _():
        for i in range(sides):
            rows = pl.ds(pl.multiple_of((side ^ i) * block, 16), block)
            outs[i][...] = acc[rows].astype(bf16)


def down_call(scal, sides, pieces, cols, wd, deps):
    experts, width, hidden = wd.shape
    tokens = cols.shape[0]
    outs = [shape((width // sides, tokens), bf16)] * sides
    return pl.pallas_call(
        lambda *refs: down_kernel(sides, *refs),
        grid=(experts,),
        in_specs=[SMEM]
        + [whole_spec(v) for v in pieces]
        + [whole_spec(cols), pl.BlockSpec((1, width, hidden), lambda n: (n, 0, 0))]
        + [ANY] * len(deps),
        out_specs=[whole_spec(v) for v in outs],
        out_shape=outs,
        scratch_shapes=[
            pltpu.VMEM((2, tokens, pieces[0].shape[1]), bf16),
            pltpu.VMEM((width, tokens), f32),
        ],
        compiler_params=params(20),
        cost_estimate=HINT,
        name="down",
    )(scal, *pieces, cols, wd, *deps)


def total_kernel(meta, stream, *refs):
    parts, (total, message) = refs[:-2], refs[-2:]
    v = parts[0][...].astype(f32)
    for ref in parts[1:]:
        v = v + ref[...].astype(f32)
    total[...] = v
    reqs = stream.shape[0]
    ends = columns_at(meta[5:6].astype(f32), v)
    ends = stream[...] + branch_scale * ends[0:reqs]
    message[...] = jnp.broadcast_to(ends[None], message.shape)


def total_call(feed, stream, parts, block, count):
    tokens = feed.shape[1]
    full = lambda v: pl.BlockSpec(v.shape, lambda n: (0,) * len(v.shape))
    outs = [shape((block, tokens), f32), shape((count, *stream.shape), f32)]
    return pl.pallas_call(
        total_kernel,
        grid=(1,),
        in_specs=[pl.BlockSpec((META, tokens), lambda n: (block // META, 0)), full(stream)]
        + [full(v) for v in parts],
        out_specs=[full(v) for v in outs],
        out_shape=outs,
        compiler_params=params(),
        cost_estimate=HINT,
        name="branch_total",
    )(feed, stream, *parts)


def head_kernel(order, got, gain, words, softness, logits, message, wide):
    blocks, block = gain.shape
    rows, columns = logits.shape
    ends, squares = [], 0.0
    for b in range(blocks):
        v = jnp.concatenate([got[i] for i in order[b]], axis=0)
        squares = squares + jnp.sum(v * v, axis=1, keepdims=True)
        ends.append(v)
    scale = lax.rsqrt(squares / WIDTH + epsilon)
    total = jnp.zeros((rows, columns), f32)
    for b in range(blocks):
        feed = (ends[b] * scale * gain[b : b + 1]).astype(bf16)
        total += jnp.dot(feed, words[b * block : (b + 1) * block], preferred_element_type=f32)
    total = total / (WIDTH / 256.0 * softness[...])
    logits[...] = total
    top = jnp.max(total, axis=1, keepdims=True)
    mass = jnp.sum(jnp.exp(total - top), axis=1, keepdims=True)
    wide[...] = jnp.zeros_like(wide)
    lane = lax.broadcasted_iota(jnp.int32, (rows, LANES), 1)
    wide[0:rows] = jnp.where(lane == 0, top, jnp.where(lane == 1, mass, 0.0))
    turned = wide[...].T
    message[...] = jnp.broadcast_to(turned[None, 0:2, 0:rows], message.shape)


def head_call(order, got, gain, words, softness):
    rows, columns = softness.shape[0], words.shape[1]
    return pl.pallas_call(
        lambda *refs: head_kernel(order, *refs),
        in_specs=[VMEM] * 4,
        out_specs=[VMEM, VMEM],
        out_shape=[shape((rows, columns), f32), shape((got.shape[0], 2, rows), f32)],
        scratch_shapes=[pltpu.VMEM((LANES, LANES), f32)],
        compiler_params=params(),
        cost_estimate=HINT,
        name="head",
    )(got, gain, words, softness)


def body(
    skip_stream_arriving,
    chosen_specialists,
    sequence_piece_tallies,
    premix_rmsnorm_gain,
    dispatcher_weights,
    specialist_switch_weights,
    specialist_expand_weights,
    specialist_contract_weights,
    terminal_rmsnorm_gain,
    lexicon_projector_weights,
    softness_per_sequence,
):
    tokens, block = skip_stream_arriving.shape
    dp, mp = lax.axis_size("dp"), lax.axis_size("mp")
    count = dp * mp
    parts = 4
    spread, sides = dp // parts, mp // parts
    assert dp == parts * spread and mp == parts * sides and sides & (sides - 1) == 0
    part = lax.axis_index("dp") // spread
    y, core = part // 2, part % 2
    side = lax.axis_index("mp") % sides

    def send(value, to):
        pairs = []
        for q in range(parts):
            for r in range(spread):
                for z in range(parts):
                    for x in range(sides):
                        q2, z2, x2 = to(q, z, x)
                        source = (q * spread + r) * mp + z * sides + x
                        pairs.append((source, (q2 * spread + r) * mp + z2 * sides + x2))
        return lax.ppermute(value, ("dp", "mp"), pairs)

    other_core = lambda q, z, x: (q ^ 1, z, x)
    other_y = lambda q, z, x: (q ^ 2, z, x)
    home = lambda q, z, x: (z, q, x)

    scal = jnp.stack([core, side, y]).astype(jnp.int32)
    sent, stream = prep_call(
        skip_stream_arriving.T, premix_rmsnorm_gain[None], chosen_specialists.T, sequence_piece_tallies
    )
    wg, wu, wd = specialist_switch_weights, specialist_expand_weights, specialist_contract_weights
    if spread > 1:
        runs = [[q * spread + r for r in range(spread)] for q in range(parts)]
        wg = lax.all_gather(wg, "dp", axis=1, tiled=True, axis_index_groups=runs)
        wu = lax.all_gather(wu, "dp", axis=1, tiled=True, axis_index_groups=runs)
        wd = lax.all_gather(wd, "dp", axis=2, tiled=True, axis_index_groups=runs)
    wd = jnp.swapaxes(wd, 1, 2)
    depth, hidden = wg.shape[1:]
    base = hidden % LANES
    wr = lax.dynamic_slice_in_dim(dispatcher_weights.T, part * depth, depth, axis=1)
    room = lambda at: jnp.pad(wr, ((at, LANES - at - wr.shape[0]), (0, 0)))
    wr = room(base + 1) + room(base + 1 + EXTRA)

    chunks = ((1,), (2,), (3,), (0,))
    first = [send(sent, lambda q, z, x, i=i: (z, (q - 1) % parts, x ^ i)) for i in range(sides)]
    pair = join_call(first)
    feeds = {1: pair}
    for group in (2, 3, 0):
        feeds[group] = send(feeds[(group - 1) % parts], lambda q, z, x: (q, (z - 1) % parts, x))
    stream = send(stream, home)
    partial, kept, pieces, shares = {}, {}, {}, {}

    def do_partial(s, *deps):
        own, give, cols = partial_call(scal, sides, [feeds[g] for g in chunks[s]], wr, wg, wu, deps)
        partial[s] = (own, send(give, other_core), cols)
        return own

    def do_sum(s, *deps):
        own, recv, _ = partial[s]
        keep, give = sum_call(scal, base, own, recv, deps)
        kept[s] = (keep, send(give, other_y))
        return keep

    def do_act(s, *deps):
        a = act_call(scal, base, *kept[s], partial[s][2], deps)
        a_y = send(a, other_y)
        pieces[s] = (a, a_y, send(a, other_core), send(a_y, other_core))
        return a

    def do_down(s, *deps):
        outs = down_call(scal, sides, pieces[s], partial[s][2], wd, deps)
        got = [outs[0]] + [send(outs[i], lambda q, z, x, i=i: (q, z, x ^ i)) for i in range(1, sides)]
        for n, group in enumerate(chunks[s]):
            to = slice(n * tokens, (n + 1) * tokens)
            if group == 0:
                shares[0] = [v[:, to] for v in got]
            else:
                share = sum(v[:, to].astype(f32) for v in got).astype(bf16)
                back = lambda q, z, x, group=group: (q, (z + group) % parts, x)
                shares[group] = [send(share, back)]
        return outs[0]

    p0 = do_partial(0)
    p1 = do_partial(1, p0)
    s0 = do_sum(0, p1)
    p2 = do_partial(2, s0)
    s1 = do_sum(1, p2)
    p3 = do_partial(3, s1)
    s2 = do_sum(2, p3)
    a0 = do_act(0, s2)
    s3 = do_sum(3, a0)
    a1 = do_act(1, s3)
    d0 = do_down(0, a1)
    a2 = do_act(2, d0)
    d1 = do_down(1, a2)
    a3 = do_act(3, d1)
    d2 = do_down(2, a3)
    do_down(3, d2)
    mine = [v for group in range(parts) for v in shares[group]]
    total, message = total_call(feeds[0], stream, mine, block, count)

    everyone = lambda v: lax.all_to_all(v, ("dp", "mp"), 0, 0, tiled=True)
    got = everyone(message)
    branch = send(total, home)
    order = [
        [
            (q * spread + r) * mp + z * sides + x
            for z in range(parts)
            for r in range(spread)
        ]
        for q in range(parts)
        for x in range(sides)
    ]
    logits, pairs = head_call(
        order,
        got,
        terminal_rmsnorm_gain.reshape(mp, block),
        lexicon_projector_weights,
        softness_per_sequence[:, None],
    )
    pairs = everyone(pairs)
    new_hidden = skip_stream_arriving + branch_scale * branch.T
    largest = jnp.max(pairs[:, 0], axis=0)
    mass = jnp.sum(pairs[:, 1] * jnp.exp(pairs[:, 0] - largest), axis=0)
    logprobs = logits - largest[:, None] - jnp.log(mass)[:, None]
    return (new_hidden, logprobs)


def solution(mesh):
    return jax.shard_map(
        body,
        mesh=mesh,
        in_specs=(
            P("dp", "mp"),
            P("dp", None),
            P("dp", None),
            P("mp"),
            P(),
            P(None, "dp", "mp"),
            P(None, "dp", "mp"),
            P(None, "mp", "dp"),
            P(),
            P(None, ("dp", "mp")),
            P(),
        ),
        out_specs=(P("dp", "mp"), P(None, ("dp", "mp"))),
        check_vma=False,
    )
```

```python
import math

import jax
import jax.numpy as jnp
from jax import lax
from jax.experimental import pallas as pl
from jax.experimental.pallas import tpu as pltpu
from jax.sharding import PartitionSpec as P

WIDTH = 2304
META = 16
LANES = 128
branch_scale = 1.4 / math.sqrt(40.0)
epsilon = 1e-05
f32, bf16 = jnp.float32, jnp.bfloat16

VMEM = pl.BlockSpec(memory_space=pltpu.VMEM)
SMEM = pl.BlockSpec(memory_space=pltpu.SMEM)
ANY = pl.BlockSpec(memory_space=pl.ANY)


def up_to(n, step=LANES):
    return -(-n // step) * step


def params(mib=16):
    return pltpu.CompilerParams(vmem_limit_bytes=mib * 2**20)


HINT = pl.CostEstimate(flops=1, bytes_accessed=1024, transcendentals=0)


def shape(dims, dtype):
    return jax.ShapeDtypeStruct(dims, dtype)


def prep_kernel(tallies, x, gain, routes, out, ends):
    block, tokens = x.shape
    v = x[...]
    wide = up_to(block)
    g = jnp.concatenate([gain[...], jnp.zeros((1, wide - block), f32)], axis=1)
    g = jnp.broadcast_to(g, (LANES, wide)).T[0:block, 0:1]
    out[0:block] = (v * g).astype(bf16)
    sq = jnp.sum(v * v, axis=0, keepdims=True)
    hi = sq.astype(bf16).astype(f32)
    mid = (sq - hi).astype(bf16).astype(f32)
    here = lax.broadcasted_iota(jnp.int32, (1, tokens), 1)
    mark, end = jnp.zeros((1, tokens), f32), jnp.int32(-1)
    for q in range(ends.shape[0]):
        end = end + tallies[0, q]
        mark = jnp.where(here == end, q + 1.0, mark)
    rows = [routes[...].astype(f32), hi, mid, sq - hi - mid, mark]
    rows.append(jnp.zeros((META - 6, tokens), f32))
    out[block:] = jnp.concatenate(rows, axis=0).astype(bf16)
    ends[...] = columns_at(mark, v)[0 : ends.shape[0]]


def columns_at(mark, v):
    row = lax.broadcasted_iota(jnp.int32, (8, mark.shape[1]), 0)
    pick = jnp.where(mark == (row + 1).astype(f32), 1.0, 0.0)
    return lax.dot_general(
        pick, v, (((1,), (1,)), ((), ())), precision=lax.Precision.HIGHEST, preferred_element_type=f32
    )


def whole_spec(v):
    return pl.BlockSpec(v.shape, lambda *_: (0,) * len(v.shape))


def prep_call(x, gain, routes, tallies):
    block, tokens = x.shape
    reqs = tallies.shape[1]
    outs = [shape((block + META, tokens), bf16), shape((reqs, block), f32)]
    return pl.pallas_call(
        prep_kernel,
        grid=(1,),
        in_specs=[SMEM] + [whole_spec(v) for v in (x, gain, routes)],
        out_specs=[whole_spec(v) for v in outs],
        out_shape=outs,
        compiler_params=params(),
        cost_estimate=HINT,
        name="prep",
    )(tallies, x, gain, routes)


def join_call(blocks):
    rows, tokens = blocks[0].shape

    def join_kernel(*refs):
        for i, ref in enumerate(refs[:-1]):
            refs[-1][i * rows : (i + 1) * rows] = ref[...]

    return pl.pallas_call(
        join_kernel,
        in_specs=[VMEM] * len(blocks),
        out_specs=VMEM,
        out_shape=shape((len(blocks) * rows, tokens), bf16),
        compiler_params=params(),
        cost_estimate=HINT,
        name="join",
    )(*blocks)


EXTRA = 5


def spread_lanes(v, base):
    lane = lax.broadcasted_iota(jnp.int32, v.shape, 1)
    hi = v.astype(bf16).astype(f32)
    return jnp.where(lane < base, v, jnp.where(lane < base + EXTRA, hi, v - hi)).astype(bf16)


def joined_lanes(v, base):
    lane = lax.broadcasted_iota(jnp.int32, v.shape, 1)
    left, right = pltpu.roll(v, LANES - EXTRA, 1), pltpu.roll(v, EXTRA, 1)
    return v + jnp.where(lane < base, 0.0, jnp.where(lane < base + EXTRA, left, right))


def slot_columns(core, cols):
    first, second = cols[:, 0:1].astype(f32), cols[:, 1:2].astype(f32)
    zero = core == 0
    return jnp.where(zero, first, second), jnp.where(zero, second, first)


def partial_kernel(sides, held, scal, *refs):
    feeds, (wr, wg, wu) = refs[:held], refs[held : held + 3]
    own, give, cols, xs, xt, acc, extra = refs[-7:]
    e = pl.program_id(0)
    core, side = scal[0], scal[1]
    depth, hidden = wg.shape[1:]
    deep, half = up_to(depth), up_to(hidden)
    base = hidden % LANES
    tokens = feeds[0].shape[1]
    block = depth // sides
    last = slice(2 * half - LANES, 2 * half)

    @pl.when(e == 0)
    def _():
        xs[depth:] = jnp.zeros((deep + LANES - depth, xs.shape[1]), bf16)
        for n, ref in enumerate(feeds):
            to = slice(n * tokens, (n + 1) * tokens)
            for i in range(sides):
                at = i * (block + META)
                xs[pl.ds(pl.multiple_of((side ^ i) * block, 16), block), to] = ref[at : at + block]
                xs[deep + i * META : deep + (i + 1) * META, to] = ref[at + block : at + block + META]
        xt[...] = xs[...].T
        more = xt[:, deep:]
        cols[...] = more
        more = more.astype(f32)
        sq = jnp.zeros((more.shape[0], 1), f32)
        for i in range(sides):
            for term in (4, 3, 2):
                sq = sq + more[:, i * META + term : i * META + term + 1]
        router = lax.dot_general(
            xt[:, 0:depth], wr[...], (((1,), (1,)), ((), ())), preferred_element_type=f32
        )
        lane = lax.broadcasted_iota(jnp.int32, router.shape, 1)
        extra[...] = router + jnp.where((lane == base) | (lane == base + EXTRA), sq, 0.0)
        for ref in (own, acc):
            ref[:, half - LANES : half] = jnp.zeros((xt.shape[0], LANES), f32)
            ref[:, last] = jnp.zeros((xt.shape[0], LANES), f32)

    mine, other = slot_columns(core, xt[:, deep : deep + LANES])
    ef = e.astype(f32)
    take = [(v == ef) | (e == 0) for v in (mine, other)]
    for which, w in enumerate((wg, wu)):
        for at in range(0, hidden, 256):
            end = min(hidden, at + 256)
            d = jnp.dot(xt[:, 0:depth], w[0, :, at:end], preferred_element_type=f32)
            to = slice(which * half + at, which * half + end)
            for ref, pick in ((own, take[0]), (acc, take[1])):
                ref[:, to] = jnp.where(pick, d, ref[:, to])

    @pl.when(e == pl.num_programs(0) - 1)
    def _():
        lane = lax.broadcasted_iota(jnp.int32, extra.shape, 1)
        more = extra[...]
        own[:, last] = jnp.where(lane < base, own[:, last], more)
        give[:, 0 : last.start] = acc[:, 0 : last.start].astype(bf16)
        give[:, last] = spread_lanes(jnp.where(lane < base, acc[:, last], more), base)


def partial_call(scal, sides, feeds, wr, wg, wu, deps):
    experts, depth, hidden = wg.shape
    tokens = feeds[0][0].shape[-1] * len(feeds)
    deep, wide = up_to(depth), 2 * up_to(hidden)
    part = pl.BlockSpec((1, depth, hidden), lambda n, s: (n, 0, 0))
    outs = [shape((tokens, wide), f32), shape((tokens, wide), bf16), shape((tokens, LANES), bf16)]
    feed_specs = []
    for v, place in feeds:
        if place is None:
            feed_specs.append(whole_spec(v))
        else:
            feed_specs.append(pl.BlockSpec((None, *v.shape[1:]), lambda n, s, place=place: (s[place], 0, 0)))
    return pl.pallas_call(
        lambda *refs: partial_kernel(sides, len(feeds), *refs),
        grid_spec=pltpu.PrefetchScalarGridSpec(
            num_scalar_prefetch=1,
            grid=(experts,),
            in_specs=feed_specs + [whole_spec(wr), part, part] + [ANY] * len(deps),
            out_specs=[whole_spec(v) for v in outs],
            scratch_shapes=[
                pltpu.VMEM((deep + LANES, tokens), bf16),
                pltpu.VMEM((tokens, deep + LANES), bf16),
                pltpu.VMEM((tokens, wide), f32),
                pltpu.VMEM((tokens, LANES), f32),
            ],
        ),
        out_shape=outs,
        compiler_params=params(20),
        cost_estimate=HINT,
        name="gate_up_partial",
    )(scal, *[v for v, _ in feeds], wr, wg, wu, *deps)


def sum_kernel(base, scal, own, recv, *refs):
    keep, send = refs[-2:]
    y = scal[2]
    th, wide = keep.shape
    main = wide - LANES
    for to, first in ((keep, y), (send, 1 - y)):
        rows = pl.ds(pl.multiple_of(first * th, th), th)
        to[:, 0:main] = (own[rows, 0:main] + recv[rows, 0:main].astype(f32)).astype(to.dtype)
        v = own[rows, main:] + joined_lanes(recv[rows, main:].astype(f32), base)
        to[:, main:] = v if to is keep else spread_lanes(v, base)


def sum_call(scal, base, own, recv, deps):
    tokens, wide = own.shape
    return pl.pallas_call(
        lambda *refs: sum_kernel(base, *refs),
        in_specs=[SMEM, VMEM, VMEM] + [ANY] * len(deps),
        out_specs=[VMEM, VMEM],
        out_shape=[shape((tokens // 2, wide), f32), shape((tokens // 2, wide), bf16)],
        compiler_params=params(),
        cost_estimate=HINT,
        name="core_sum",
    )(scal, own, recv, *deps)


def act_kernel(base, scal, keep, recv, cols, *refs):
    act = refs[-1]
    core, y = scal[0], scal[2]
    th, half = act.shape
    main = 2 * half - LANES
    recv = recv.at[1 - y]
    m = keep[:, main:] + joined_lanes(recv[:, main:].astype(f32), base)
    mine, other = slot_columns(core, cols[pl.ds(pl.multiple_of(y * th, th), th)])
    scale = lax.rsqrt(m[:, base : base + 1] / WIDTH + epsilon)
    la = lb = jnp.zeros_like(scale)
    for e in range(4):
        logit = m[:, base + 1 + e : base + 2 + e] * scale
        la = jnp.where(mine == e, logit, la)
        lb = jnp.where(other == e, logit, lb)
    mix = scale / (1.0 + jnp.exp(lb - la))
    g = (keep[:, 0:half] + recv[:, 0:half].astype(f32)) * scale
    u = (keep[:, half:] + recv[:, half:].astype(f32)) * mix
    act[...] = (g / (1.0 + jnp.exp(-g)) * u).astype(bf16)


def act_call(scal, base, keep, recv, cols, deps):
    th, wide = keep.shape
    return pl.pallas_call(
        lambda *refs: act_kernel(base, *refs),
        in_specs=[SMEM] + [VMEM] * 3 + [ANY] * len(deps),
        out_specs=VMEM,
        out_shape=shape((th, wide // 2), bf16),
        compiler_params=params(),
        cost_estimate=HINT,
        name="act",
    )(scal, keep, recv, cols, *deps)


def down_kernel(sides, scal, mine, other, cols, wd, *refs):
    outs, acc = refs[-sides - 1 : -1], refs[-1]
    e = pl.program_id(0)
    core, side = scal[0], scal[1]
    width, hidden = wd.shape[1:]
    block = width // sides
    ef = e.astype(f32)
    masks = [jnp.where(v == ef, 1.0, 0.0).astype(bf16) for v in slot_columns(core, cols[...])]
    rows = mine[:, 0:hidden] * masks[0] + other[:, 0:hidden] * masks[1]
    d = lax.dot_general(wd[0], rows, (((1,), (1,)), ((), ())), preferred_element_type=f32)

    @pl.when(e == 0)
    def _():
        acc[...] = d

    @pl.when(e > 0)
    def _():
        acc[...] += d

    @pl.when(e == pl.num_programs(0) - 1)
    def _():
        for i in range(sides):
            rows = pl.ds(pl.multiple_of((side ^ i) * block, 16), block)
            outs[i][...] = acc[rows].astype(bf16)


def down_call(scal, sides, pieces, cols, wd, deps):
    experts, width, hidden = wd.shape
    tokens = cols.shape[0]
    outs = [shape((width // sides, tokens), bf16)] * sides
    return pl.pallas_call(
        lambda *refs: down_kernel(sides, *refs),
        grid=(experts,),
        in_specs=[SMEM]
        + [whole_spec(v) for v in pieces]
        + [whole_spec(cols), pl.BlockSpec((1, width, hidden), lambda n: (n, 0, 0))]
        + [ANY] * len(deps),
        out_specs=[whole_spec(v) for v in outs],
        out_shape=outs,
        scratch_shapes=[pltpu.VMEM((width, tokens), f32)],
        compiler_params=params(16),
        cost_estimate=HINT,
        name="down",
    )(scal, *pieces, cols, wd, *deps)


def total_kernel(cols, stream, *refs):
    parts, (total, message) = refs[:-2], refs[-2:]
    v = parts[0][...].astype(f32)
    for ref in parts[1:]:
        v = v + ref[...].astype(f32)
    total[...] = v
    reqs = stream.shape[0]
    ends = columns_at(cols[...].astype(f32).T[5:6], v)
    ends = stream[...] + branch_scale * ends[0:reqs]
    message[...] = jnp.broadcast_to(ends[None], message.shape)


def total_call(cols, stream, parts, block, count):
    outs = [shape((block, cols.shape[0]), f32), shape((count, *stream.shape), f32)]
    return pl.pallas_call(
        total_kernel,
        grid=(1,),
        in_specs=[whole_spec(v) for v in (cols, stream, *parts)],
        out_specs=[whole_spec(v) for v in outs],
        out_shape=outs,
        compiler_params=params(),
        cost_estimate=HINT,
        name="branch_total",
    )(cols, stream, *parts)


def head_kernel(order, got, gain, words, softness, logits, message, wide):
    blocks, block = gain.shape
    rows, columns = logits.shape
    ends, squares = [], 0.0
    for b in range(blocks):
        v = jnp.concatenate([got[i] for i in order[b]], axis=0)
        squares = squares + jnp.sum(v * v, axis=1, keepdims=True)
        ends.append(v)
    scale = lax.rsqrt(squares / WIDTH + epsilon)
    total = jnp.zeros((rows, columns), f32)
    for b in range(blocks):
        feed = (ends[b] * scale * gain[b : b + 1]).astype(bf16)
        total += jnp.dot(feed, words[b * block : (b + 1) * block], preferred_element_type=f32)
    total = total / (WIDTH / 256.0 * softness[...])
    logits[...] = total
    top = jnp.max(total, axis=1, keepdims=True)
    mass = jnp.sum(jnp.exp(total - top), axis=1, keepdims=True)
    wide[...] = jnp.zeros_like(wide)
    lane = lax.broadcasted_iota(jnp.int32, (rows, LANES), 1)
    wide[0:rows] = jnp.where(lane == 0, top, jnp.where(lane == 1, mass, 0.0))
    turned = wide[...].T
    message[...] = jnp.broadcast_to(turned[None, 0:2, 0:rows], message.shape)


def head_call(order, got, gain, words, softness):
    rows, columns = softness.shape[0], words.shape[1]
    return pl.pallas_call(
        lambda *refs: head_kernel(order, *refs),
        in_specs=[VMEM] * 4,
        out_specs=[VMEM, VMEM],
        out_shape=[shape((rows, columns), f32), shape((got.shape[0], 2, rows), f32)],
        scratch_shapes=[pltpu.VMEM((LANES, LANES), f32)],
        compiler_params=params(),
        cost_estimate=HINT,
        name="head",
    )(got, gain, words, softness)


def body(
    skip_stream_arriving,
    chosen_specialists,
    sequence_piece_tallies,
    premix_rmsnorm_gain,
    dispatcher_weights,
    specialist_switch_weights,
    specialist_expand_weights,
    specialist_contract_weights,
    terminal_rmsnorm_gain,
    lexicon_projector_weights,
    softness_per_sequence,
):
    tokens, block = skip_stream_arriving.shape
    dp, mp = lax.axis_size("dp"), lax.axis_size("mp")
    count = dp * mp
    parts = 4
    spread, sides = dp // parts, mp // parts
    assert dp == parts * spread and mp == parts * sides and sides & (sides - 1) == 0
    part = lax.axis_index("dp") // spread
    y, core = part // 2, part % 2
    side, z = lax.axis_index("mp") % sides, lax.axis_index("mp") // sides

    def send(value, to):
        pairs = []
        for q in range(parts):
            for r in range(spread):
                for z in range(parts):
                    for x in range(sides):
                        q2, z2, x2 = to(q, z, x)
                        source = (q * spread + r) * mp + z * sides + x
                        pairs.append((source, (q2 * spread + r) * mp + z2 * sides + x2))
        return lax.ppermute(value, ("dp", "mp"), pairs)

    other_core = lambda q, z, x: (q ^ 1, z, x)
    home = lambda q, z, x: (z, q, x)

    scal = jnp.stack([core, side, y] + [(z + s) % parts for s in range(parts)]).astype(jnp.int32)
    sent, stream = prep_call(
        skip_stream_arriving.T, premix_rmsnorm_gain[None], chosen_specialists.T, sequence_piece_tallies
    )
    wg, wu, wd = specialist_switch_weights, specialist_expand_weights, specialist_contract_weights
    if spread > 1:
        runs = [[q * spread + r for r in range(spread)] for q in range(parts)]
        wg = lax.all_gather(wg, "dp", axis=1, tiled=True, axis_index_groups=runs)
        wu = lax.all_gather(wu, "dp", axis=1, tiled=True, axis_index_groups=runs)
        wd = lax.all_gather(wd, "dp", axis=2, tiled=True, axis_index_groups=runs)
    wd = jnp.swapaxes(wd, 1, 2)
    depth, hidden = wg.shape[1:]
    base = hidden % LANES
    wr = lax.dynamic_slice_in_dim(dispatcher_weights.T, part * depth, depth, axis=1)
    room = lambda at: jnp.pad(wr, ((at, LANES - at - wr.shape[0]), (0, 0)))
    wr = room(base + 1) + room(base + 1 + EXTRA)

    chunks = ((1,), (2,), (3,), (0,))
    first = [send(sent, lambda q, z, x, i=i: (z, (q - 1) % parts, x ^ i)) for i in range(sides)]
    pair = join_call(first)
    along_z = [[n * sides + x for n in range(parts)] for x in range(sides)]
    along_y = [[(q + n) * spread + r for n in (0, 2)] for q in range(2) for r in range(spread)]
    pairs = lax.all_gather(pair, "mp", axis_index_groups=along_z)
    feeds = {1: (pair, None), 2: (send(pair, lambda q, z, x: (q, (z - 1) % parts, x)), None)}
    feeds |= {3: (pairs, 3 + 2), 0: (pairs, 3 + 3)}
    stream = send(stream, home)
    partial, kept, pieces, shares = {}, {}, {}, {}

    def do_partial(s, *deps):
        own, give, cols = partial_call(scal, sides, [feeds[g] for g in chunks[s]], wr, wg, wu, deps)
        partial[s] = (own, send(give, other_core), cols)
        return own

    def do_sum(s, *deps):
        own, recv, _ = partial[s]
        keep, give = sum_call(scal, base, own, recv, deps)
        kept[s] = (keep, lax.all_gather(give, "dp", axis_index_groups=along_y))
        return keep

    def do_act(s, *deps):
        a = act_call(scal, base, *kept[s], partial[s][2], deps)
        both = lax.all_gather(a, "dp", axis_index_groups=along_y, tiled=True)
        pieces[s] = (both, send(both, other_core))
        return a

    def do_down(s, *deps):
        outs = down_call(scal, sides, pieces[s], partial[s][2], wd, deps)
        got = [outs[0]] + [send(outs[i], lambda q, z, x, i=i: (q, z, x ^ i)) for i in range(1, sides)]
        for n, group in enumerate(chunks[s]):
            to = slice(n * tokens, (n + 1) * tokens)
            if group == 0:
                shares[0] = [v[:, to] for v in got]
            else:
                share = sum(v[:, to].astype(f32) for v in got).astype(bf16)
                back = lambda q, z, x, group=group: (q, (z + group) % parts, x)
                shares[group] = [send(share, back)]
        return outs[0]

    p0 = do_partial(0)
    p1 = do_partial(1, p0)
    s0 = do_sum(0, p1)
    s1 = do_sum(1, s0)
    p2 = do_partial(2, s1)
    a0 = do_act(0, p2)
    p3 = do_partial(3, a0)
    s2 = do_sum(2, p3)
    a1 = do_act(1, s2)
    s3 = do_sum(3, a1)
    d0 = do_down(0, s3)
    a2 = do_act(2, d0)
    d1 = do_down(1, a2)
    a3 = do_act(3, d1)
    d2 = do_down(2, a3)
    do_down(3, d2)
    mine = [v for group in range(parts) for v in shares[group]]
    total, message = total_call(partial[parts - 1][2], stream, mine, block, count)

    everyone = lambda v: lax.all_to_all(v, ("dp", "mp"), 0, 0, tiled=True)
    got = everyone(message)
    branch = send(total, home)
    order = [
        [
            (q * spread + r) * mp + z * sides + x
            for z in range(parts)
            for r in range(spread)
        ]
        for q in range(parts)
        for x in range(sides)
    ]
    logits, pairs = head_call(
        order,
        got,
        terminal_rmsnorm_gain.reshape(mp, block),
        lexicon_projector_weights,
        softness_per_sequence[:, None],
    )
    pairs = everyone(pairs)
    new_hidden = skip_stream_arriving + branch_scale * branch.T
    largest = jnp.max(pairs[:, 0], axis=0)
    mass = jnp.sum(pairs[:, 1] * jnp.exp(pairs[:, 0] - largest), axis=0)
    logprobs = logits - largest[:, None] - jnp.log(mass)[:, None]
    return (new_hidden, logprobs)


def solution(mesh):
    return jax.shard_map(
        body,
        mesh=mesh,
        in_specs=(
            P("dp", "mp"),
            P("dp", None),
            P("dp", None),
            P("mp"),
            P(),
            P(None, "dp", "mp"),
            P(None, "dp", "mp"),
            P(None, "mp", "dp"),
            P(),
            P(None, ("dp", "mp")),
            P(),
        ),
        out_specs=(P("dp", "mp"), P(None, ("dp", "mp"))),
        check_vma=False,
    )
```

```python
import math

import jax
import jax.numpy as jnp
from jax import lax
from jax.experimental import pallas as pl
from jax.experimental.pallas import tpu as pltpu
from jax.sharding import PartitionSpec as P

WIDTH = 2304
META = 16
LANES = 128
branch_scale = 1.4 / math.sqrt(40.0)
epsilon = 1e-05
f32, bf16 = jnp.float32, jnp.bfloat16

VMEM = pl.BlockSpec(memory_space=pltpu.VMEM)
SMEM = pl.BlockSpec(memory_space=pltpu.SMEM)
ANY = pl.BlockSpec(memory_space=pl.ANY)


def up_to(n, step=LANES):
    return -(-n // step) * step


def params(mib=16):
    return pltpu.CompilerParams(vmem_limit_bytes=mib * 2**20)


HINT = pl.CostEstimate(flops=1, bytes_accessed=1024, transcendentals=0)


def shape(dims, dtype):
    return jax.ShapeDtypeStruct(dims, dtype)


def prep_kernel(tallies, x, gain, routes, out, ends):
    block, tokens = x.shape
    v = x[...]
    wide = up_to(block)
    g = jnp.concatenate([gain[...], jnp.zeros((1, wide - block), f32)], axis=1)
    g = jnp.broadcast_to(g, (LANES, wide)).T[0:block, 0:1]
    out[0:block] = (v * g).astype(bf16)
    sq = jnp.sum(v * v, axis=0, keepdims=True)
    hi = sq.astype(bf16).astype(f32)
    mid = (sq - hi).astype(bf16).astype(f32)
    here = lax.broadcasted_iota(jnp.int32, (1, tokens), 1)
    mark, end = jnp.zeros((1, tokens), f32), jnp.int32(-1)
    for q in range(ends.shape[0]):
        end = end + tallies[0, q]
        mark = jnp.where(here == end, q + 1.0, mark)
    rows = [routes[...].astype(f32), hi, mid, sq - hi - mid, mark]
    rows.append(jnp.zeros((META - 6, tokens), f32))
    out[block:] = jnp.concatenate(rows, axis=0).astype(bf16)
    ends[...] = columns_at(mark, v)[0 : ends.shape[0]]


def columns_at(mark, v):
    row = lax.broadcasted_iota(jnp.int32, (8, mark.shape[1]), 0)
    pick = jnp.where(mark == (row + 1).astype(f32), 1.0, 0.0)
    return lax.dot_general(
        pick, v, (((1,), (1,)), ((), ())), precision=lax.Precision.HIGHEST, preferred_element_type=f32
    )


def whole_spec(v):
    return pl.BlockSpec(v.shape, lambda *_: (0,) * len(v.shape))


def prep_call(x, gain, routes, tallies):
    block, tokens = x.shape
    reqs = tallies.shape[1]
    outs = [shape((block + META, tokens), bf16), shape((reqs, block), f32)]
    return pl.pallas_call(
        prep_kernel,
        grid=(1,),
        in_specs=[SMEM] + [whole_spec(v) for v in (x, gain, routes)],
        out_specs=[whole_spec(v) for v in outs],
        out_shape=outs,
        compiler_params=params(),
        cost_estimate=HINT,
        name="prep",
    )(tallies, x, gain, routes)


def join_call(blocks):
    rows, tokens = blocks[0].shape

    def join_kernel(*refs):
        for i, ref in enumerate(refs[:-1]):
            refs[-1][i * rows : (i + 1) * rows] = ref[...]

    return pl.pallas_call(
        join_kernel,
        in_specs=[VMEM] * len(blocks),
        out_specs=VMEM,
        out_shape=shape((len(blocks) * rows, tokens), bf16),
        compiler_params=params(),
        cost_estimate=HINT,
        name="join",
    )(*blocks)


EXTRA = 5


def spread_lanes(v, base):
    lane = lax.broadcasted_iota(jnp.int32, v.shape, 1)
    hi = v.astype(bf16).astype(f32)
    return jnp.where(lane < base, v, jnp.where(lane < base + EXTRA, hi, v - hi)).astype(bf16)


def joined_lanes(v, base):
    lane = lax.broadcasted_iota(jnp.int32, v.shape, 1)
    left, right = pltpu.roll(v, LANES - EXTRA, 1), pltpu.roll(v, EXTRA, 1)
    return v + jnp.where(lane < base, 0.0, jnp.where(lane < base + EXTRA, left, right))


def slot_columns(core, cols):
    first, second = cols[:, 0:1].astype(f32), cols[:, 1:2].astype(f32)
    zero = core == 0
    return jnp.where(zero, first, second), jnp.where(zero, second, first)


def partial_kernel(sides, held, scal, *refs):
    feeds, (wr, wg, wu) = refs[:held], refs[held : held + 3]
    own, give, cols, xs, xt, acc, extra = refs[-7:]
    e = pl.program_id(0)
    core, side = scal[0], scal[1]
    depth, hidden = wg.shape[1:]
    deep, half = up_to(depth), up_to(hidden)
    base = hidden % LANES
    tokens = feeds[0].shape[1]
    block = depth // sides
    last = slice(2 * half - LANES, 2 * half)

    @pl.when(e == 0)
    def _():
        xs[depth:] = jnp.zeros((deep + LANES - depth, xs.shape[1]), bf16)
        for n, ref in enumerate(feeds):
            to = slice(n * tokens, (n + 1) * tokens)
            for i in range(sides):
                at = i * (block + META)
                xs[pl.ds(pl.multiple_of((side ^ i) * block, 16), block), to] = ref[at : at + block]
                xs[deep + i * META : deep + (i + 1) * META, to] = ref[at + block : at + block + META]
        xt[...] = xs[...].T
        more = xt[:, deep:]
        cols[...] = more
        more = more.astype(f32)
        sq = jnp.zeros((more.shape[0], 1), f32)
        for i in range(sides):
            for term in (4, 3, 2):
                sq = sq + more[:, i * META + term : i * META + term + 1]
        router = lax.dot_general(
            xt[:, 0:depth], wr[...], (((1,), (1,)), ((), ())), preferred_element_type=f32
        )
        lane = lax.broadcasted_iota(jnp.int32, router.shape, 1)
        extra[...] = router + jnp.where((lane == base) | (lane == base + EXTRA), sq, 0.0)
        for ref in (own, acc):
            ref[:, half - LANES : half] = jnp.zeros((xt.shape[0], LANES), f32)
            ref[:, last] = jnp.zeros((xt.shape[0], LANES), f32)

    mine, other = slot_columns(core, xt[:, deep : deep + LANES])
    ef = e.astype(f32)
    take = [(v == ef) | (e == 0) for v in (mine, other)]
    for which, w in enumerate((wg, wu)):
        for at in range(0, hidden, 256):
            end = min(hidden, at + 256)
            d = jnp.dot(xt[:, 0:depth], w[0, :, at:end], preferred_element_type=f32)
            to = slice(which * half + at, which * half + end)
            for ref, pick in ((own, take[0]), (acc, take[1])):
                ref[:, to] = jnp.where(pick, d, ref[:, to])

    @pl.when(e == pl.num_programs(0) - 1)
    def _():
        lane = lax.broadcasted_iota(jnp.int32, extra.shape, 1)
        more = extra[...]
        own[:, last] = jnp.where(lane < base, own[:, last], more)
        give[:, 0 : last.start] = acc[:, 0 : last.start].astype(bf16)
        give[:, last] = spread_lanes(jnp.where(lane < base, acc[:, last], more), base)


def partial_call(scal, sides, feeds, wr, wg, wu, deps):
    experts, depth, hidden = wg.shape
    tokens = feeds[0].shape[1] * len(feeds)
    deep, wide = up_to(depth), 2 * up_to(hidden)
    part = pl.BlockSpec((1, depth, hidden), lambda n: (n, 0, 0))
    outs = [shape((tokens, wide), f32), shape((tokens, wide), bf16), shape((tokens, LANES), bf16)]
    return pl.pallas_call(
        lambda *refs: partial_kernel(sides, len(feeds), *refs),
        grid=(experts,),
        in_specs=[SMEM] + [whole_spec(v) for v in feeds] + [whole_spec(wr), part, part] + [ANY] * len(deps),
        out_specs=[whole_spec(v) for v in outs],
        out_shape=outs,
        scratch_shapes=[
            pltpu.VMEM((deep + LANES, tokens), bf16),
            pltpu.VMEM((tokens, deep + LANES), bf16),
            pltpu.VMEM((tokens, wide), f32),
            pltpu.VMEM((tokens, LANES), f32),
        ],
        compiler_params=params(20),
        cost_estimate=HINT,
        name="gate_up_partial",
    )(scal, *feeds, wr, wg, wu, *deps)


def sum_kernel(base, scal, own, recv, *refs):
    keep, send = refs[-2:]
    y = scal[2]
    th, wide = keep.shape
    main = wide - LANES
    for to, first in ((keep, y), (send, 1 - y)):
        rows = pl.ds(pl.multiple_of(first * th, th), th)
        to[:, 0:main] = (own[rows, 0:main] + recv[rows, 0:main].astype(f32)).astype(to.dtype)
        v = own[rows, main:] + joined_lanes(recv[rows, main:].astype(f32), base)
        to[:, main:] = v if to is keep else spread_lanes(v, base)


def sum_call(scal, base, own, recv, deps):
    tokens, wide = own.shape
    return pl.pallas_call(
        lambda *refs: sum_kernel(base, *refs),
        in_specs=[SMEM, VMEM, VMEM] + [ANY] * len(deps),
        out_specs=[VMEM, VMEM],
        out_shape=[shape((tokens // 2, wide), f32), shape((tokens // 2, wide), bf16)],
        compiler_params=params(),
        cost_estimate=HINT,
        name="core_sum",
    )(scal, own, recv, *deps)


def act_kernel(base, scal, keep, recv, cols, *refs):
    act = refs[-1]
    core, y = scal[0], scal[2]
    th, half = act.shape
    main = 2 * half - LANES
    m = keep[:, main:] + joined_lanes(recv[:, main:].astype(f32), base)
    mine, other = slot_columns(core, cols[pl.ds(pl.multiple_of(y * th, th), th)])
    scale = lax.rsqrt(m[:, base : base + 1] / WIDTH + epsilon)
    la = lb = jnp.zeros_like(scale)
    for e in range(4):
        logit = m[:, base + 1 + e : base + 2 + e] * scale
        la = jnp.where(mine == e, logit, la)
        lb = jnp.where(other == e, logit, lb)
    mix = scale / (1.0 + jnp.exp(lb - la))
    g = (keep[:, 0:half] + recv[:, 0:half].astype(f32)) * scale
    u = (keep[:, half:] + recv[:, half:].astype(f32)) * mix
    act[...] = (g / (1.0 + jnp.exp(-g)) * u).astype(bf16)


def act_call(scal, base, keep, recv, cols, deps):
    th, wide = keep.shape
    return pl.pallas_call(
        lambda *refs: act_kernel(base, *refs),
        in_specs=[SMEM] + [VMEM] * 3 + [ANY] * len(deps),
        out_specs=VMEM,
        out_shape=shape((th, wide // 2), bf16),
        compiler_params=params(),
        cost_estimate=HINT,
        name="act",
    )(scal, keep, recv, cols, *deps)


def down_kernel(sides, scal, a, a_y, b, b_y, cols, wd, *refs):
    outs = refs[-sides - 2 : -2]
    whole, acc = refs[-2:]
    e = pl.program_id(0)
    core, side, y = scal[0], scal[1], scal[2]
    th = a.shape[0]
    width, hidden = wd.shape[1:]
    block = width // sides

    @pl.when(e == 0)
    def _():
        for k, near, far in ((0, a, a_y), (1, b, b_y)):
            whole[k, pl.ds(pl.multiple_of(y * th, th), th)] = near[...]
            whole[k, pl.ds(pl.multiple_of((1 - y) * th, th), th)] = far[...]

    ef = e.astype(f32)
    masks = [jnp.where(v == ef, 1.0, 0.0).astype(bf16) for v in slot_columns(core, cols[...])]
    rows = whole[0, :, 0:hidden] * masks[0] + whole[1, :, 0:hidden] * masks[1]
    d = lax.dot_general(wd[0], rows, (((1,), (1,)), ((), ())), preferred_element_type=f32)

    @pl.when(e == 0)
    def _():
        acc[...] = d

    @pl.when(e > 0)
    def _():
        acc[...] += d

    @pl.when(e == pl.num_programs(0) - 1)
    def _():
        for i in range(sides):
            rows = pl.ds(pl.multiple_of((side ^ i) * block, 16), block)
            outs[i][...] = acc[rows].astype(bf16)


def down_call(scal, sides, pieces, cols, wd, deps):
    experts, width, hidden = wd.shape
    tokens = cols.shape[0]
    outs = [shape((width // sides, tokens), bf16)] * sides
    return pl.pallas_call(
        lambda *refs: down_kernel(sides, *refs),
        grid=(experts,),
        in_specs=[SMEM]
        + [whole_spec(v) for v in pieces]
        + [whole_spec(cols), pl.BlockSpec((1, width, hidden), lambda n: (n, 0, 0))]
        + [ANY] * len(deps),
        out_specs=[whole_spec(v) for v in outs],
        out_shape=outs,
        scratch_shapes=[
            pltpu.VMEM((2, tokens, pieces[0].shape[1]), bf16),
            pltpu.VMEM((width, tokens), f32),
        ],
        compiler_params=params(20),
        cost_estimate=HINT,
        name="down",
    )(scal, *pieces, cols, wd, *deps)


def total_kernel(meta, stream, *refs):
    parts, (total, message) = refs[:-2], refs[-2:]
    v = parts[0][...].astype(f32)
    for ref in parts[1:]:
        v = v + ref[...].astype(f32)
    total[...] = v
    reqs = stream.shape[0]
    ends = columns_at(meta[5:6].astype(f32), v)
    ends = stream[...] + branch_scale * ends[0:reqs]
    message[...] = jnp.broadcast_to(ends[None], message.shape)


def total_call(feed, stream, parts, block, count):
    tokens = feed.shape[1]
    full = lambda v: pl.BlockSpec(v.shape, lambda n: (0,) * len(v.shape))
    outs = [shape((block, tokens), f32), shape((count, *stream.shape), f32)]
    return pl.pallas_call(
        total_kernel,
        grid=(1,),
        in_specs=[pl.BlockSpec((META, tokens), lambda n: (block // META, 0)), full(stream)]
        + [full(v) for v in parts],
        out_specs=[full(v) for v in outs],
        out_shape=outs,
        compiler_params=params(),
        cost_estimate=HINT,
        name="branch_total",
    )(feed, stream, *parts)


def head_kernel(order, got, gain, words, softness, logits, message, wide):
    blocks, block = gain.shape
    rows, columns = logits.shape
    ends, squares = [], 0.0
    for b in range(blocks):
        v = jnp.concatenate([got[i] for i in order[b]], axis=0)
        squares = squares + jnp.sum(v * v, axis=1, keepdims=True)
        ends.append(v)
    scale = lax.rsqrt(squares / WIDTH + epsilon)
    total = jnp.zeros((rows, columns), f32)
    for b in range(blocks):
        feed = (ends[b] * scale * gain[b : b + 1]).astype(bf16)
        total += jnp.dot(feed, words[b * block : (b + 1) * block], preferred_element_type=f32)
    total = total / (WIDTH / 256.0 * softness[...])
    logits[...] = total
    top = jnp.max(total, axis=1, keepdims=True)
    mass = jnp.sum(jnp.exp(total - top), axis=1, keepdims=True)
    wide[...] = jnp.zeros_like(wide)
    lane = lax.broadcasted_iota(jnp.int32, (rows, LANES), 1)
    wide[0:rows] = jnp.where(lane == 0, top, jnp.where(lane == 1, mass, 0.0))
    turned = wide[...].T
    message[...] = jnp.broadcast_to(turned[None, 0:2, 0:rows], message.shape)


def head_call(order, got, gain, words, softness):
    rows, columns = softness.shape[0], words.shape[1]
    return pl.pallas_call(
        lambda *refs: head_kernel(order, *refs),
        in_specs=[VMEM] * 4,
        out_specs=[VMEM, VMEM],
        out_shape=[shape((rows, columns), f32), shape((got.shape[0], 2, rows), f32)],
        scratch_shapes=[pltpu.VMEM((LANES, LANES), f32)],
        compiler_params=params(),
        cost_estimate=HINT,
        name="head",
    )(got, gain, words, softness)


def body(
    skip_stream_arriving,
    chosen_specialists,
    sequence_piece_tallies,
    premix_rmsnorm_gain,
    dispatcher_weights,
    specialist_switch_weights,
    specialist_expand_weights,
    specialist_contract_weights,
    terminal_rmsnorm_gain,
    lexicon_projector_weights,
    softness_per_sequence,
):
    tokens, block = skip_stream_arriving.shape
    dp, mp = lax.axis_size("dp"), lax.axis_size("mp")
    count = dp * mp
    parts = 4
    spread, sides = dp // parts, mp // parts
    assert dp == parts * spread and mp == parts * sides and sides & (sides - 1) == 0
    part = lax.axis_index("dp") // spread
    y, core = part // 2, part % 2
    side = lax.axis_index("mp") % sides

    def send(value, to):
        pairs = []
        for q in range(parts):
            for r in range(spread):
                for z in range(parts):
                    for x in range(sides):
                        q2, z2, x2 = to(q, z, x)
                        source = (q * spread + r) * mp + z * sides + x
                        pairs.append((source, (q2 * spread + r) * mp + z2 * sides + x2))
        return lax.ppermute(value, ("dp", "mp"), pairs)

    other_core = lambda q, z, x: (q ^ 1, z, x)
    other_y = lambda q, z, x: (q ^ 2, z, x)
    home = lambda q, z, x: (z, q, x)

    scal = jnp.stack([core, side, y]).astype(jnp.int32)
    sent, stream = prep_call(
        skip_stream_arriving.T, premix_rmsnorm_gain[None], chosen_specialists.T, sequence_piece_tallies
    )
    wg, wu, wd = specialist_switch_weights, specialist_expand_weights, specialist_contract_weights
    if spread > 1:
        runs = [[q * spread + r for r in range(spread)] for q in range(parts)]
        wg = lax.all_gather(wg, "dp", axis=1, tiled=True, axis_index_groups=runs)
        wu = lax.all_gather(wu, "dp", axis=1, tiled=True, axis_index_groups=runs)
        wd = lax.all_gather(wd, "dp", axis=2, tiled=True, axis_index_groups=runs)
    wd = jnp.swapaxes(wd, 1, 2)
    depth, hidden = wg.shape[1:]
    base = hidden % LANES
    wr = lax.dynamic_slice_in_dim(dispatcher_weights.T, part * depth, depth, axis=1)
    room = lambda at: jnp.pad(wr, ((at, LANES - at - wr.shape[0]), (0, 0)))
    wr = room(base + 1) + room(base + 1 + EXTRA)

    chunks = ((1,), (2,), (3,), (0,))
    first = [send(sent, lambda q, z, x, i=i: (z, (q - 1) % parts, x ^ i)) for i in range(sides)]
    pair = join_call(first)
    feeds = {1: pair}
    for group in (2, 3, 0):
        feeds[group] = send(pair, lambda q, z, x, group=group: (q, (z - group + 1) % parts, x))
    stream = send(stream, home)
    partial, kept, pieces, shares = {}, {}, {}, {}

    def do_partial(s, *deps):
        own, give, cols = partial_call(scal, sides, [feeds[g] for g in chunks[s]], wr, wg, wu, deps)
        partial[s] = (own, send(give, other_core), cols)
        return own

    def do_sum(s, *deps):
        own, recv, _ = partial[s]
        keep, give = sum_call(scal, base, own, recv, deps)
        kept[s] = (keep, send(give, other_y))
        return keep

    def do_act(s, *deps):
        a = act_call(scal, base, *kept[s], partial[s][2], deps)
        a_y = send(a, other_y)
        pieces[s] = (a, a_y, send(a, other_core), send(a_y, other_core))
        return a

    def do_down(s, *deps):
        outs = down_call(scal, sides, pieces[s], partial[s][2], wd, deps)
        got = [outs[0]] + [send(outs[i], lambda q, z, x, i=i: (q, z, x ^ i)) for i in range(1, sides)]
        for n, group in enumerate(chunks[s]):
            to = slice(n * tokens, (n + 1) * tokens)
            if group == 0:
                shares[0] = [v[:, to] for v in got]
            else:
                share = sum(v[:, to].astype(f32) for v in got).astype(bf16)
                back = lambda q, z, x, group=group: (q, (z + group) % parts, x)
                shares[group] = [send(share, back)]
        return outs[0]

    p0 = do_partial(0)
    p1 = do_partial(1, p0)
    s0 = do_sum(0, p1)
    s1 = do_sum(1, s0)
    p2 = do_partial(2, s1)
    a0 = do_act(0, p2)
    p3 = do_partial(3, a0)
    a1 = do_act(1, p3)
    s2 = do_sum(2, a1)
    s3 = do_sum(3, s2)
    d0 = do_down(0, s3)
    a2 = do_act(2, d0)
    d1 = do_down(1, a2)
    a3 = do_act(3, d1)
    d2 = do_down(2, a3)
    do_down(3, d2)
    mine = [v for group in range(parts) for v in shares[group]]
    total, message = total_call(feeds[0], stream, mine, block, count)

    everyone = lambda v: lax.all_to_all(v, ("dp", "mp"), 0, 0, tiled=True)
    got = everyone(message)
    branch = send(total, home)
    order = [
        [
            (q * spread + r) * mp + z * sides + x
            for z in range(parts)
            for r in range(spread)
        ]
        for q in range(parts)
        for x in range(sides)
    ]
    logits, pairs = head_call(
        order,
        got,
        terminal_rmsnorm_gain.reshape(mp, block),
        lexicon_projector_weights,
        softness_per_sequence[:, None],
    )
    pairs = everyone(pairs)
    new_hidden = skip_stream_arriving + branch_scale * branch.T
    largest = jnp.max(pairs[:, 0], axis=0)
    mass = jnp.sum(pairs[:, 1] * jnp.exp(pairs[:, 0] - largest), axis=0)
    logprobs = logits - largest[:, None] - jnp.log(mass)[:, None]
    return (new_hidden, logprobs)


def solution(mesh):
    return jax.shard_map(
        body,
        mesh=mesh,
        in_specs=(
            P("dp", "mp"),
            P("dp", None),
            P("dp", None),
            P("mp"),
            P(),
            P(None, "dp", "mp"),
            P(None, "dp", "mp"),
            P(None, "mp", "dp"),
            P(),
            P(None, ("dp", "mp")),
            P(),
        ),
        out_specs=(P("dp", "mp"), P(None, ("dp", "mp"))),
        check_vma=False,
    )
```

```python
import math

import jax
import jax.numpy as jnp
from jax import lax
from jax.experimental import pallas as pl
from jax.experimental.pallas import tpu as pltpu
from jax.sharding import PartitionSpec as P

WIDTH = 2304
META = 16
LANES = 128
branch_scale = 1.4 / math.sqrt(40.0)
epsilon = 1e-05
f32, bf16 = jnp.float32, jnp.bfloat16

VMEM = pl.BlockSpec(memory_space=pltpu.VMEM)
SMEM = pl.BlockSpec(memory_space=pltpu.SMEM)
ANY = pl.BlockSpec(memory_space=pl.ANY)


def up_to(n, step=LANES):
    return -(-n // step) * step


def params(mib=16):
    return pltpu.CompilerParams(vmem_limit_bytes=mib * 2**20)


def hint(flops, bytes_accessed, scale=0.3):
    return pl.CostEstimate(flops=int(flops * scale), bytes_accessed=int(bytes_accessed * scale), transcendentals=0)


def shape(dims, dtype):
    return jax.ShapeDtypeStruct(dims, dtype)


def prep_kernel(tallies, x, gain, routes, out, ends):
    block, tokens = x.shape
    v = x[...]
    wide = up_to(block)
    g = jnp.concatenate([gain[...], jnp.zeros((1, wide - block), f32)], axis=1)
    g = jnp.broadcast_to(g, (LANES, wide)).T[0:block, 0:1]
    out[0:block] = (v * g).astype(bf16)
    sq = jnp.sum(v * v, axis=0, keepdims=True)
    hi = sq.astype(bf16).astype(f32)
    mid = (sq - hi).astype(bf16).astype(f32)
    here = lax.broadcasted_iota(jnp.int32, (1, tokens), 1)
    mark, end = jnp.zeros((1, tokens), f32), jnp.int32(-1)
    for q in range(ends.shape[0]):
        end = end + tallies[0, q]
        mark = jnp.where(here == end, q + 1.0, mark)
    rows = [routes[...].astype(f32), hi, mid, sq - hi - mid, mark]
    rows.append(jnp.zeros((META - 6, tokens), f32))
    out[block:] = jnp.concatenate(rows, axis=0).astype(bf16)
    ends[...] = columns_at(mark, v)[0 : ends.shape[0]]


def columns_at(mark, v):
    row = lax.broadcasted_iota(jnp.int32, (8, mark.shape[1]), 0)
    pick = jnp.where(mark == (row + 1).astype(f32), 1.0, 0.0)
    return lax.dot_general(
        pick, v, (((1,), (1,)), ((), ())), precision=lax.Precision.HIGHEST, preferred_element_type=f32
    )


def whole_spec(v):
    return pl.BlockSpec(v.shape, lambda *_: (0,) * len(v.shape))


def prep_call(x, gain, routes, tallies):
    block, tokens = x.shape
    reqs = tallies.shape[1]
    outs = [shape((block + META, tokens), bf16), shape((reqs, block), f32)]
    return pl.pallas_call(
        prep_kernel,
        grid=(1,),
        in_specs=[SMEM] + [whole_spec(v) for v in (x, gain, routes)],
        out_specs=[whole_spec(v) for v in outs],
        out_shape=outs,
        compiler_params=params(),
        cost_estimate=hint(4 * tokens * block, 6 * tokens * block),
        name="prep",
    )(tallies, x, gain, routes)


def join_call(blocks):
    rows, tokens = blocks[0].shape

    def join_kernel(*refs):
        for i, ref in enumerate(refs[:-1]):
            refs[-1][i * rows : (i + 1) * rows] = ref[...]

    return pl.pallas_call(
        join_kernel,
        in_specs=[VMEM] * len(blocks),
        out_specs=VMEM,
        out_shape=shape((len(blocks) * rows, tokens), bf16),
        compiler_params=params(),
        cost_estimate=hint(1, 4 * len(blocks) * rows * tokens),
        name="join",
    )(*blocks)


EXTRA = 5


def spread_lanes(v, base):
    lane = lax.broadcasted_iota(jnp.int32, v.shape, 1)
    hi = v.astype(bf16).astype(f32)
    return jnp.where(lane < base, v, jnp.where(lane < base + EXTRA, hi, v - hi)).astype(bf16)


def joined_lanes(v, base):
    lane = lax.broadcasted_iota(jnp.int32, v.shape, 1)
    left, right = pltpu.roll(v, LANES - EXTRA, 1), pltpu.roll(v, EXTRA, 1)
    return v + jnp.where(lane < base, 0.0, jnp.where(lane < base + EXTRA, left, right))


def slot_columns(core, cols):
    first, second = cols[:, 0:1].astype(f32), cols[:, 1:2].astype(f32)
    zero = core == 0
    return jnp.where(zero, first, second), jnp.where(zero, second, first)


def partial_kernel(sides, held, scal, *refs):
    feeds, (wr, wg, wu) = refs[:held], refs[held : held + 3]
    own, give, cols, xs, xt, acc, extra = refs[-7:]
    e = pl.program_id(0)
    core, side = scal[0], scal[1]
    depth, hidden = wg.shape[1:]
    deep, half = up_to(depth), up_to(hidden)
    base = hidden % LANES
    tokens = feeds[0].shape[1]
    block = depth // sides
    last = slice(2 * half - LANES, 2 * half)

    @pl.when(e == 0)
    def _():
        xs[depth:] = jnp.zeros((deep + LANES - depth, xs.shape[1]), bf16)
        for n, ref in enumerate(feeds):
            to = slice(n * tokens, (n + 1) * tokens)
            for i in range(sides):
                at = i * (block + META)
                xs[pl.ds(pl.multiple_of((side ^ i) * block, 16), block), to] = ref[at : at + block]
                xs[deep + i * META : deep + (i + 1) * META, to] = ref[at + block : at + block + META]
        xt[...] = xs[...].T
        more = xt[:, deep:]
        cols[...] = more
        more = more.astype(f32)
        sq = jnp.zeros((more.shape[0], 1), f32)
        for i in range(sides):
            for term in (4, 3, 2):
                sq = sq + more[:, i * META + term : i * META + term + 1]
        router = lax.dot_general(
            xt[:, 0:depth], wr[...], (((1,), (1,)), ((), ())), preferred_element_type=f32
        )
        lane = lax.broadcasted_iota(jnp.int32, router.shape, 1)
        extra[...] = router + jnp.where((lane == base) | (lane == base + EXTRA), sq, 0.0)
        for ref in (own, acc):
            ref[:, half - LANES : half] = jnp.zeros((xt.shape[0], LANES), f32)
            ref[:, last] = jnp.zeros((xt.shape[0], LANES), f32)

    mine, other = slot_columns(core, xt[:, deep : deep + LANES])
    ef = e.astype(f32)
    take = [(v == ef) | (e == 0) for v in (mine, other)]
    for which, w in enumerate((wg, wu)):
        for at in range(0, hidden, 256):
            end = min(hidden, at + 256)
            d = jnp.dot(xt[:, 0:depth], w[0, :, at:end], preferred_element_type=f32)
            to = slice(which * half + at, which * half + end)
            for ref, pick in ((own, take[0]), (acc, take[1])):
                ref[:, to] = jnp.where(pick, d, ref[:, to])

    @pl.when(e == pl.num_programs(0) - 1)
    def _():
        lane = lax.broadcasted_iota(jnp.int32, extra.shape, 1)
        more = extra[...]
        own[:, last] = jnp.where(lane < base, own[:, last], more)
        give[:, 0 : last.start] = acc[:, 0 : last.start].astype(bf16)
        give[:, last] = spread_lanes(jnp.where(lane < base, acc[:, last], more), base)


def partial_call(scal, sides, feeds, wr, wg, wu, deps):
    experts, depth, hidden = wg.shape
    tokens = feeds[0].shape[1] * len(feeds)
    deep, wide = up_to(depth), 2 * up_to(hidden)
    part = pl.BlockSpec((1, depth, hidden), lambda n: (n, 0, 0))
    outs = [shape((tokens, wide), f32), shape((tokens, wide), bf16), shape((tokens, LANES), bf16)]
    return pl.pallas_call(
        lambda *refs: partial_kernel(sides, len(feeds), *refs),
        grid=(experts,),
        in_specs=[SMEM] + [whole_spec(v) for v in feeds] + [whole_spec(wr), part, part] + [ANY] * len(deps),
        out_specs=[whole_spec(v) for v in outs],
        out_shape=outs,
        scratch_shapes=[
            pltpu.VMEM((deep + LANES, tokens), bf16),
            pltpu.VMEM((tokens, deep + LANES), bf16),
            pltpu.VMEM((tokens, wide), f32),
            pltpu.VMEM((tokens, LANES), f32),
        ],
        compiler_params=params(20),
        cost_estimate=hint(
            4 * experts * depth * hidden * tokens, 4 * experts * depth * hidden + 6 * tokens * wide, 4.0
        ),
        name="gate_up_partial",
    )(scal, *feeds, wr, wg, wu, *deps)


def sum_kernel(base, scal, own, recv, *refs):
    keep, send = refs[-2:]
    y = scal[2]
    th, wide = keep.shape
    main = wide - LANES
    for to, first in ((keep, y), (send, 1 - y)):
        rows = pl.ds(pl.multiple_of(first * th, th), th)
        to[:, 0:main] = (own[rows, 0:main] + recv[rows, 0:main].astype(f32)).astype(to.dtype)
        v = own[rows, main:] + joined_lanes(recv[rows, main:].astype(f32), base)
        to[:, main:] = v if to is keep else spread_lanes(v, base)


def sum_call(scal, base, own, recv, deps):
    tokens, wide = own.shape
    return pl.pallas_call(
        lambda *refs: sum_kernel(base, *refs),
        in_specs=[SMEM, VMEM, VMEM] + [ANY] * len(deps),
        out_specs=[VMEM, VMEM],
        out_shape=[shape((tokens // 2, wide), f32), shape((tokens // 2, wide), bf16)],
        compiler_params=params(),
        cost_estimate=hint(tokens * wide, 9 * tokens * wide),
        name="core_sum",
    )(scal, own, recv, *deps)


def act_kernel(base, scal, keep, recv, cols, *refs):
    act = refs[-1]
    core, y = scal[0], scal[2]
    th, half = act.shape
    main = 2 * half - LANES
    m = keep[:, main:] + joined_lanes(recv[:, main:].astype(f32), base)
    mine, other = slot_columns(core, cols[pl.ds(pl.multiple_of(y * th, th), th)])
    scale = lax.rsqrt(m[:, base : base + 1] / WIDTH + epsilon)
    la = lb = jnp.zeros_like(scale)
    for e in range(4):
        logit = m[:, base + 1 + e : base + 2 + e] * scale
        la = jnp.where(mine == e, logit, la)
        lb = jnp.where(other == e, logit, lb)
    mix = scale / (1.0 + jnp.exp(lb - la))
    g = (keep[:, 0:half] + recv[:, 0:half].astype(f32)) * scale
    u = (keep[:, half:] + recv[:, half:].astype(f32)) * mix
    act[...] = (g / (1.0 + jnp.exp(-g)) * u).astype(bf16)


def act_call(scal, base, keep, recv, cols, deps):
    th, wide = keep.shape
    return pl.pallas_call(
        lambda *refs: act_kernel(base, *refs),
        in_specs=[SMEM] + [VMEM] * 3 + [ANY] * len(deps),
        out_specs=VMEM,
        out_shape=shape((th, wide // 2), bf16),
        compiler_params=params(),
        cost_estimate=hint(6 * th * wide, 7 * th * wide),
        name="act",
    )(scal, keep, recv, cols, *deps)


def down_kernel(sides, scal, a, a_y, b, b_y, cols, wd, *refs):
    outs = refs[-sides - 2 : -2]
    whole, acc = refs[-2:]
    e = pl.program_id(0)
    core, side, y = scal[0], scal[1], scal[2]
    th = a.shape[0]
    width, hidden = wd.shape[1:]
    block = width // sides

    @pl.when(e == 0)
    def _():
        for k, near, far in ((0, a, a_y), (1, b, b_y)):
            whole[k, pl.ds(pl.multiple_of(y * th, th), th)] = near[...]
            whole[k, pl.ds(pl.multiple_of((1 - y) * th, th), th)] = far[...]

    ef = e.astype(f32)
    masks = [jnp.where(v == ef, 1.0, 0.0).astype(bf16) for v in slot_columns(core, cols[...])]
    rows = whole[0, :, 0:hidden] * masks[0] + whole[1, :, 0:hidden] * masks[1]
    d = lax.dot_general(wd[0], rows, (((1,), (1,)), ((), ())), preferred_element_type=f32)

    @pl.when(e == 0)
    def _():
        acc[...] = d

    @pl.when(e > 0)
    def _():
        acc[...] += d

    @pl.when(e == pl.num_programs(0) - 1)
    def _():
        for i in range(sides):
            rows = pl.ds(pl.multiple_of((side ^ i) * block, 16), block)
            outs[i][...] = acc[rows].astype(bf16)


def down_call(scal, sides, pieces, cols, wd, deps):
    experts, width, hidden = wd.shape
    tokens = cols.shape[0]
    outs = [shape((width // sides, tokens), bf16)] * sides
    return pl.pallas_call(
        lambda *refs: down_kernel(sides, *refs),
        grid=(experts,),
        in_specs=[SMEM]
        + [whole_spec(v) for v in pieces]
        + [whole_spec(cols), pl.BlockSpec((1, width, hidden), lambda n: (n, 0, 0))]
        + [ANY] * len(deps),
        out_specs=[whole_spec(v) for v in outs],
        out_shape=outs,
        scratch_shapes=[
            pltpu.VMEM((2, tokens, pieces[0].shape[1]), bf16),
            pltpu.VMEM((width, tokens), f32),
        ],
        compiler_params=params(20),
        cost_estimate=hint(
            2 * experts * width * hidden * tokens, 2 * experts * width * hidden + 2 * width * tokens, 4.0
        ),
        name="down",
    )(scal, *pieces, cols, wd, *deps)


def total_kernel(meta, stream, *refs):
    parts, (total, message) = refs[:-2], refs[-2:]
    v = parts[0][...].astype(f32)
    for ref in parts[1:]:
        v = v + ref[...].astype(f32)
    total[...] = v
    reqs = stream.shape[0]
    ends = columns_at(meta[5:6].astype(f32), v)
    ends = stream[...] + branch_scale * ends[0:reqs]
    message[...] = jnp.broadcast_to(ends[None], message.shape)


def total_call(feed, stream, parts, block, count):
    tokens = feed.shape[1]
    full = lambda v: pl.BlockSpec(v.shape, lambda n: (0,) * len(v.shape))
    outs = [shape((block, tokens), f32), shape((count, *stream.shape), f32)]
    return pl.pallas_call(
        total_kernel,
        grid=(1,),
        in_specs=[pl.BlockSpec((META, tokens), lambda n: (block // META, 0)), full(stream)]
        + [full(v) for v in parts],
        out_specs=[full(v) for v in outs],
        out_shape=outs,
        compiler_params=params(),
        cost_estimate=hint(16 * block * tokens, 14 * block * tokens),
        name="branch_total",
    )(feed, stream, *parts)


def head_kernel(order, got, gain, words, softness, logits, message, wide):
    blocks, block = gain.shape
    rows, columns = logits.shape
    ends, squares = [], 0.0
    for b in range(blocks):
        v = jnp.concatenate([got[i] for i in order[b]], axis=0)
        squares = squares + jnp.sum(v * v, axis=1, keepdims=True)
        ends.append(v)
    scale = lax.rsqrt(squares / WIDTH + epsilon)
    total = jnp.zeros((rows, columns), f32)
    for b in range(blocks):
        feed = (ends[b] * scale * gain[b : b + 1]).astype(bf16)
        total += jnp.dot(feed, words[b * block : (b + 1) * block], preferred_element_type=f32)
    total = total / (WIDTH / 256.0 * softness[...])
    logits[...] = total
    top = jnp.max(total, axis=1, keepdims=True)
    mass = jnp.sum(jnp.exp(total - top), axis=1, keepdims=True)
    wide[...] = jnp.zeros_like(wide)
    lane = lax.broadcasted_iota(jnp.int32, (rows, LANES), 1)
    wide[0:rows] = jnp.where(lane == 0, top, jnp.where(lane == 1, mass, 0.0))
    turned = wide[...].T
    message[...] = jnp.broadcast_to(turned[None, 0:2, 0:rows], message.shape)


def head_call(order, got, gain, words, softness):
    rows, columns = softness.shape[0], words.shape[1]
    return pl.pallas_call(
        lambda *refs: head_kernel(order, *refs),
        in_specs=[VMEM] * 4,
        out_specs=[VMEM, VMEM],
        out_shape=[shape((rows, columns), f32), shape((got.shape[0], 2, rows), f32)],
        scratch_shapes=[pltpu.VMEM((LANES, LANES), f32)],
        compiler_params=params(),
        cost_estimate=hint(2 * rows * WIDTH * columns, 2 * WIDTH * columns),
        name="head",
    )(got, gain, words, softness)


def body(
    skip_stream_arriving,
    chosen_specialists,
    sequence_piece_tallies,
    premix_rmsnorm_gain,
    dispatcher_weights,
    specialist_switch_weights,
    specialist_expand_weights,
    specialist_contract_weights,
    terminal_rmsnorm_gain,
    lexicon_projector_weights,
    softness_per_sequence,
):
    tokens, block = skip_stream_arriving.shape
    dp, mp = lax.axis_size("dp"), lax.axis_size("mp")
    count = dp * mp
    parts = 4
    spread, sides = dp // parts, mp // parts
    assert dp == parts * spread and mp == parts * sides and sides & (sides - 1) == 0
    part = lax.axis_index("dp") // spread
    y, core = part // 2, part % 2
    side = lax.axis_index("mp") % sides

    def send(value, to):
        pairs = []
        for q in range(parts):
            for r in range(spread):
                for z in range(parts):
                    for x in range(sides):
                        q2, z2, x2 = to(q, z, x)
                        source = (q * spread + r) * mp + z * sides + x
                        pairs.append((source, (q2 * spread + r) * mp + z2 * sides + x2))
        return lax.ppermute(value, ("dp", "mp"), pairs)

    other_core = lambda q, z, x: (q ^ 1, z, x)
    other_y = lambda q, z, x: (q ^ 2, z, x)
    home = lambda q, z, x: (z, q, x)

    scal = jnp.stack([core, side, y]).astype(jnp.int32)
    sent, stream = prep_call(
        skip_stream_arriving.T, premix_rmsnorm_gain[None], chosen_specialists.T, sequence_piece_tallies
    )
    wg, wu, wd = specialist_switch_weights, specialist_expand_weights, specialist_contract_weights
    if spread > 1:
        runs = [[q * spread + r for r in range(spread)] for q in range(parts)]
        wg = lax.all_gather(wg, "dp", axis=1, tiled=True, axis_index_groups=runs)
        wu = lax.all_gather(wu, "dp", axis=1, tiled=True, axis_index_groups=runs)
        wd = lax.all_gather(wd, "dp", axis=2, tiled=True, axis_index_groups=runs)
    wd = jnp.swapaxes(wd, 1, 2)
    depth, hidden = wg.shape[1:]
    base = hidden % LANES
    wr = lax.dynamic_slice_in_dim(dispatcher_weights.T, part * depth, depth, axis=1)
    room = lambda at: jnp.pad(wr, ((at, LANES - at - wr.shape[0]), (0, 0)))
    wr = room(base + 1) + room(base + 1 + EXTRA)

    chunks = ((1,), (2,), (3,), (0,))
    first = [send(sent, lambda q, z, x, i=i: (z, (q - 1) % parts, x ^ i)) for i in range(sides)]
    pair = join_call(first)
    feeds = {1: pair}
    for group in (2, 3, 0):
        feeds[group] = send(feeds[(group - 1) % parts], lambda q, z, x: (q, (z - 1) % parts, x))
    stream = send(stream, home)
    partial, kept, pieces, shares = {}, {}, {}, {}

    def do_partial(s, *deps):
        own, give, cols = partial_call(scal, sides, [feeds[g] for g in chunks[s]], wr, wg, wu, deps)
        partial[s] = (own, send(give, other_core), cols)
        return own

    def do_sum(s, *deps):
        own, recv, _ = partial[s]
        keep, give = sum_call(scal, base, own, recv, deps)
        kept[s] = (keep, send(give, other_y))
        return keep

    def do_act(s, *deps):
        a = act_call(scal, base, *kept[s], partial[s][2], deps)
        a_y = send(a, other_y)
        pieces[s] = (a, a_y, send(a, other_core), send(a_y, other_core))
        return a

    def do_down(s, *deps):
        outs = down_call(scal, sides, pieces[s], partial[s][2], wd, deps)
        got = [outs[0]] + [send(outs[i], lambda q, z, x, i=i: (q, z, x ^ i)) for i in range(1, sides)]
        for n, group in enumerate(chunks[s]):
            to = slice(n * tokens, (n + 1) * tokens)
            if group == 0:
                shares[0] = [v[:, to] for v in got]
            else:
                share = sum(v[:, to].astype(f32) for v in got).astype(bf16)
                back = lambda q, z, x, group=group: (q, (z + group) % parts, x)
                shares[group] = [send(share, back)]
        return outs[0]

    p0 = do_partial(0)
    p1 = do_partial(1, p0)
    s0 = do_sum(0, p1)
    p2 = do_partial(2, s0)
    s1 = do_sum(1, p2)
    a0 = do_act(0, s1)
    p3 = do_partial(3, a0)
    s2 = do_sum(2, p3)
    a1 = do_act(1, s2)
    d0 = do_down(0, a1)
    s3 = do_sum(3, d0)
    a2 = do_act(2, s3)
    d1 = do_down(1, a2)
    a3 = do_act(3, d1)
    d2 = do_down(2, a3)
    d3 = do_down(3, d2)
    mine = [v for group in range(parts) for v in shares[group]]
    total, message = total_call(feeds[0], stream, mine, block, count)

    everyone = lambda v: lax.all_to_all(v, ("dp", "mp"), 0, 0, tiled=True)
    got = everyone(message)
    branch = send(total, home)
    order = [
        [
            (q * spread + r) * mp + z * sides + x
            for z in range(parts)
            for r in range(spread)
        ]
        for q in range(parts)
        for x in range(sides)
    ]
    logits, pairs = head_call(
        order,
        got,
        terminal_rmsnorm_gain.reshape(mp, block),
        lexicon_projector_weights,
        softness_per_sequence[:, None],
    )
    pairs = everyone(pairs)
    new_hidden = skip_stream_arriving + branch_scale * branch.T
    largest = jnp.max(pairs[:, 0], axis=0)
    mass = jnp.sum(pairs[:, 1] * jnp.exp(pairs[:, 0] - largest), axis=0)
    logprobs = logits - largest[:, None] - jnp.log(mass)[:, None]
    return (new_hidden, logprobs)


def solution(mesh):
    return jax.shard_map(
        body,
        mesh=mesh,
        in_specs=(
            P("dp", "mp"),
            P("dp", None),
            P("dp", None),
            P("mp"),
            P(),
            P(None, "dp", "mp"),
            P(None, "dp", "mp"),
            P(None, "mp", "dp"),
            P(),
            P(None, ("dp", "mp")),
            P(),
        ),
        out_specs=(P("dp", "mp"), P(None, ("dp", "mp"))),
        check_vma=False,
    )
```

```python
import math

import jax
import jax.numpy as jnp
from jax import lax
from jax.experimental import pallas as pl
from jax.experimental.pallas import tpu as pltpu
from jax.sharding import PartitionSpec as P

WIDTH = 2304
META = 16
LANES = 128
branch_scale = 1.4 / math.sqrt(40.0)
epsilon = 1e-05
f32, bf16 = jnp.float32, jnp.bfloat16

VMEM = pl.BlockSpec(memory_space=pltpu.VMEM)
SMEM = pl.BlockSpec(memory_space=pltpu.SMEM)
ANY = pl.BlockSpec(memory_space=pl.ANY)


def up_to(n, step=LANES):
    return -(-n // step) * step


def params(mib=16):
    return pltpu.CompilerParams(vmem_limit_bytes=mib * 2**20)


def hint(flops, bytes_accessed, scale=0.3):
    return pl.CostEstimate(int(flops * scale), 0, int(bytes_accessed * scale))


def shape(dims, dtype):
    return jax.ShapeDtypeStruct(dims, dtype)


def prep_kernel(tallies, x, gain, routes, out, ends):
    block, tokens = x.shape
    v = x[...]
    wide = up_to(block)
    g = jnp.concatenate([gain[...], jnp.zeros((1, wide - block), f32)], axis=1)
    g = jnp.broadcast_to(g, (LANES, wide)).T[0:block, 0:1]
    out[0:block] = (v * g).astype(bf16)
    sq = jnp.sum(v * v, axis=0, keepdims=True)
    hi = sq.astype(bf16).astype(f32)
    mid = (sq - hi).astype(bf16).astype(f32)
    here = lax.broadcasted_iota(jnp.int32, (1, tokens), 1)
    mark, end = jnp.zeros((1, tokens), f32), jnp.int32(-1)
    for q in range(ends.shape[0]):
        end = end + tallies[0, q]
        mark = jnp.where(here == end, q + 1.0, mark)
    rows = [routes[...].astype(f32), hi, mid, sq - hi - mid, mark]
    rows.append(jnp.zeros((META - 6, tokens), f32))
    out[block:] = jnp.concatenate(rows, axis=0).astype(bf16)
    ends[...] = columns_at(mark, v)[0 : ends.shape[0]]


def columns_at(mark, v):
    row = lax.broadcasted_iota(jnp.int32, (8, mark.shape[1]), 0)
    pick = jnp.where(mark == (row + 1).astype(f32), 1.0, 0.0)
    return lax.dot_general(
        pick, v, (((1,), (1,)), ((), ())), precision=lax.Precision.HIGHEST, preferred_element_type=f32
    )


def whole_spec(v):
    return pl.BlockSpec(v.shape, lambda *_: (0,) * len(v.shape))


def prep_call(x, gain, routes, tallies):
    block, tokens = x.shape
    reqs = tallies.shape[1]
    outs = [shape((block + META, tokens), bf16), shape((reqs, block), f32)]
    return pl.pallas_call(
        prep_kernel,
        grid=(1,),
        in_specs=[SMEM] + [whole_spec(v) for v in (x, gain, routes)],
        out_specs=[whole_spec(v) for v in outs],
        out_shape=outs,
        compiler_params=params(60),
        cost_estimate=hint(4 * tokens * block, 6 * tokens * block),
        name="prep",
    )(tallies, x, gain, routes)


def join_call(blocks):
    rows, tokens = blocks[0].shape

    def join_kernel(*refs):
        for i, ref in enumerate(refs[:-1]):
            refs[-1][i * rows : (i + 1) * rows] = ref[...]

    return pl.pallas_call(
        join_kernel,
        in_specs=[VMEM] * len(blocks),
        out_specs=VMEM,
        out_shape=shape((len(blocks) * rows, tokens), bf16),
        compiler_params=params(),
        cost_estimate=hint(1, 4 * len(blocks) * rows * tokens),
        name="join",
    )(*blocks)


EXTRA = 5


def spread_lanes(v, base):
    lane = lax.broadcasted_iota(jnp.int32, v.shape, 1)
    hi = v.astype(bf16).astype(f32)
    return jnp.where(lane < base, v, jnp.where(lane < base + EXTRA, hi, v - hi)).astype(bf16)


def joined_lanes(v, base):
    lane = lax.broadcasted_iota(jnp.int32, v.shape, 1)
    left, right = pltpu.roll(v, LANES - EXTRA, 1), pltpu.roll(v, EXTRA, 1)
    return v + jnp.where(lane < base, 0.0, jnp.where(lane < base + EXTRA, left, right))


def slot_columns(core, cols):
    first, second = cols[:, 0:1].astype(f32), cols[:, 1:2].astype(f32)
    zero = core == 0
    return jnp.where(zero, first, second), jnp.where(zero, second, first)


def partial_kernel(sides, held, scal, *refs):
    feeds, (wr, wg, wu) = refs[:held], refs[held : held + 3]
    own, give, cols, xs, xt, acc, extra = refs[-7:]
    e = pl.program_id(0)
    core, side = scal[0], scal[1]
    depth, hidden = wg.shape[1:]
    deep, half = up_to(depth), up_to(hidden)
    base = hidden % LANES
    tokens = feeds[0].shape[1]
    block = depth // sides
    last = slice(2 * half - LANES, 2 * half)

    @pl.when(e == 0)
    def _():
        xs[depth:] = jnp.zeros((deep + LANES - depth, xs.shape[1]), bf16)
        for n, ref in enumerate(feeds):
            to = slice(n * tokens, (n + 1) * tokens)
            for i in range(sides):
                at = i * (block + META)
                xs[pl.ds(pl.multiple_of((side ^ i) * block, 16), block), to] = ref[at : at + block]
                xs[deep + i * META : deep + (i + 1) * META, to] = ref[at + block : at + block + META]
        xt[...] = xs[...].T
        more = xt[:, deep:]
        cols[...] = more
        more = more.astype(f32)
        sq = jnp.zeros((more.shape[0], 1), f32)
        for i in range(sides):
            for term in (4, 3, 2):
                sq = sq + more[:, i * META + term : i * META + term + 1]
        router = lax.dot_general(
            xt[:, 0:depth], wr[...], (((1,), (1,)), ((), ())), preferred_element_type=f32
        )
        lane = lax.broadcasted_iota(jnp.int32, router.shape, 1)
        extra[...] = router + jnp.where((lane == base) | (lane == base + EXTRA), sq, 0.0)
        for ref in (own, acc):
            ref[:, half - LANES : half] = jnp.zeros((xt.shape[0], LANES), f32)
            ref[:, last] = jnp.zeros((xt.shape[0], LANES), f32)

    mine, other = slot_columns(core, xt[:, deep : deep + LANES])
    ef = e.astype(f32)
    take = [(v == ef) | (e == 0) for v in (mine, other)]
    for which, w in enumerate((wg, wu)):
        for at in range(0, hidden, 256):
            end = min(hidden, at + 256)
            d = jnp.dot(xt[:, 0:depth], w[0, :, at:end], preferred_element_type=f32)
            to = slice(which * half + at, which * half + end)
            for ref, pick in ((own, take[0]), (acc, take[1])):
                ref[:, to] = jnp.where(pick, d, ref[:, to])

    @pl.when(e == pl.num_programs(0) - 1)
    def _():
        lane = lax.broadcasted_iota(jnp.int32, extra.shape, 1)
        more = extra[...]
        own[:, last] = jnp.where(lane < base, own[:, last], more)
        give[:, 0 : last.start] = acc[:, 0 : last.start].astype(bf16)
        give[:, last] = spread_lanes(jnp.where(lane < base, acc[:, last], more), base)


def partial_call(scal, sides, feeds, wr, wg, wu, mib, deps):
    experts, depth, hidden = wg.shape
    tokens = feeds[0].shape[1] * len(feeds)
    deep, wide = up_to(depth), 2 * up_to(hidden)
    part = pl.BlockSpec((1, depth, hidden), lambda n: (n, 0, 0))
    outs = [shape((tokens, wide), f32), shape((tokens, wide), bf16), shape((tokens, LANES), bf16)]
    return pl.pallas_call(
        lambda *refs: partial_kernel(sides, len(feeds), *refs),
        grid=(experts,),
        in_specs=[SMEM] + [whole_spec(v) for v in feeds] + [whole_spec(wr), part, part] + [ANY] * len(deps),
        out_specs=[whole_spec(v) for v in outs],
        out_shape=outs,
        scratch_shapes=[
            pltpu.VMEM((deep + LANES, tokens), bf16),
            pltpu.VMEM((tokens, deep + LANES), bf16),
            pltpu.VMEM((tokens, wide), f32),
            pltpu.VMEM((tokens, LANES), f32),
        ],
        compiler_params=params(mib),
        cost_estimate=hint(
            4 * experts * depth * hidden * tokens, 4 * experts * depth * hidden + 6 * tokens * wide, 4
        ),
        name="gate_up_partial",
    )(scal, *feeds, wr, wg, wu, *deps)


def sum_kernel(base, scal, own, recv, *refs):
    keep, send = refs[-2:]
    y = scal[2]
    th, wide = keep.shape
    main = wide - LANES
    for to, first in ((keep, y), (send, 1 - y)):
        rows = pl.ds(pl.multiple_of(first * th, th), th)
        to[:, 0:main] = (own[rows, 0:main] + recv[rows, 0:main].astype(f32)).astype(to.dtype)
        v = own[rows, main:] + joined_lanes(recv[rows, main:].astype(f32), base)
        to[:, main:] = v if to is keep else spread_lanes(v, base)


def sum_call(scal, base, own, recv, deps):
    tokens, wide = own.shape
    return pl.pallas_call(
        lambda *refs: sum_kernel(base, *refs),
        in_specs=[SMEM, VMEM, VMEM] + [ANY] * len(deps),
        out_specs=[VMEM, VMEM],
        out_shape=[shape((tokens // 2, wide), f32), shape((tokens // 2, wide), bf16)],
        compiler_params=params(),
        cost_estimate=hint(tokens * wide, 9 * tokens * wide),
        name="core_sum",
    )(scal, own, recv, *deps)


def act_kernel(base, scal, keep, recv, cols, *refs):
    act = refs[-1]
    core, y = scal[0], scal[2]
    th, half = act.shape
    main = 2 * half - LANES
    m = keep[:, main:] + joined_lanes(recv[:, main:].astype(f32), base)
    mine, other = slot_columns(core, cols[pl.ds(pl.multiple_of(y * th, th), th)])
    scale = lax.rsqrt(m[:, base : base + 1] / WIDTH + epsilon)
    la = lb = jnp.zeros_like(scale)
    for e in range(4):
        logit = m[:, base + 1 + e : base + 2 + e] * scale
        la = jnp.where(mine == e, logit, la)
        lb = jnp.where(other == e, logit, lb)
    mix = scale / (1.0 + jnp.exp(lb - la))
    g = (keep[:, 0:half] + recv[:, 0:half].astype(f32)) * scale
    u = (keep[:, half:] + recv[:, half:].astype(f32)) * mix
    act[...] = (g / (1.0 + jnp.exp(-g)) * u).astype(bf16)


def act_call(scal, base, keep, recv, cols, deps):
    th, wide = keep.shape
    return pl.pallas_call(
        lambda *refs: act_kernel(base, *refs),
        in_specs=[SMEM] + [VMEM] * 3 + [ANY] * len(deps),
        out_specs=VMEM,
        out_shape=shape((th, wide // 2), bf16),
        compiler_params=params(),
        cost_estimate=hint(6 * th * wide, 7 * th * wide),
        name="act",
    )(scal, keep, recv, cols, *deps)


def down_kernel(sides, scal, a, a_y, b, b_y, cols, wd, *refs):
    outs = refs[-sides - 2 : -2]
    whole, acc = refs[-2:]
    e = pl.program_id(0)
    core, side, y = scal[0], scal[1], scal[2]
    th = a.shape[0]
    width, hidden = wd.shape[1:]
    block = width // sides

    @pl.when(e == 0)
    def _():
        for k, near, far in ((0, a, a_y), (1, b, b_y)):
            whole[k, pl.ds(pl.multiple_of(y * th, th), th)] = near[...]
            whole[k, pl.ds(pl.multiple_of((1 - y) * th, th), th)] = far[...]

    ef = e.astype(f32)
    masks = [jnp.where(v == ef, 1.0, 0.0).astype(bf16) for v in slot_columns(core, cols[...])]
    rows = whole[0, :, 0:hidden] * masks[0] + whole[1, :, 0:hidden] * masks[1]
    d = lax.dot_general(wd[0], rows, (((1,), (1,)), ((), ())), preferred_element_type=f32)

    @pl.when(e == 0)
    def _():
        acc[...] = d

    @pl.when(e > 0)
    def _():
        acc[...] += d

    @pl.when(e == pl.num_programs(0) - 1)
    def _():
        for i in range(sides):
            rows = pl.ds(pl.multiple_of((side ^ i) * block, 16), block)
            outs[i][...] = acc[rows].astype(bf16)


def down_call(scal, sides, pieces, cols, wd, deps):
    experts, width, hidden = wd.shape
    tokens = cols.shape[0]
    outs = [shape((width // sides, tokens), bf16)] * sides
    return pl.pallas_call(
        lambda *refs: down_kernel(sides, *refs),
        grid=(experts,),
        in_specs=[SMEM]
        + [whole_spec(v) for v in pieces]
        + [whole_spec(cols), pl.BlockSpec((1, width, hidden), lambda n: (n, 0, 0))]
        + [ANY] * len(deps),
        out_specs=[whole_spec(v) for v in outs],
        out_shape=outs,
        scratch_shapes=[
            pltpu.VMEM((2, tokens, pieces[0].shape[1]), bf16),
            pltpu.VMEM((width, tokens), f32),
        ],
        compiler_params=params(20),
        cost_estimate=hint(
            2 * experts * width * hidden * tokens, 2 * experts * width * hidden + 2 * width * tokens, 4
        ),
        name="down",
    )(scal, *pieces, cols, wd, *deps)


def ends_kernel(sides, cols, stream, *refs):
    outs, backs, message = refs[:sides], refs[sides : sides + 3], refs[sides + 3]
    reqs = stream.shape[0]
    mark = cols[...].astype(f32).T[5:6]
    for i, ref in enumerate(outs):
        v = ref[...].astype(f32)
        if i == 0:
            for back in backs:
                v = v + back[...].astype(f32)
        ends = branch_scale * columns_at(mark, v)[0:reqs]
        if i == 0:
            ends = ends + stream[...]
        message[:, i * reqs : (i + 1) * reqs] = jnp.broadcast_to(ends[None], (message.shape[0], *ends.shape))


def ends_call(cols, stream, outs, backs, count):
    reqs, block = stream.shape
    args = (cols, stream, *outs, *backs)
    out = shape((count, len(outs) * reqs, block), f32)
    return pl.pallas_call(
        lambda *refs: ends_kernel(len(outs), *refs),
        grid=(1,),
        in_specs=[whole_spec(v) for v in args],
        out_specs=whole_spec(out),
        out_shape=out,
        compiler_params=params(),
        cost_estimate=hint(16 * block * cols.shape[0], 14 * block * cols.shape[0]),
        name="end_rows",
    )(*args)


def head_kernel(order, got, gain, words, softness, logits, message, wide):
    blocks, block = gain.shape
    rows, columns = logits.shape
    ends, squares = [], 0.0
    reqs = rows // len(order[0])
    for b in range(blocks):
        v = []
        for sources in order[b]:
            terms = [got[at, i * reqs : (i + 1) * reqs] for at, i in sources]
            v.append(sum(terms[1:], terms[0]))
        v = jnp.concatenate(v, axis=0)
        squares = squares + jnp.sum(v * v, axis=1, keepdims=True)
        ends.append(v)
    scale = lax.rsqrt(squares / WIDTH + epsilon)
    total = jnp.zeros((rows, columns), f32)
    for b in range(blocks):
        feed = (ends[b] * scale * gain[b : b + 1]).astype(bf16)
        total += jnp.dot(feed, words[b * block : (b + 1) * block], preferred_element_type=f32)
    total = total / (WIDTH / 256.0 * softness[...])
    logits[...] = total
    top = jnp.max(total, axis=1, keepdims=True)
    mass = jnp.sum(jnp.exp(total - top), axis=1, keepdims=True)
    wide[...] = jnp.zeros_like(wide)
    lane = lax.broadcasted_iota(jnp.int32, (rows, LANES), 1)
    wide[0:rows] = jnp.where(lane == 0, top, jnp.where(lane == 1, mass, 0.0))
    turned = wide[...].T
    message[...] = jnp.broadcast_to(turned[None, 0:2, 0:rows], message.shape)


def head_call(order, got, gain, words, softness):
    rows, columns = softness.shape[0], words.shape[1]
    return pl.pallas_call(
        lambda *refs: head_kernel(order, *refs),
        in_specs=[VMEM] * 4,
        out_specs=[VMEM, VMEM],
        out_shape=[shape((rows, columns), f32), shape((got.shape[0], 2, rows), f32)],
        scratch_shapes=[pltpu.VMEM((LANES, LANES), f32)],
        compiler_params=params(),
        cost_estimate=hint(2 * rows * WIDTH * columns, 2 * WIDTH * columns),
        name="head",
    )(got, gain, words, softness)


def body(
    skip_stream_arriving,
    chosen_specialists,
    sequence_piece_tallies,
    premix_rmsnorm_gain,
    dispatcher_weights,
    specialist_switch_weights,
    specialist_expand_weights,
    specialist_contract_weights,
    terminal_rmsnorm_gain,
    lexicon_projector_weights,
    softness_per_sequence,
):
    tokens, block = skip_stream_arriving.shape
    dp, mp = lax.axis_size("dp"), lax.axis_size("mp")
    count = dp * mp
    parts = 4
    spread, sides = dp // parts, mp // parts
    assert dp == parts * spread and mp == parts * sides and sides & (sides - 1) == 0
    part = lax.axis_index("dp") // spread
    y, core = part // 2, part % 2
    side = lax.axis_index("mp") % sides

    def send(value, to):
        pairs = []
        for q in range(parts):
            for r in range(spread):
                for z in range(parts):
                    for x in range(sides):
                        q2, z2, x2 = to(q, z, x)
                        source = (q * spread + r) * mp + z * sides + x
                        pairs.append((source, (q2 * spread + r) * mp + z2 * sides + x2))
        return lax.ppermute(value, ("dp", "mp"), pairs)

    other_core = lambda q, z, x: (q ^ 1, z, x)
    other_y = lambda q, z, x: (q ^ 2, z, x)
    home = lambda q, z, x: (z, q, x)

    scal = jnp.stack([core, side, y]).astype(jnp.int32)
    sent, stream = prep_call(
        skip_stream_arriving.T, premix_rmsnorm_gain[None], chosen_specialists.T, sequence_piece_tallies
    )
    wg, wu, wd = specialist_switch_weights, specialist_expand_weights, specialist_contract_weights
    if spread > 1:
        runs = [[q * spread + r for r in range(spread)] for q in range(parts)]
        wg = lax.all_gather(wg, "dp", axis=1, tiled=True, axis_index_groups=runs)
        wu = lax.all_gather(wu, "dp", axis=1, tiled=True, axis_index_groups=runs)
        wd = lax.all_gather(wd, "dp", axis=2, tiled=True, axis_index_groups=runs)
    wd = jnp.swapaxes(wd, 1, 2)
    depth, hidden = wg.shape[1:]
    base = hidden % LANES
    wr = lax.dynamic_slice_in_dim(dispatcher_weights.T, part * depth, depth, axis=1)
    room = lambda at: jnp.pad(wr, ((at, LANES - at - wr.shape[0]), (0, 0)))
    wr = room(base + 1) + room(base + 1 + EXTRA)

    chunks = ((1,), (2,), (3,), (0,))
    first = [send(sent, lambda q, z, x, i=i: (z, (q - 1) % parts, x ^ i)) for i in range(sides)]
    pair = join_call(first)
    feeds = {1: pair}
    step = lambda v: send(v, lambda q, z, x: (q, (z - 1) % parts, x))
    feeds[2] = step(pair)
    feeds[3] = step(feeds[2])
    stream = send(stream, home)
    partial, kept, pieces, shares, last = {}, {}, {}, {}, []

    def do_partial(s, *deps):
        own, give, cols = partial_call(scal, sides, [feeds[g] for g in chunks[s]], wr, wg, wu, 20 if s else 57, deps)
        partial[s] = (own, send(give, other_core), cols)
        return own

    def do_sum(s, *deps):
        own, recv, _ = partial[s]
        keep, give = sum_call(scal, base, own, recv, deps)
        kept[s] = (keep, send(give, other_y))
        return keep

    def do_act(s, *deps):
        a = act_call(scal, base, *kept[s], partial[s][2], deps)
        pieces[s] = (a, send(a, other_y))
        return a

    def do_hop(s, dep):
        a, a_y = pieces[s]
        late = [v if dep is None else lax.optimization_barrier((v, dep))[0] for v in (a, a_y)]
        pieces[s] = (a, a_y, *[send(v, other_core) for v in late])

    def do_down(s, *deps):
        outs = down_call(scal, sides, pieces[s], partial[s][2], wd, deps)
        last[:] = outs
        got = [outs[0]] + [send(outs[i], lambda q, z, x, i=i: (q, z, x ^ i)) for i in range(1, sides)]
        for n, group in enumerate(chunks[s]):
            to = slice(n * tokens, (n + 1) * tokens)
            if group == 0:
                shares[0] = [v[:, to] for v in got]
            else:
                share = sum(v[:, to].astype(f32) for v in got).astype(bf16)
                back = lambda q, z, x, group=group: (q, (z + group) % parts, x)
                shares[group] = [send(share, back)]
        return outs[0]

    p0 = do_partial(0)
    p1 = do_partial(1, p0)
    s0 = do_sum(0, p1)
    p2 = do_partial(2, s0)
    feeds[0] = step(lax.optimization_barrier((feeds[3], p2))[0])
    s1 = do_sum(1, p2)
    a0 = do_act(0, s1)
    p3 = do_partial(3, a0)
    s2 = do_sum(2, p3)
    do_hop(0, s2)
    a1 = do_act(1, s2)
    d0 = do_down(0, a1)
    s3 = do_sum(3, d0)
    do_hop(1, s3)
    a2 = do_act(2, s3)
    d1 = do_down(1, a2)
    do_hop(2, None)
    a3 = do_act(3, d1)
    d2 = do_down(2, a3)
    do_hop(3, None)
    d3 = do_down(3, d2)
    backs = [shares[group][0] for group in range(1, parts)]
    message = ends_call(partial[parts - 1][2], stream, last, backs, count)
    total = sum(v.astype(f32) for v in shares[0] + backs)

    everyone = lambda v: lax.all_to_all(v, ("dp", "mp"), 0, 0, tiled=True)
    got = everyone(message)
    branch = send(total, home)
    order = [
        [
            [((q * spread + r) * mp + z * sides + x2, x2 ^ x) for x2 in range(sides)]
            for z in range(parts)
            for r in range(spread)
        ]
        for q in range(parts)
        for x in range(sides)
    ]
    logits, pairs = head_call(
        order,
        got,
        terminal_rmsnorm_gain.reshape(mp, block),
        lexicon_projector_weights,
        softness_per_sequence[:, None],
    )
    pairs = everyone(pairs)
    new_hidden = skip_stream_arriving + branch_scale * branch.T
    largest = jnp.max(pairs[:, 0], axis=0)
    mass = jnp.sum(pairs[:, 1] * jnp.exp(pairs[:, 0] - largest), axis=0)
    logprobs = logits - largest[:, None] - jnp.log(mass)[:, None]
    return (new_hidden, logprobs)


def solution(mesh):
    return jax.shard_map(
        body,
        mesh=mesh,
        in_specs=(
            P("dp", "mp"),
            P("dp", None),
            P("dp", None),
            P("mp"),
            P(),
            P(None, "dp", "mp"),
            P(None, "dp", "mp"),
            P(None, "mp", "dp"),
            P(),
            P(None, ("dp", "mp")),
            P(),
        ),
        out_specs=(P("dp", "mp"), P(None, ("dp", "mp"))),
        check_vma=False,
    )
```

```python
import math

import jax
import jax.numpy as jnp
from jax import lax
from jax.experimental import pallas as pl
from jax.experimental.pallas import tpu as pltpu
from jax.sharding import PartitionSpec as P

WIDTH = 2304
META = 16
LANES = 128
branch_scale = 1.4 / math.sqrt(40.0)
epsilon = 1e-05
f32, bf16 = jnp.float32, jnp.bfloat16

VMEM = pl.BlockSpec(memory_space=pltpu.VMEM)
SMEM = pl.BlockSpec(memory_space=pltpu.SMEM)
ANY = pl.BlockSpec(memory_space=pl.ANY)


def up_to(n, step=LANES):
    return -(-n // step) * step


def params(mib=16):
    return pltpu.CompilerParams(vmem_limit_bytes=mib * 2**20)


def hint(flops, bytes_accessed, scale=0.3):
    return pl.CostEstimate(int(flops * scale), 0, int(bytes_accessed * scale))


def shape(dims, dtype):
    return jax.ShapeDtypeStruct(dims, dtype)


def prep_kernel(tallies, x, gain, routes, out, ends):
    block, tokens = x.shape
    v = x[...]
    wide = up_to(block)
    g = jnp.concatenate([gain[...], jnp.zeros((1, wide - block), f32)], axis=1)
    g = jnp.broadcast_to(g, (LANES, wide)).T[0:block, 0:1]
    out[0:block] = (v * g).astype(bf16)
    sq = jnp.sum(v * v, axis=0, keepdims=True)
    hi = sq.astype(bf16).astype(f32)
    mid = (sq - hi).astype(bf16).astype(f32)
    here = lax.broadcasted_iota(jnp.int32, (1, tokens), 1)
    mark, end = jnp.zeros((1, tokens), f32), jnp.int32(-1)
    for q in range(ends.shape[0]):
        end = end + tallies[0, q]
        mark = jnp.where(here == end, q + 1.0, mark)
    rows = [routes[...].astype(f32), hi, mid, sq - hi - mid, mark]
    rows.append(jnp.zeros((META - 6, tokens), f32))
    out[block:] = jnp.concatenate(rows, axis=0).astype(bf16)
    ends[...] = columns_at(mark, v)[0 : ends.shape[0]]


def columns_at(mark, v):
    row = lax.broadcasted_iota(jnp.int32, (8, mark.shape[1]), 0)
    pick = jnp.where(mark == (row + 1).astype(f32), 1.0, 0.0)
    return lax.dot_general(
        pick, v, (((1,), (1,)), ((), ())), precision=lax.Precision.HIGHEST, preferred_element_type=f32
    )


def whole_spec(v):
    return pl.BlockSpec(v.shape, lambda *_: (0,) * len(v.shape))


def prep_call(x, gain, routes, tallies):
    block, tokens = x.shape
    reqs = tallies.shape[1]
    outs = [shape((block + META, tokens), bf16), shape((reqs, block), f32)]
    return pl.pallas_call(
        prep_kernel,
        grid=(1,),
        in_specs=[SMEM] + [whole_spec(v) for v in (x, gain, routes)],
        out_specs=[whole_spec(v) for v in outs],
        out_shape=outs,
        compiler_params=params(60),
        cost_estimate=hint(4 * tokens * block, 6 * tokens * block),
        name="prep",
    )(tallies, x, gain, routes)


def join_call(blocks):
    rows, tokens = blocks[0].shape

    def join_kernel(*refs):
        for i, ref in enumerate(refs[:-1]):
            refs[-1][i * rows : (i + 1) * rows] = ref[...]

    return pl.pallas_call(
        join_kernel,
        in_specs=[VMEM] * len(blocks),
        out_specs=VMEM,
        out_shape=shape((len(blocks) * rows, tokens), bf16),
        compiler_params=params(),
        cost_estimate=hint(1, 4 * len(blocks) * rows * tokens),
        name="join",
    )(*blocks)


EXTRA = 5


def spread_lanes(v, base):
    lane = lax.broadcasted_iota(jnp.int32, v.shape, 1)
    hi = v.astype(bf16).astype(f32)
    return jnp.where(lane < base, v, jnp.where(lane < base + EXTRA, hi, v - hi)).astype(bf16)


def joined_lanes(v, base):
    lane = lax.broadcasted_iota(jnp.int32, v.shape, 1)
    left, right = pltpu.roll(v, LANES - EXTRA, 1), pltpu.roll(v, EXTRA, 1)
    return v + jnp.where(lane < base, 0.0, jnp.where(lane < base + EXTRA, left, right))


def slot_columns(core, cols):
    first, second = cols[:, 0:1].astype(f32), cols[:, 1:2].astype(f32)
    zero = core == 0
    return jnp.where(zero, first, second), jnp.where(zero, second, first)


def partial_kernel(sides, held, scal, *refs):
    feeds, (wr, wg, wu) = refs[:held], refs[held : held + 3]
    own, give, cols, xs, xt, acc, extra = refs[-7:]
    e = pl.program_id(0)
    core, side = scal[0], scal[1]
    depth, hidden = wg.shape[1:]
    deep, half = up_to(depth), up_to(hidden)
    base = hidden % LANES
    tokens = feeds[0].shape[1]
    block = depth // sides
    last = slice(2 * half - LANES, 2 * half)

    @pl.when(e == 0)
    def _():
        xs[depth:] = jnp.zeros((deep + LANES - depth, xs.shape[1]), bf16)
        for n, ref in enumerate(feeds):
            to = slice(n * tokens, (n + 1) * tokens)
            for i in range(sides):
                at = i * (block + META)
                xs[pl.ds(pl.multiple_of((side ^ i) * block, 16), block), to] = ref[at : at + block]
                xs[deep + i * META : deep + (i + 1) * META, to] = ref[at + block : at + block + META]
        xt[...] = xs[...].T
        more = xt[:, deep:]
        cols[...] = more
        more = more.astype(f32)
        sq = jnp.zeros((more.shape[0], 1), f32)
        for i in range(sides):
            for term in (4, 3, 2):
                sq = sq + more[:, i * META + term : i * META + term + 1]
        router = lax.dot_general(
            xt[:, 0:depth], wr[...], (((1,), (1,)), ((), ())), preferred_element_type=f32
        )
        lane = lax.broadcasted_iota(jnp.int32, router.shape, 1)
        extra[...] = router + jnp.where((lane == base) | (lane == base + EXTRA), sq, 0.0)
        for ref in (own, acc):
            ref[:, half - LANES : half] = jnp.zeros((xt.shape[0], LANES), f32)
            ref[:, last] = jnp.zeros((xt.shape[0], LANES), f32)

    mine, other = slot_columns(core, xt[:, deep : deep + LANES])
    ef = e.astype(f32)
    take = [(v == ef) | (e == 0) for v in (mine, other)]
    for which, w in enumerate((wg, wu)):
        for at in range(0, hidden, 256):
            end = min(hidden, at + 256)
            d = jnp.dot(xt[:, 0:depth], w[0, :, at:end], preferred_element_type=f32)
            to = slice(which * half + at, which * half + end)
            for ref, pick in ((own, take[0]), (acc, take[1])):
                ref[:, to] = jnp.where(pick, d, ref[:, to])

    @pl.when(e == pl.num_programs(0) - 1)
    def _():
        lane = lax.broadcasted_iota(jnp.int32, extra.shape, 1)
        more = extra[...]
        own[:, last] = jnp.where(lane < base, own[:, last], more)
        give[:, 0 : last.start] = acc[:, 0 : last.start].astype(bf16)
        give[:, last] = spread_lanes(jnp.where(lane < base, acc[:, last], more), base)


def partial_call(scal, sides, feeds, wr, wg, wu, deps):
    experts, depth, hidden = wg.shape
    tokens = feeds[0].shape[1] * len(feeds)
    deep, wide = up_to(depth), 2 * up_to(hidden)
    part = pl.BlockSpec((1, depth, hidden), lambda n: (n, 0, 0))
    outs = [shape((tokens, wide), f32), shape((tokens, wide), bf16), shape((tokens, LANES), bf16)]
    return pl.pallas_call(
        lambda *refs: partial_kernel(sides, len(feeds), *refs),
        grid=(experts,),
        in_specs=[SMEM] + [whole_spec(v) for v in feeds] + [whole_spec(wr), part, part] + [ANY] * len(deps),
        out_specs=[whole_spec(v) for v in outs],
        out_shape=outs,
        scratch_shapes=[
            pltpu.VMEM((deep + LANES, tokens), bf16),
            pltpu.VMEM((tokens, deep + LANES), bf16),
            pltpu.VMEM((tokens, wide), f32),
            pltpu.VMEM((tokens, LANES), f32),
        ],
        compiler_params=params(20),
        cost_estimate=hint(
            4 * experts * depth * hidden * tokens, 4 * experts * depth * hidden + 6 * tokens * wide, 4
        ),
        name="gate_up_partial",
    )(scal, *feeds, wr, wg, wu, *deps)


def sum_kernel(base, scal, own, recv, *refs):
    keep, send = refs[-2:]
    y = scal[2]
    th, wide = keep.shape
    main = wide - LANES
    for to, first in ((keep, y), (send, 1 - y)):
        rows = pl.ds(pl.multiple_of(first * th, th), th)
        to[:, 0:main] = (own[rows, 0:main] + recv[rows, 0:main].astype(f32)).astype(to.dtype)
        v = own[rows, main:] + joined_lanes(recv[rows, main:].astype(f32), base)
        to[:, main:] = v if to is keep else spread_lanes(v, base)


def sum_call(scal, base, own, recv, deps):
    tokens, wide = own.shape
    return pl.pallas_call(
        lambda *refs: sum_kernel(base, *refs),
        in_specs=[SMEM, VMEM, VMEM] + [ANY] * len(deps),
        out_specs=[VMEM, VMEM],
        out_shape=[shape((tokens // 2, wide), f32), shape((tokens // 2, wide), bf16)],
        compiler_params=params(),
        cost_estimate=hint(tokens * wide, 9 * tokens * wide),
        name="core_sum",
    )(scal, own, recv, *deps)


def act_kernel(base, scal, keep, recv, cols, *refs):
    act = refs[-1]
    core, y = scal[0], scal[2]
    th, half = act.shape
    main = 2 * half - LANES
    m = keep[:, main:] + joined_lanes(recv[:, main:].astype(f32), base)
    mine, other = slot_columns(core, cols[pl.ds(pl.multiple_of(y * th, th), th)])
    scale = lax.rsqrt(m[:, base : base + 1] / WIDTH + epsilon)
    la = lb = jnp.zeros_like(scale)
    for e in range(4):
        logit = m[:, base + 1 + e : base + 2 + e] * scale
        la = jnp.where(mine == e, logit, la)
        lb = jnp.where(other == e, logit, lb)
    mix = scale / (1.0 + jnp.exp(lb - la))
    g = (keep[:, 0:half] + recv[:, 0:half].astype(f32)) * scale
    u = (keep[:, half:] + recv[:, half:].astype(f32)) * mix
    act[...] = (g / (1.0 + jnp.exp(-g)) * u).astype(bf16)


def act_call(scal, base, keep, recv, cols, deps):
    th, wide = keep.shape
    return pl.pallas_call(
        lambda *refs: act_kernel(base, *refs),
        in_specs=[SMEM] + [VMEM] * 3 + [ANY] * len(deps),
        out_specs=VMEM,
        out_shape=shape((th, wide // 2), bf16),
        compiler_params=params(),
        cost_estimate=hint(6 * th * wide, 7 * th * wide),
        name="act",
    )(scal, keep, recv, cols, *deps)


def down_kernel(sides, scal, a, a_y, b, b_y, cols, wd, *refs):
    outs = refs[-sides - 2 : -2]
    whole, acc = refs[-2:]
    e = pl.program_id(0)
    core, side, y = scal[0], scal[1], scal[2]
    th = a.shape[0]
    width, hidden = wd.shape[1:]
    block = width // sides

    @pl.when(e == 0)
    def _():
        for k, near, far in ((0, a, a_y), (1, b, b_y)):
            whole[k, pl.ds(pl.multiple_of(y * th, th), th)] = near[...]
            whole[k, pl.ds(pl.multiple_of((1 - y) * th, th), th)] = far[...]

    ef = e.astype(f32)
    masks = [jnp.where(v == ef, 1.0, 0.0).astype(bf16) for v in slot_columns(core, cols[...])]
    rows = whole[0, :, 0:hidden] * masks[0] + whole[1, :, 0:hidden] * masks[1]
    d = lax.dot_general(wd[0], rows, (((1,), (1,)), ((), ())), preferred_element_type=f32)

    @pl.when(e == 0)
    def _():
        acc[...] = d

    @pl.when(e > 0)
    def _():
        acc[...] += d

    @pl.when(e == pl.num_programs(0) - 1)
    def _():
        for i in range(sides):
            rows = pl.ds(pl.multiple_of((side ^ i) * block, 16), block)
            outs[i][...] = acc[rows].astype(bf16)


def down_call(scal, sides, pieces, cols, wd, deps):
    experts, width, hidden = wd.shape
    tokens = cols.shape[0]
    outs = [shape((width // sides, tokens), bf16)] * sides
    return pl.pallas_call(
        lambda *refs: down_kernel(sides, *refs),
        grid=(experts,),
        in_specs=[SMEM]
        + [whole_spec(v) for v in pieces]
        + [whole_spec(cols), pl.BlockSpec((1, width, hidden), lambda n: (n, 0, 0))]
        + [ANY] * len(deps),
        out_specs=[whole_spec(v) for v in outs],
        out_shape=outs,
        scratch_shapes=[
            pltpu.VMEM((2, tokens, pieces[0].shape[1]), bf16),
            pltpu.VMEM((width, tokens), f32),
        ],
        compiler_params=params(20),
        cost_estimate=hint(
            2 * experts * width * hidden * tokens, 2 * experts * width * hidden + 2 * width * tokens, 4
        ),
        name="down",
    )(scal, *pieces, cols, wd, *deps)


def ends_kernel(sides, cols, stream, *refs):
    outs, backs, message = refs[:sides], refs[sides : sides + 3], refs[sides + 3]
    reqs = stream.shape[0]
    mark = cols[...].astype(f32).T[5:6]
    for i, ref in enumerate(outs):
        v = ref[...].astype(f32)
        if i == 0:
            for back in backs:
                v = v + back[...].astype(f32)
        ends = branch_scale * columns_at(mark, v)[0:reqs]
        if i == 0:
            ends = ends + stream[...]
        message[:, i * reqs : (i + 1) * reqs] = jnp.broadcast_to(ends[None], (message.shape[0], *ends.shape))


def ends_call(cols, stream, outs, backs, count):
    reqs, block = stream.shape
    args = (cols, stream, *outs, *backs)
    out = shape((count, len(outs) * reqs, block), f32)
    return pl.pallas_call(
        lambda *refs: ends_kernel(len(outs), *refs),
        grid=(1,),
        in_specs=[whole_spec(v) for v in args],
        out_specs=whole_spec(out),
        out_shape=out,
        compiler_params=params(),
        cost_estimate=hint(16 * block * cols.shape[0], 14 * block * cols.shape[0]),
        name="end_rows",
    )(*args)


def gather_kernel(sides, got, message):
    reqs = got.shape[1] // sides
    for i in range(sides):
        for group in range(got.shape[0] // sides):
            v = 0.0
            for x in range(sides):
                at = (x ^ i) * reqs
                v = v + got[group * sides + x, at : at + reqs]
            at = (i * (got.shape[0] // sides) + group) * reqs
            message[:, at : at + reqs] = jnp.broadcast_to(v[None], (message.shape[0], *v.shape))


def gather_call(sides, got, copies):
    out = shape((copies, got.shape[0] * got.shape[1] // sides, got.shape[2]), f32)
    return pl.pallas_call(
        lambda *refs: gather_kernel(sides, *refs),
        in_specs=[VMEM],
        out_specs=VMEM,
        out_shape=out,
        compiler_params=params(),
        cost_estimate=hint(got.size, 8 * got.size),
        name="end_rows_whole",
    )(got)


def head_kernel(order, got, gain, words, softness, logits, message, wide):
    blocks, block = gain.shape
    rows, columns = logits.shape
    ends, squares = [], 0.0
    reqs = rows // len(order[0])
    for b in range(blocks):
        v = jnp.concatenate([got[at, row : row + reqs] for at, row in order[b]], axis=0)
        squares = squares + jnp.sum(v * v, axis=1, keepdims=True)
        ends.append(v)
    scale = lax.rsqrt(squares / WIDTH + epsilon)
    total = jnp.zeros((rows, columns), f32)
    for b in range(blocks):
        feed = (ends[b] * scale * gain[b : b + 1]).astype(bf16)
        total += jnp.dot(feed, words[b * block : (b + 1) * block], preferred_element_type=f32)
    total = total / (WIDTH / 256.0 * softness[...])
    logits[...] = total
    top = jnp.max(total, axis=1, keepdims=True)
    mass = jnp.sum(jnp.exp(total - top), axis=1, keepdims=True)
    wide[...] = jnp.zeros_like(wide)
    lane = lax.broadcasted_iota(jnp.int32, (rows, LANES), 1)
    wide[0:rows] = jnp.where(lane == 0, top, jnp.where(lane == 1, mass, 0.0))
    turned = wide[...].T
    message[...] = jnp.broadcast_to(turned[None, 0:2, 0:rows], message.shape)


def pairs_kernel(pairs, message):
    top, mass = pairs[:, 0], pairs[:, 1]
    largest = jnp.max(top, axis=0, keepdims=True)
    total = jnp.sum(mass * jnp.exp(top - largest), axis=0, keepdims=True)
    both = jnp.concatenate([largest, total], axis=0)
    message[...] = jnp.broadcast_to(both[None], message.shape)


def pairs_call(pairs, copies):
    return pl.pallas_call(
        pairs_kernel,
        in_specs=[VMEM],
        out_specs=VMEM,
        out_shape=shape((copies, *pairs.shape[1:]), f32),
        compiler_params=params(),
        cost_estimate=hint(pairs.size, 8 * pairs.size),
        name="pairs",
    )(pairs)


def head_call(order, got, gain, words, softness, copies):
    rows, columns = softness.shape[0], words.shape[1]
    return pl.pallas_call(
        lambda *refs: head_kernel(order, *refs),
        in_specs=[VMEM] * 4,
        out_specs=[VMEM, VMEM],
        out_shape=[shape((rows, columns), f32), shape((copies, 2, rows), f32)],
        scratch_shapes=[pltpu.VMEM((LANES, LANES), f32)],
        compiler_params=params(),
        cost_estimate=hint(2 * rows * WIDTH * columns, 2 * WIDTH * columns),
        name="head",
    )(got, gain, words, softness)


def body(
    skip_stream_arriving,
    chosen_specialists,
    sequence_piece_tallies,
    premix_rmsnorm_gain,
    dispatcher_weights,
    specialist_switch_weights,
    specialist_expand_weights,
    specialist_contract_weights,
    terminal_rmsnorm_gain,
    lexicon_projector_weights,
    softness_per_sequence,
):
    tokens, block = skip_stream_arriving.shape
    dp, mp = lax.axis_size("dp"), lax.axis_size("mp")
    parts = 4
    spread, sides = dp // parts, mp // parts
    assert dp == parts * spread and mp == parts * sides and sides & (sides - 1) == 0
    part = lax.axis_index("dp") // spread
    y, core = part // 2, part % 2
    side = lax.axis_index("mp") % sides

    def send(value, to):
        pairs = []
        for q in range(parts):
            for r in range(spread):
                for z in range(parts):
                    for x in range(sides):
                        q2, z2, x2 = to(q, z, x)
                        source = (q * spread + r) * mp + z * sides + x
                        pairs.append((source, (q2 * spread + r) * mp + z2 * sides + x2))
        return lax.ppermute(value, ("dp", "mp"), pairs)

    other_core = lambda q, z, x: (q ^ 1, z, x)
    other_y = lambda q, z, x: (q ^ 2, z, x)
    home = lambda q, z, x: (z, q, x)

    scal = jnp.stack([core, side, y]).astype(jnp.int32)
    sent, stream = prep_call(
        skip_stream_arriving.T, premix_rmsnorm_gain[None], chosen_specialists.T, sequence_piece_tallies
    )
    wg, wu, wd = specialist_switch_weights, specialist_expand_weights, specialist_contract_weights
    if spread > 1:
        runs = [[q * spread + r for r in range(spread)] for q in range(parts)]
        wg = lax.all_gather(wg, "dp", axis=1, tiled=True, axis_index_groups=runs)
        wu = lax.all_gather(wu, "dp", axis=1, tiled=True, axis_index_groups=runs)
        wd = lax.all_gather(wd, "dp", axis=2, tiled=True, axis_index_groups=runs)
    wd = jnp.swapaxes(wd, 1, 2)
    depth, hidden = wg.shape[1:]
    base = hidden % LANES
    wr = lax.dynamic_slice_in_dim(dispatcher_weights.T, part * depth, depth, axis=1)
    room = lambda at: jnp.pad(wr, ((at, LANES - at - wr.shape[0]), (0, 0)))
    wr = room(base + 1) + room(base + 1 + EXTRA)

    chunks = ((1,), (2,), (3,), (0,))
    first = [send(sent, lambda q, z, x, i=i: (z, (q - 1) % parts, x ^ i)) for i in range(sides)]
    pair = join_call(first)
    feeds = {1: pair}
    step = lambda v: send(v, lambda q, z, x: (q, (z - 1) % parts, x))
    stream = send(stream, home)
    reqs = sequence_piece_tallies.shape[1]
    partial, kept, pieces, shares, last = {}, {}, {}, {}, []

    def after(v, dep):
        return lax.optimization_barrier((v, dep))[0]

    def do_partial(s, *deps):
        own, give, cols = partial_call(scal, sides, [feeds[g] for g in chunks[s]], wr, wg, wu, deps)
        partial[s] = (own, send(give, other_core), cols)
        return own

    def do_sum(s, *deps):
        own, recv, _ = partial[s]
        keep, give = sum_call(scal, base, own, recv, deps)
        kept[s] = (keep, send(give, other_y))
        return keep

    def do_act(s, *deps):
        a = act_call(scal, base, *kept[s], partial[s][2], deps)
        pieces[s] = (a, send(a, other_y))
        return a

    def do_hop(s, dep):
        a, a_y = pieces[s]
        late = [v if dep is None else after(v, dep) for v in (a, a_y)]
        pieces[s] = (a, a_y, *[send(v, other_core) for v in late])

    def do_down(s, *deps):
        outs = down_call(scal, sides, pieces[s], partial[s][2], wd, deps)
        last[:] = outs
        got = [outs[0]] + [send(outs[i], lambda q, z, x, i=i: (q, z, x ^ i)) for i in range(1, sides)]
        for n, group in enumerate(chunks[s]):
            to = slice(n * tokens, (n + 1) * tokens)
            if group == 0:
                shares[0] = [v[:, to] for v in got]
            else:
                share = sum(v[:, to].astype(f32) for v in got).astype(bf16)
                back = lambda q, z, x, group=group: (q, (z + group) % parts, x)
                shares[group] = [send(share, back)]
        return outs[0]

    feeds[2] = step(feeds[1])
    feeds[3] = step(feeds[2])
    p0 = do_partial(0)
    p1 = do_partial(1, p0)
    s0 = do_sum(0, p1)
    p2 = do_partial(2, s0)
    feeds[0] = step(after(feeds[3], p2))
    s1 = do_sum(1, p2)
    a0 = do_act(0, s1)
    p3 = do_partial(3, a0)
    s2 = do_sum(2, p3)
    do_hop(0, s2)
    a1 = do_act(1, s2)
    d0 = do_down(0, a1)
    s3 = do_sum(3, d0)
    do_hop(1, s3)
    a2 = do_act(2, s3)
    d1 = do_down(1, a2)
    do_hop(2, None)
    a3 = do_act(3, d1)
    d2 = do_down(2, a3)
    do_hop(3, None)
    d3 = do_down(3, d2)
    backs = [shares[group][0] for group in range(1, parts)]
    exchange = lambda v, axis: lax.all_to_all(v, axis, 0, 0, tiled=True)
    message = ends_call(partial[parts - 1][2], stream, last, backs, mp)
    got, shares[0] = lax.optimization_barrier((exchange(message, "mp"), shares[0]))
    got = exchange(gather_call(sides, got, dp), "dp")
    total = sum(v.astype(f32) for v in shares[0] + backs)
    branch = send(total, home)
    order = [
        [(q * spread + r, (x * parts + group) * reqs) for group in range(parts) for r in range(spread)]
        for q in range(parts)
        for x in range(sides)
    ]
    logits, pairs = head_call(
        order,
        got,
        terminal_rmsnorm_gain.reshape(mp, block),
        lexicon_projector_weights,
        softness_per_sequence[:, None],
        mp,
    )
    pairs = exchange(pairs_call(exchange(pairs, "mp"), dp), "dp")
    new_hidden = skip_stream_arriving + branch_scale * branch.T
    largest = jnp.max(pairs[:, 0], axis=0)
    mass = jnp.sum(pairs[:, 1] * jnp.exp(pairs[:, 0] - largest), axis=0)
    logprobs = logits - largest[:, None] - jnp.log(mass)[:, None]
    return (new_hidden, logprobs)


def solution(mesh):
    return jax.shard_map(
        body,
        mesh=mesh,
        in_specs=(
            P("dp", "mp"),
            P("dp", None),
            P("dp", None),
            P("mp"),
            P(),
            P(None, "dp", "mp"),
            P(None, "dp", "mp"),
            P(None, "mp", "dp"),
            P(),
            P(None, ("dp", "mp")),
            P(),
        ),
        out_specs=(P("dp", "mp"), P(None, ("dp", "mp"))),
        check_vma=False,
    )
```

```python
import math

import jax
import jax.numpy as jnp
from jax import lax
from jax.experimental import pallas as pl
from jax.experimental.pallas import tpu as pltpu
from jax.sharding import PartitionSpec as P

WIDTH = 2304
META = 16
LANES = 128
branch_scale = 1.4 / math.sqrt(40.0)
epsilon = 1e-05
f32, bf16 = jnp.float32, jnp.bfloat16

VMEM = pl.BlockSpec(memory_space=pltpu.VMEM)
SMEM = pl.BlockSpec(memory_space=pltpu.SMEM)
ANY = pl.BlockSpec(memory_space=pl.ANY)


def up_to(n, step=LANES):
    return -(-n // step) * step


def params(mib=16):
    return pltpu.CompilerParams(vmem_limit_bytes=mib * 2**20)


def hint(flops, bytes_accessed, scale=0.3):
    return pl.CostEstimate(int(flops * scale), 0, int(bytes_accessed * scale))


def shape(dims, dtype):
    return jax.ShapeDtypeStruct(dims, dtype)


def prep_kernel(tallies, x, gain, routes, out, ends):
    block, tokens = x.shape
    v = x[...]
    wide = up_to(block)
    g = jnp.concatenate([gain[...], jnp.zeros((1, wide - block), f32)], axis=1)
    g = jnp.broadcast_to(g, (LANES, wide)).T[0:block, 0:1]
    out[0:block] = (v * g).astype(bf16)
    sq = jnp.sum(v * v, axis=0, keepdims=True)
    hi = sq.astype(bf16).astype(f32)
    mid = (sq - hi).astype(bf16).astype(f32)
    here = lax.broadcasted_iota(jnp.int32, (1, tokens), 1)
    mark, end = jnp.zeros((1, tokens), f32), jnp.int32(-1)
    for q in range(ends.shape[0]):
        end = end + tallies[0, q]
        mark = jnp.where(here == end, q + 1.0, mark)
    rows = [routes[...].astype(f32), hi, mid, sq - hi - mid, mark]
    rows.append(jnp.zeros((META - 6, tokens), f32))
    out[block:] = jnp.concatenate(rows, axis=0).astype(bf16)
    ends[...] = columns_at(mark, v)[0 : ends.shape[0]]


def columns_at(mark, v):
    row = lax.broadcasted_iota(jnp.int32, (8, mark.shape[1]), 0)
    pick = jnp.where(mark == (row + 1).astype(f32), 1.0, 0.0)
    return lax.dot_general(
        pick, v, (((1,), (1,)), ((), ())), precision=lax.Precision.HIGHEST, preferred_element_type=f32
    )


def whole_spec(v):
    return pl.BlockSpec(v.shape, lambda *_: (0,) * len(v.shape))


def prep_call(x, gain, routes, tallies):
    block, tokens = x.shape
    reqs = tallies.shape[1]
    outs = [shape((block + META, tokens), bf16), shape((reqs, block), f32)]
    return pl.pallas_call(
        prep_kernel,
        grid=(1,),
        in_specs=[SMEM] + [whole_spec(v) for v in (x, gain, routes)],
        out_specs=[whole_spec(v) for v in outs],
        out_shape=outs,
        compiler_params=params(60),
        cost_estimate=hint(4 * tokens * block, 6 * tokens * block),
        name="prep",
    )(tallies, x, gain, routes)


def join_call(blocks):
    rows, tokens = blocks[0].shape

    def join_kernel(*refs):
        for i, ref in enumerate(refs[:-1]):
            refs[-1][i * rows : (i + 1) * rows] = ref[...]

    return pl.pallas_call(
        join_kernel,
        in_specs=[VMEM] * len(blocks),
        out_specs=VMEM,
        out_shape=shape((len(blocks) * rows, tokens), bf16),
        compiler_params=params(),
        cost_estimate=hint(1, 4 * len(blocks) * rows * tokens),
        name="join",
    )(*blocks)


EXTRA = 5


def spread_lanes(v, base):
    lane = lax.broadcasted_iota(jnp.int32, v.shape, 1)
    hi = v.astype(bf16).astype(f32)
    return jnp.where(lane < base, v, jnp.where(lane < base + EXTRA, hi, v - hi)).astype(bf16)


def joined_lanes(v, base):
    lane = lax.broadcasted_iota(jnp.int32, v.shape, 1)
    left, right = pltpu.roll(v, LANES - EXTRA, 1), pltpu.roll(v, EXTRA, 1)
    return v + jnp.where(lane < base, 0.0, jnp.where(lane < base + EXTRA, left, right))


def slot_columns(core, cols):
    first, second = cols[:, 0:1].astype(f32), cols[:, 1:2].astype(f32)
    zero = core == 0
    return jnp.where(zero, first, second), jnp.where(zero, second, first)


def partial_kernel(sides, held, scal, *refs):
    feeds, (wr, wg, wu) = refs[:held], refs[held : held + 3]
    own, give, cols, xs, xt, acc, extra = refs[-7:]
    e = pl.program_id(0)
    core, side = scal[0], scal[1]
    depth, hidden = wg.shape[1:]
    deep, half = up_to(depth), up_to(hidden)
    base = hidden % LANES
    tokens = feeds[0].shape[1]
    block = depth // sides
    last = slice(2 * half - LANES, 2 * half)

    @pl.when(e == 0)
    def _():
        xs[depth:] = jnp.zeros((deep + LANES - depth, xs.shape[1]), bf16)
        for n, ref in enumerate(feeds):
            to = slice(n * tokens, (n + 1) * tokens)
            for i in range(sides):
                at = i * (block + META)
                xs[pl.ds(pl.multiple_of((side ^ i) * block, 16), block), to] = ref[at : at + block]
                xs[deep + i * META : deep + (i + 1) * META, to] = ref[at + block : at + block + META]
        xt[...] = xs[...].T
        more = xt[:, deep:]
        cols[...] = more
        more = more.astype(f32)
        sq = jnp.zeros((more.shape[0], 1), f32)
        for i in range(sides):
            for term in (4, 3, 2):
                sq = sq + more[:, i * META + term : i * META + term + 1]
        router = lax.dot_general(
            xt[:, 0:depth], wr[...], (((1,), (1,)), ((), ())), preferred_element_type=f32
        )
        lane = lax.broadcasted_iota(jnp.int32, router.shape, 1)
        extra[...] = router + jnp.where((lane == base) | (lane == base + EXTRA), sq, 0.0)
        for ref in (own, acc):
            ref[:, half - LANES : half] = jnp.zeros((xt.shape[0], LANES), f32)
            ref[:, last] = jnp.zeros((xt.shape[0], LANES), f32)

    mine, other = slot_columns(core, xt[:, deep : deep + LANES])
    ef = e.astype(f32)
    take = [(v == ef) | (e == 0) for v in (mine, other)]
    for which, w in enumerate((wg, wu)):
        for at in range(0, hidden, 256):
            end = min(hidden, at + 256)
            d = jnp.dot(xt[:, 0:depth], w[0, :, at:end], preferred_element_type=f32)
            to = slice(which * half + at, which * half + end)
            for ref, pick in ((own, take[0]), (acc, take[1])):
                ref[:, to] = jnp.where(pick, d, ref[:, to])

    @pl.when(e == pl.num_programs(0) - 1)
    def _():
        lane = lax.broadcasted_iota(jnp.int32, extra.shape, 1)
        more = extra[...]
        own[:, last] = jnp.where(lane < base, own[:, last], more)
        give[:, 0 : last.start] = acc[:, 0 : last.start].astype(bf16)
        give[:, last] = spread_lanes(jnp.where(lane < base, acc[:, last], more), base)


def partial_call(scal, sides, feeds, wr, wg, wu, deps):
    experts, depth, hidden = wg.shape
    tokens = feeds[0].shape[1] * len(feeds)
    deep, wide = up_to(depth), 2 * up_to(hidden)
    part = pl.BlockSpec((1, depth, hidden), lambda n: (n, 0, 0))
    outs = [shape((tokens, wide), f32), shape((tokens, wide), bf16), shape((tokens, LANES), bf16)]
    return pl.pallas_call(
        lambda *refs: partial_kernel(sides, len(feeds), *refs),
        grid=(experts,),
        in_specs=[SMEM] + [whole_spec(v) for v in feeds] + [whole_spec(wr), part, part] + [ANY] * len(deps),
        out_specs=[whole_spec(v) for v in outs],
        out_shape=outs,
        scratch_shapes=[
            pltpu.VMEM((deep + LANES, tokens), bf16),
            pltpu.VMEM((tokens, deep + LANES), bf16),
            pltpu.VMEM((tokens, wide), f32),
            pltpu.VMEM((tokens, LANES), f32),
        ],
        compiler_params=params(20),
        cost_estimate=hint(
            4 * experts * depth * hidden * tokens, 4 * experts * depth * hidden + 6 * tokens * wide, 4
        ),
        name="gate_up_partial",
    )(scal, *feeds, wr, wg, wu, *deps)


def sum_kernel(base, scal, own, recv, *refs):
    keep, send = refs[-2:]
    y = scal[2]
    th, wide = keep.shape
    main = wide - LANES
    for to, first in ((keep, y), (send, 1 - y)):
        rows = pl.ds(pl.multiple_of(first * th, th), th)
        to[:, 0:main] = (own[rows, 0:main] + recv[rows, 0:main].astype(f32)).astype(to.dtype)
        v = own[rows, main:] + joined_lanes(recv[rows, main:].astype(f32), base)
        to[:, main:] = v if to is keep else spread_lanes(v, base)


def sum_call(scal, base, own, recv, deps):
    tokens, wide = own.shape
    return pl.pallas_call(
        lambda *refs: sum_kernel(base, *refs),
        in_specs=[SMEM, VMEM, VMEM] + [ANY] * len(deps),
        out_specs=[VMEM, VMEM],
        out_shape=[shape((tokens // 2, wide), f32), shape((tokens // 2, wide), bf16)],
        compiler_params=params(),
        cost_estimate=hint(tokens * wide, 9 * tokens * wide),
        name="core_sum",
    )(scal, own, recv, *deps)


def act_kernel(base, scal, keep, recv, cols, *refs):
    act = refs[-1]
    core, y = scal[0], scal[2]
    th, half = act.shape
    main = 2 * half - LANES
    m = keep[:, main:] + joined_lanes(recv[:, main:].astype(f32), base)
    mine, other = slot_columns(core, cols[pl.ds(pl.multiple_of(y * th, th), th)])
    scale = lax.rsqrt(m[:, base : base + 1] / WIDTH + epsilon)
    la = lb = jnp.zeros_like(scale)
    for e in range(4):
        logit = m[:, base + 1 + e : base + 2 + e] * scale
        la = jnp.where(mine == e, logit, la)
        lb = jnp.where(other == e, logit, lb)
    mix = scale / (1.0 + jnp.exp(lb - la))
    g = (keep[:, 0:half] + recv[:, 0:half].astype(f32)) * scale
    u = (keep[:, half:] + recv[:, half:].astype(f32)) * mix
    act[...] = (g / (1.0 + jnp.exp(-g)) * u).astype(bf16)


def act_call(scal, base, keep, recv, cols, deps):
    th, wide = keep.shape
    return pl.pallas_call(
        lambda *refs: act_kernel(base, *refs),
        in_specs=[SMEM] + [VMEM] * 3 + [ANY] * len(deps),
        out_specs=VMEM,
        out_shape=shape((th, wide // 2), bf16),
        compiler_params=params(),
        cost_estimate=hint(6 * th * wide, 7 * th * wide),
        name="act",
    )(scal, keep, recv, cols, *deps)


def down_kernel(sides, scal, a, a_y, b, b_y, cols, wd, *refs):
    outs = refs[-sides - 2 : -2]
    whole, acc = refs[-2:]
    e = pl.program_id(0)
    core, side, y = scal[0], scal[1], scal[2]
    th = a.shape[0]
    width, hidden = wd.shape[1:]
    block = width // sides

    @pl.when(e == 0)
    def _():
        for k, near, far in ((0, a, a_y), (1, b, b_y)):
            whole[k, pl.ds(pl.multiple_of(y * th, th), th)] = near[...]
            whole[k, pl.ds(pl.multiple_of((1 - y) * th, th), th)] = far[...]

    ef = e.astype(f32)
    masks = [jnp.where(v == ef, 1.0, 0.0).astype(bf16) for v in slot_columns(core, cols[...])]
    rows = whole[0, :, 0:hidden] * masks[0] + whole[1, :, 0:hidden] * masks[1]
    d = lax.dot_general(wd[0], rows, (((1,), (1,)), ((), ())), preferred_element_type=f32)

    @pl.when(e == 0)
    def _():
        acc[...] = d

    @pl.when(e > 0)
    def _():
        acc[...] += d

    @pl.when(e == pl.num_programs(0) - 1)
    def _():
        for i in range(sides):
            rows = pl.ds(pl.multiple_of((side ^ i) * block, 16), block)
            outs[i][...] = acc[rows].astype(bf16)


def down_call(scal, sides, pieces, cols, wd, deps):
    experts, width, hidden = wd.shape
    tokens = cols.shape[0]
    outs = [shape((width // sides, tokens), bf16)] * sides
    return pl.pallas_call(
        lambda *refs: down_kernel(sides, *refs),
        grid=(experts,),
        in_specs=[SMEM]
        + [whole_spec(v) for v in pieces]
        + [whole_spec(cols), pl.BlockSpec((1, width, hidden), lambda n: (n, 0, 0))]
        + [ANY] * len(deps),
        out_specs=[whole_spec(v) for v in outs],
        out_shape=outs,
        scratch_shapes=[
            pltpu.VMEM((2, tokens, pieces[0].shape[1]), bf16),
            pltpu.VMEM((width, tokens), f32),
        ],
        compiler_params=params(20),
        cost_estimate=hint(
            2 * experts * width * hidden * tokens, 2 * experts * width * hidden + 2 * width * tokens, 4
        ),
        name="down",
    )(scal, *pieces, cols, wd, *deps)


def total_kernel(cols, stream, *refs):
    parts, (total, message) = refs[:-2], refs[-2:]
    v = parts[0][...].astype(f32)
    for ref in parts[1:]:
        v = v + ref[...].astype(f32)
    total[...] = v
    ends = columns_at(cols[...].astype(f32).T[5:6], v)[0 : stream.shape[0]]
    ends = stream[...] + branch_scale * ends
    message[...] = jnp.broadcast_to(ends[None], message.shape)


def total_call(cols, stream, parts, count):
    reqs, block = stream.shape
    tokens = cols.shape[0]
    outs = [shape((block, tokens), f32), shape((count, reqs, block), f32)]
    return pl.pallas_call(
        total_kernel,
        grid=(1,),
        in_specs=[whole_spec(v) for v in (cols, stream, *parts)],
        out_specs=[whole_spec(v) for v in outs],
        out_shape=outs,
        compiler_params=params(),
        cost_estimate=hint(16 * block * tokens, 14 * block * tokens),
        name="branch_total",
    )(cols, stream, *parts)


def head_kernel(order, got, gain, words, softness, logits, message, wide):
    blocks, block = gain.shape
    rows, columns = logits.shape
    ends, squares = [], 0.0
    for b in range(blocks):
        v = jnp.concatenate([got[at] for at in order[b]], axis=0)
        squares = squares + jnp.sum(v * v, axis=1, keepdims=True)
        ends.append(v)
    scale = lax.rsqrt(squares / WIDTH + epsilon)
    total = jnp.zeros((rows, columns), f32)
    for b in range(blocks):
        feed = (ends[b] * scale * gain[b : b + 1]).astype(bf16)
        total += jnp.dot(feed, words[b * block : (b + 1) * block], preferred_element_type=f32)
    total = total / (WIDTH / 256.0 * softness[...])
    logits[...] = total
    top = jnp.max(total, axis=1, keepdims=True)
    mass = jnp.sum(jnp.exp(total - top), axis=1, keepdims=True)
    wide[...] = jnp.zeros_like(wide)
    lane = lax.broadcasted_iota(jnp.int32, (rows, LANES), 1)
    wide[0:rows] = jnp.where(lane == 0, top, jnp.where(lane == 1, mass, 0.0))
    turned = wide[...].T
    message[...] = jnp.broadcast_to(turned[None, 0:2, 0:rows], message.shape)


def head_call(order, got, gain, words, softness):
    rows, columns = softness.shape[0], words.shape[1]
    return pl.pallas_call(
        lambda *refs: head_kernel(order, *refs),
        in_specs=[VMEM] * 4,
        out_specs=[VMEM, VMEM],
        out_shape=[shape((rows, columns), f32), shape((got.shape[0], 2, rows), f32)],
        scratch_shapes=[pltpu.VMEM((LANES, LANES), f32)],
        compiler_params=params(),
        cost_estimate=hint(2 * rows * WIDTH * columns, 2 * WIDTH * columns),
        name="head",
    )(got, gain, words, softness)


def body(
    skip_stream_arriving,
    chosen_specialists,
    sequence_piece_tallies,
    premix_rmsnorm_gain,
    dispatcher_weights,
    specialist_switch_weights,
    specialist_expand_weights,
    specialist_contract_weights,
    terminal_rmsnorm_gain,
    lexicon_projector_weights,
    softness_per_sequence,
):
    tokens, block = skip_stream_arriving.shape
    dp, mp = lax.axis_size("dp"), lax.axis_size("mp")
    parts = 4
    spread, sides = dp // parts, mp // parts
    assert dp == parts * spread and mp == parts * sides and sides & (sides - 1) == 0
    part = lax.axis_index("dp") // spread
    y, core = part // 2, part % 2
    side = lax.axis_index("mp") % sides

    def send(value, to):
        pairs = []
        for q in range(parts):
            for r in range(spread):
                for z in range(parts):
                    for x in range(sides):
                        q2, z2, x2 = to(q, z, x)
                        source = (q * spread + r) * mp + z * sides + x
                        pairs.append((source, (q2 * spread + r) * mp + z2 * sides + x2))
        return lax.ppermute(value, ("dp", "mp"), pairs)

    other_core = lambda q, z, x: (q ^ 1, z, x)
    other_y = lambda q, z, x: (q ^ 2, z, x)
    home = lambda q, z, x: (z, q, x)

    scal = jnp.stack([core, side, y]).astype(jnp.int32)
    sent, stream = prep_call(
        skip_stream_arriving.T, premix_rmsnorm_gain[None], chosen_specialists.T, sequence_piece_tallies
    )
    wg, wu, wd = specialist_switch_weights, specialist_expand_weights, specialist_contract_weights
    if spread > 1:
        runs = [[q * spread + r for r in range(spread)] for q in range(parts)]
        wg = lax.all_gather(wg, "dp", axis=1, tiled=True, axis_index_groups=runs)
        wu = lax.all_gather(wu, "dp", axis=1, tiled=True, axis_index_groups=runs)
        wd = lax.all_gather(wd, "dp", axis=2, tiled=True, axis_index_groups=runs)
    wd = jnp.swapaxes(wd, 1, 2)
    depth, hidden = wg.shape[1:]
    base = hidden % LANES
    wr = lax.dynamic_slice_in_dim(dispatcher_weights.T, part * depth, depth, axis=1)
    room = lambda at: jnp.pad(wr, ((at, LANES - at - wr.shape[0]), (0, 0)))
    wr = room(base + 1) + room(base + 1 + EXTRA)

    chunks = ((1,), (2,), (3,), (0,))
    first = [send(sent, lambda q, z, x, i=i: (z, (q - 1) % parts, x ^ i)) for i in range(sides)]
    pair = join_call(first)
    feeds = {1: pair}
    step = lambda v: send(v, lambda q, z, x: (q, (z - 1) % parts, x))
    stream = send(stream, home)
    partial, kept, pieces, shares = {}, {}, {}, {}

    def after(v, dep):
        return lax.optimization_barrier((v, dep))[0]

    def do_partial(s, *deps):
        own, give, cols = partial_call(scal, sides, [feeds[g] for g in chunks[s]], wr, wg, wu, deps)
        partial[s] = (own, send(give, other_core), cols)
        return own

    def do_sum(s, *deps):
        own, recv, _ = partial[s]
        keep, give = sum_call(scal, base, own, recv, deps)
        kept[s] = (keep, send(give, other_y))
        return keep

    def do_act(s, *deps):
        a = act_call(scal, base, *kept[s], partial[s][2], deps)
        pieces[s] = (a, send(a, other_y))
        return a

    def do_hop(s, dep):
        a, a_y = pieces[s]
        late = [v if dep is None else after(v, dep) for v in (a, a_y)]
        pieces[s] = (a, a_y, *[send(v, other_core) for v in late])

    def do_down(s, *deps):
        outs = down_call(scal, sides, pieces[s], partial[s][2], wd, deps)
        got = [outs[0]] + [send(outs[i], lambda q, z, x, i=i: (q, z, x ^ i)) for i in range(1, sides)]
        for n, group in enumerate(chunks[s]):
            to = slice(n * tokens, (n + 1) * tokens)
            if group == 0:
                shares[0] = [v[:, to] for v in got]
            else:
                share = sum(v[:, to].astype(f32) for v in got).astype(bf16)
                back = lambda q, z, x, group=group: (q, (z + group) % parts, x)
                shares[group] = [send(share, back)]
        return outs[0]

    feeds[2] = step(feeds[1])
    feeds[3] = step(feeds[2])
    p0 = do_partial(0)
    p1 = do_partial(1, p0)
    s0 = do_sum(0, p1)
    p2 = do_partial(2, s0)
    feeds[0] = step(after(feeds[3], p2))
    s1 = do_sum(1, p2)
    a0 = do_act(0, s1)
    p3 = do_partial(3, a0)
    s2 = do_sum(2, p3)
    do_hop(0, s2)
    a1 = do_act(1, s2)
    d0 = do_down(0, a1)
    s3 = do_sum(3, d0)
    do_hop(1, s3)
    a2 = do_act(2, s3)
    d1 = do_down(1, a2)
    do_hop(2, None)
    a3 = do_act(3, d1)
    d2 = do_down(2, a3)
    do_hop(3, None)
    d3 = do_down(3, d2)
    terms = [v for group in range(parts) for v in shares[group]]
    total, message = total_call(partial[parts - 1][2], stream, terms, dp * mp)
    exchange = lambda v: lax.all_to_all(v, ("dp", "mp"), 0, 0, tiled=True)
    got = exchange(message)
    branch = send(total, home)
    order = [
        [(q * spread + r) * mp + group * sides + x for group in range(parts) for r in range(spread)]
        for q in range(parts)
        for x in range(sides)
    ]
    logits, pairs = head_call(
        order,
        got,
        terminal_rmsnorm_gain.reshape(mp, block),
        lexicon_projector_weights,
        softness_per_sequence[:, None],
    )
    pairs = exchange(pairs)
    new_hidden = skip_stream_arriving + branch_scale * branch.T
    largest = jnp.max(pairs[:, 0], axis=0)
    mass = jnp.sum(pairs[:, 1] * jnp.exp(pairs[:, 0] - largest), axis=0)
    logprobs = logits - largest[:, None] - jnp.log(mass)[:, None]
    return (new_hidden, logprobs)


def solution(mesh):
    return jax.shard_map(
        body,
        mesh=mesh,
        in_specs=(
            P("dp", "mp"),
            P("dp", None),
            P("dp", None),
            P("mp"),
            P(),
            P(None, "dp", "mp"),
            P(None, "dp", "mp"),
            P(None, "mp", "dp"),
            P(),
            P(None, ("dp", "mp")),
            P(),
        ),
        out_specs=(P("dp", "mp"), P(None, ("dp", "mp"))),
        check_vma=False,
    )
```

```python
import math

import jax
import jax.numpy as jnp
from jax import lax
from jax.experimental import pallas as pl
from jax.experimental.pallas import tpu as pltpu
from jax.sharding import PartitionSpec as P

WIDTH = 2304
META = 16
LANES = 128
branch_scale = 1.4 / math.sqrt(40.0)
epsilon = 1e-05
f32, bf16 = jnp.float32, jnp.bfloat16

VMEM = pl.BlockSpec(memory_space=pltpu.VMEM)
SMEM = pl.BlockSpec(memory_space=pltpu.SMEM)
ANY = pl.BlockSpec(memory_space=pl.ANY)


def up_to(n, step=LANES):
    return -(-n // step) * step


def params(mib=16):
    return pltpu.CompilerParams(vmem_limit_bytes=mib * 2**20)


def hint(flops, bytes_accessed, scale=0.3):
    return pl.CostEstimate(int(flops * scale), 0, int(bytes_accessed * scale))


def shape(dims, dtype):
    return jax.ShapeDtypeStruct(dims, dtype)


def prep_kernel(tallies, x, gain, routes, out, ends):
    block, tokens = x.shape
    v = x[...]
    wide = up_to(block)
    g = jnp.concatenate([gain[...], jnp.zeros((1, wide - block), f32)], axis=1)
    g = jnp.broadcast_to(g, (LANES, wide)).T[0:block, 0:1]
    out[0:block] = (v * g).astype(bf16)
    sq = jnp.sum(v * v, axis=0, keepdims=True)
    hi = sq.astype(bf16).astype(f32)
    mid = (sq - hi).astype(bf16).astype(f32)
    here = lax.broadcasted_iota(jnp.int32, (1, tokens), 1)
    mark, end = jnp.zeros((1, tokens), f32), jnp.int32(-1)
    for q in range(ends.shape[0]):
        end = end + tallies[0, q]
        mark = jnp.where(here == end, q + 1.0, mark)
    rows = [routes[...].astype(f32), hi, mid, sq - hi - mid, mark]
    rows.append(jnp.zeros((META - 6, tokens), f32))
    out[block:] = jnp.concatenate(rows, axis=0).astype(bf16)
    ends[...] = columns_at(mark, v)[0 : ends.shape[0]]


def columns_at(mark, v):
    row = lax.broadcasted_iota(jnp.int32, (8, mark.shape[1]), 0)
    pick = jnp.where(mark == (row + 1).astype(f32), 1.0, 0.0)
    return lax.dot_general(
        pick, v, (((1,), (1,)), ((), ())), precision=lax.Precision.HIGHEST, preferred_element_type=f32
    )


def whole_spec(v):
    return pl.BlockSpec(v.shape, lambda *_: (0,) * len(v.shape))


def prep_call(x, gain, routes, tallies):
    block, tokens = x.shape
    reqs = tallies.shape[1]
    outs = [shape((block + META, tokens), bf16), shape((reqs, block), f32)]
    return pl.pallas_call(
        prep_kernel,
        grid=(1,),
        in_specs=[SMEM] + [whole_spec(v) for v in (x, gain, routes)],
        out_specs=[whole_spec(v) for v in outs],
        out_shape=outs,
        compiler_params=params(60),
        cost_estimate=hint(4 * tokens * block, 6 * tokens * block),
        name="prep",
    )(tallies, x, gain, routes)


def join_call(blocks):
    rows, tokens = blocks[0].shape

    def join_kernel(*refs):
        for i, ref in enumerate(refs[:-1]):
            refs[-1][i * rows : (i + 1) * rows] = ref[...]

    return pl.pallas_call(
        join_kernel,
        in_specs=[VMEM] * len(blocks),
        out_specs=VMEM,
        out_shape=shape((len(blocks) * rows, tokens), bf16),
        compiler_params=params(),
        cost_estimate=hint(1, 4 * len(blocks) * rows * tokens),
        name="join",
    )(*blocks)


EXTRA = 5


def spread_lanes(v, base):
    lane = lax.broadcasted_iota(jnp.int32, v.shape, 1)
    hi = v.astype(bf16).astype(f32)
    return jnp.where(lane < base, v, jnp.where(lane < base + EXTRA, hi, v - hi)).astype(bf16)


def joined_lanes(v, base):
    lane = lax.broadcasted_iota(jnp.int32, v.shape, 1)
    left, right = pltpu.roll(v, LANES - EXTRA, 1), pltpu.roll(v, EXTRA, 1)
    return v + jnp.where(lane < base, 0.0, jnp.where(lane < base + EXTRA, left, right))


def slot_columns(core, cols):
    first, second = cols[:, 0:1].astype(f32), cols[:, 1:2].astype(f32)
    zero = core == 0
    return jnp.where(zero, first, second), jnp.where(zero, second, first)


def partial_kernel(sides, held, scal, *refs):
    feeds, (wr, wg, wu) = refs[:held], refs[held : held + 3]
    own, give, cols, xs, xt, acc, extra = refs[-7:]
    e = pl.program_id(0)
    core, side = scal[0], scal[1]
    depth, hidden = wg.shape[1:]
    deep, half = up_to(depth), up_to(hidden)
    base = hidden % LANES
    tokens = feeds[0].shape[1]
    block = depth // sides
    last = slice(2 * half - LANES, 2 * half)

    @pl.when(e == 0)
    def _():
        xs[depth:] = jnp.zeros((deep + LANES - depth, xs.shape[1]), bf16)
        for n, ref in enumerate(feeds):
            to = slice(n * tokens, (n + 1) * tokens)
            for i in range(sides):
                at = i * (block + META)
                xs[pl.ds(pl.multiple_of((side ^ i) * block, 16), block), to] = ref[at : at + block]
                xs[deep + i * META : deep + (i + 1) * META, to] = ref[at + block : at + block + META]
        xt[...] = xs[...].T
        more = xt[:, deep:]
        cols[...] = more
        more = more.astype(f32)
        sq = jnp.zeros((more.shape[0], 1), f32)
        for i in range(sides):
            for term in (4, 3, 2):
                sq = sq + more[:, i * META + term : i * META + term + 1]
        router = lax.dot_general(
            xt[:, 0:depth], wr[...], (((1,), (1,)), ((), ())), preferred_element_type=f32
        )
        lane = lax.broadcasted_iota(jnp.int32, router.shape, 1)
        extra[...] = router + jnp.where((lane == base) | (lane == base + EXTRA), sq, 0.0)
        for ref in (own, acc):
            ref[:, half - LANES : half] = jnp.zeros((xt.shape[0], LANES), f32)
            ref[:, last] = jnp.zeros((xt.shape[0], LANES), f32)

    mine, other = slot_columns(core, xt[:, deep : deep + LANES])
    ef = e.astype(f32)
    take = [(v == ef) | (e == 0) for v in (mine, other)]
    for which, w in enumerate((wg, wu)):
        for at in range(0, hidden, 256):
            end = min(hidden, at + 256)
            d = jnp.dot(xt[:, 0:depth], w[0, :, at:end], preferred_element_type=f32)
            to = slice(which * half + at, which * half + end)
            for ref, pick in ((own, take[0]), (acc, take[1])):
                ref[:, to] = jnp.where(pick, d, ref[:, to])

    @pl.when(e == pl.num_programs(0) - 1)
    def _():
        lane = lax.broadcasted_iota(jnp.int32, extra.shape, 1)
        more = extra[...]
        own[:, last] = jnp.where(lane < base, own[:, last], more)
        give[:, 0 : last.start] = acc[:, 0 : last.start].astype(bf16)
        give[:, last] = spread_lanes(jnp.where(lane < base, acc[:, last], more), base)


def partial_call(scal, sides, feeds, wr, wg, wu, deps):
    experts, depth, hidden = wg.shape
    tokens = feeds[0].shape[1] * len(feeds)
    deep, wide = up_to(depth), 2 * up_to(hidden)
    part = pl.BlockSpec((1, depth, hidden), lambda n: (n, 0, 0))
    outs = [shape((tokens, wide), f32), shape((tokens, wide), bf16), shape((tokens, LANES), bf16)]
    return pl.pallas_call(
        lambda *refs: partial_kernel(sides, len(feeds), *refs),
        grid=(experts,),
        in_specs=[SMEM] + [whole_spec(v) for v in feeds] + [whole_spec(wr), part, part] + [ANY] * len(deps),
        out_specs=[whole_spec(v) for v in outs],
        out_shape=outs,
        scratch_shapes=[
            pltpu.VMEM((deep + LANES, tokens), bf16),
            pltpu.VMEM((tokens, deep + LANES), bf16),
            pltpu.VMEM((tokens, wide), f32),
            pltpu.VMEM((tokens, LANES), f32),
        ],
        compiler_params=params(20),
        cost_estimate=hint(
            4 * experts * depth * hidden * tokens, 4 * experts * depth * hidden + 6 * tokens * wide, 4
        ),
        name="gate_up_partial",
    )(scal, *feeds, wr, wg, wu, *deps)


def sum_kernel(base, scal, own, recv, *refs):
    keep, send = refs[-2:]
    y = scal[2]
    th, wide = keep.shape
    main = wide - LANES
    for to, first in ((keep, y), (send, 1 - y)):
        rows = pl.ds(pl.multiple_of(first * th, th), th)
        to[:, 0:main] = (own[rows, 0:main] + recv[rows, 0:main].astype(f32)).astype(to.dtype)
        v = own[rows, main:] + joined_lanes(recv[rows, main:].astype(f32), base)
        to[:, main:] = v if to is keep else spread_lanes(v, base)


def sum_call(scal, base, own, recv, deps):
    tokens, wide = own.shape
    return pl.pallas_call(
        lambda *refs: sum_kernel(base, *refs),
        in_specs=[SMEM, VMEM, VMEM] + [ANY] * len(deps),
        out_specs=[VMEM, VMEM],
        out_shape=[shape((tokens // 2, wide), f32), shape((tokens // 2, wide), bf16)],
        compiler_params=params(),
        cost_estimate=hint(tokens * wide, 9 * tokens * wide),
        name="core_sum",
    )(scal, own, recv, *deps)


def act_kernel(base, scal, keep, recv, cols, *refs):
    act = refs[-1]
    core, y = scal[0], scal[2]
    th, half = act.shape
    main = 2 * half - LANES
    m = keep[:, main:] + joined_lanes(recv[:, main:].astype(f32), base)
    mine, other = slot_columns(core, cols[pl.ds(pl.multiple_of(y * th, th), th)])
    scale = lax.rsqrt(m[:, base : base + 1] / WIDTH + epsilon)
    la = lb = jnp.zeros_like(scale)
    for e in range(4):
        logit = m[:, base + 1 + e : base + 2 + e] * scale
        la = jnp.where(mine == e, logit, la)
        lb = jnp.where(other == e, logit, lb)
    mix = scale / (1.0 + jnp.exp(lb - la))
    g = (keep[:, 0:half] + recv[:, 0:half].astype(f32)) * scale
    u = (keep[:, half:] + recv[:, half:].astype(f32)) * mix
    act[...] = (g / (1.0 + jnp.exp(-g)) * u).astype(bf16)


def act_call(scal, base, keep, recv, cols, deps):
    th, wide = keep.shape
    return pl.pallas_call(
        lambda *refs: act_kernel(base, *refs),
        in_specs=[SMEM] + [VMEM] * 3 + [ANY] * len(deps),
        out_specs=VMEM,
        out_shape=shape((th, wide // 2), bf16),
        compiler_params=params(),
        cost_estimate=hint(6 * th * wide, 7 * th * wide),
        name="act",
    )(scal, keep, recv, cols, *deps)


def down_kernel(sides, scal, a, a_y, b, b_y, cols, wd, *refs):
    outs = refs[-sides - 2 : -2]
    whole, acc = refs[-2:]
    e = pl.program_id(0)
    core, side, y = scal[0], scal[1], scal[2]
    th = a.shape[0]
    width, hidden = wd.shape[1:]
    block = width // sides

    @pl.when(e == 0)
    def _():
        for k, near, far in ((0, a, a_y), (1, b, b_y)):
            whole[k, pl.ds(pl.multiple_of(y * th, th), th)] = near[...]
            whole[k, pl.ds(pl.multiple_of((1 - y) * th, th), th)] = far[...]

    ef = e.astype(f32)
    masks = [jnp.where(v == ef, 1.0, 0.0).astype(bf16) for v in slot_columns(core, cols[...])]
    rows = whole[0, :, 0:hidden] * masks[0] + whole[1, :, 0:hidden] * masks[1]
    d = lax.dot_general(wd[0], rows, (((1,), (1,)), ((), ())), preferred_element_type=f32)

    @pl.when(e == 0)
    def _():
        acc[...] = d

    @pl.when(e > 0)
    def _():
        acc[...] += d

    @pl.when(e == pl.num_programs(0) - 1)
    def _():
        for i in range(sides):
            rows = pl.ds(pl.multiple_of((side ^ i) * block, 16), block)
            outs[i][...] = acc[rows].astype(bf16)


def down_call(scal, sides, pieces, cols, wd, deps):
    experts, width, hidden = wd.shape
    tokens = cols.shape[0]
    outs = [shape((width // sides, tokens), bf16)] * sides
    return pl.pallas_call(
        lambda *refs: down_kernel(sides, *refs),
        grid=(experts,),
        in_specs=[SMEM]
        + [whole_spec(v) for v in pieces]
        + [whole_spec(cols), pl.BlockSpec((1, width, hidden), lambda n: (n, 0, 0))]
        + [ANY] * len(deps),
        out_specs=[whole_spec(v) for v in outs],
        out_shape=outs,
        scratch_shapes=[
            pltpu.VMEM((2, tokens, pieces[0].shape[1]), bf16),
            pltpu.VMEM((width, tokens), f32),
        ],
        compiler_params=params(20),
        cost_estimate=hint(
            2 * experts * width * hidden * tokens, 2 * experts * width * hidden + 2 * width * tokens, 4
        ),
        name="down",
    )(scal, *pieces, cols, wd, *deps)


def total_kernel(cols, stream, *refs):
    parts, (total, message) = refs[:-2], refs[-2:]
    v = parts[0][...].astype(f32)
    for ref in parts[1:]:
        v = v + ref[...].astype(f32)
    total[...] = v.astype(bf16)
    ends = columns_at(cols[...].astype(f32).T[5:6], v)[0 : stream.shape[0]]
    ends = stream[...] + branch_scale * ends
    message[...] = jnp.broadcast_to(ends[None], message.shape)


def total_call(cols, stream, parts, count):
    reqs, block = stream.shape
    tokens = cols.shape[0]
    outs = [shape((block, tokens), bf16), shape((count, reqs, block), f32)]
    return pl.pallas_call(
        total_kernel,
        grid=(1,),
        in_specs=[whole_spec(v) for v in (cols, stream, *parts)],
        out_specs=[whole_spec(v) for v in outs],
        out_shape=outs,
        compiler_params=params(),
        cost_estimate=hint(16 * block * tokens, 14 * block * tokens),
        name="branch_total",
    )(cols, stream, *parts)


def head_kernel(order, got, gain, words, softness, logits, message, wide):
    blocks, block = gain.shape
    rows, columns = logits.shape
    ends, squares = [], 0.0
    for b in range(blocks):
        v = jnp.concatenate([got[at] for at in order[b]], axis=0)
        squares = squares + jnp.sum(v * v, axis=1, keepdims=True)
        ends.append(v)
    scale = lax.rsqrt(squares / WIDTH + epsilon)
    total = jnp.zeros((rows, columns), f32)
    for b in range(blocks):
        feed = (ends[b] * scale * gain[b : b + 1]).astype(bf16)
        total += jnp.dot(feed, words[b * block : (b + 1) * block], preferred_element_type=f32)
    total = total / (WIDTH / 256.0 * softness[...])
    logits[...] = total
    top = jnp.max(total, axis=1, keepdims=True)
    mass = jnp.sum(jnp.exp(total - top), axis=1, keepdims=True)
    wide[...] = jnp.zeros_like(wide)
    lane = lax.broadcasted_iota(jnp.int32, (rows, LANES), 1)
    wide[0:rows] = jnp.where(lane == 0, top, jnp.where(lane == 1, mass, 0.0))
    turned = wide[...].T
    message[...] = jnp.broadcast_to(turned[None, 0:2, 0:rows], message.shape)


def head_call(order, got, gain, words, softness):
    rows, columns = softness.shape[0], words.shape[1]
    return pl.pallas_call(
        lambda *refs: head_kernel(order, *refs),
        in_specs=[VMEM] * 4,
        out_specs=[VMEM, VMEM],
        out_shape=[shape((rows, columns), f32), shape((got.shape[0], 2, rows), f32)],
        scratch_shapes=[pltpu.VMEM((LANES, LANES), f32)],
        compiler_params=params(),
        cost_estimate=hint(2 * rows * WIDTH * columns, 2 * WIDTH * columns),
        name="head",
    )(got, gain, words, softness)


def body(
    skip_stream_arriving,
    chosen_specialists,
    sequence_piece_tallies,
    premix_rmsnorm_gain,
    dispatcher_weights,
    specialist_switch_weights,
    specialist_expand_weights,
    specialist_contract_weights,
    terminal_rmsnorm_gain,
    lexicon_projector_weights,
    softness_per_sequence,
):
    tokens, block = skip_stream_arriving.shape
    dp, mp = lax.axis_size("dp"), lax.axis_size("mp")
    parts = 4
    spread, sides = dp // parts, mp // parts
    assert dp == parts * spread and mp == parts * sides and sides & (sides - 1) == 0
    part = lax.axis_index("dp") // spread
    y, core = part // 2, part % 2
    side = lax.axis_index("mp") % sides

    def send(value, to):
        pairs = []
        for q in range(parts):
            for r in range(spread):
                for z in range(parts):
                    for x in range(sides):
                        q2, z2, x2 = to(q, z, x)
                        source = (q * spread + r) * mp + z * sides + x
                        pairs.append((source, (q2 * spread + r) * mp + z2 * sides + x2))
        return lax.ppermute(value, ("dp", "mp"), pairs)

    other_core = lambda q, z, x: (q ^ 1, z, x)
    other_y = lambda q, z, x: (q ^ 2, z, x)
    home = lambda q, z, x: (z, q, x)

    scal = jnp.stack([core, side, y]).astype(jnp.int32)
    sent, stream = prep_call(
        skip_stream_arriving.T, premix_rmsnorm_gain[None], chosen_specialists.T, sequence_piece_tallies
    )
    wg, wu, wd = specialist_switch_weights, specialist_expand_weights, specialist_contract_weights
    if spread > 1:
        runs = [[q * spread + r for r in range(spread)] for q in range(parts)]
        wg = lax.all_gather(wg, "dp", axis=1, tiled=True, axis_index_groups=runs)
        wu = lax.all_gather(wu, "dp", axis=1, tiled=True, axis_index_groups=runs)
        wd = lax.all_gather(wd, "dp", axis=2, tiled=True, axis_index_groups=runs)
    wd = jnp.swapaxes(wd, 1, 2)
    depth, hidden = wg.shape[1:]
    base = hidden % LANES
    wr = lax.dynamic_slice_in_dim(dispatcher_weights.T, part * depth, depth, axis=1)
    room = lambda at: jnp.pad(wr, ((at, LANES - at - wr.shape[0]), (0, 0)))
    wr = room(base + 1) + room(base + 1 + EXTRA)

    chunks = ((1,), (2,), (3,), (0,))
    first = [send(sent, lambda q, z, x, i=i: (z, (q - 1) % parts, x ^ i)) for i in range(sides)]
    pair = join_call(first)
    feeds = {1: pair}
    step = lambda v: send(v, lambda q, z, x: (q, (z - 1) % parts, x))
    stream = send(stream, home)
    partial, kept, pieces, shares = {}, {}, {}, {}

    def after(v, dep):
        return lax.optimization_barrier((v, dep))[0]

    def do_partial(s, *deps):
        own, give, cols = partial_call(scal, sides, [feeds[g] for g in chunks[s]], wr, wg, wu, deps)
        partial[s] = (own, send(give, other_core), cols)
        return own

    def do_sum(s, *deps):
        own, recv, _ = partial[s]
        keep, give = sum_call(scal, base, own, recv, deps)
        kept[s] = (keep, send(give, other_y))
        return keep

    def do_act(s, *deps):
        a = act_call(scal, base, *kept[s], partial[s][2], deps)
        pieces[s] = (a, send(a, other_y))
        return a

    def do_hop(s, dep):
        a, a_y = pieces[s]
        late = [v if dep is None else after(v, dep) for v in (a, a_y)]
        pieces[s] = (a, a_y, *[send(v, other_core) for v in late])

    def do_down(s, *deps):
        outs = down_call(scal, sides, pieces[s], partial[s][2], wd, deps)
        got = [outs[0]] + [send(outs[i], lambda q, z, x, i=i: (q, z, x ^ i)) for i in range(1, sides)]
        for n, group in enumerate(chunks[s]):
            to = slice(n * tokens, (n + 1) * tokens)
            if group == 0:
                shares[0] = [v[:, to] for v in got]
            else:
                share = sum(v[:, to].astype(f32) for v in got).astype(bf16)
                back = lambda q, z, x, group=group: (q, (z + group) % parts, x)
                shares[group] = [send(share, back)]
        return outs[0]

    feeds[2] = step(feeds[1])
    feeds[3] = step(feeds[2])
    feeds[2] = step(feeds[1])
    feeds[3] = step(feeds[2])
    p0 = do_partial(0)
    p1 = do_partial(1, p0)
    s0 = do_sum(0, p1)
    p2 = do_partial(2, s0)
    feeds[0] = step(after(feeds[3], p2))
    s1 = do_sum(1, p2)
    a0 = do_act(0, s1)
    p3 = do_partial(3, a0)
    s2 = do_sum(2, p3)
    a1 = do_act(1, s2)
    do_hop(0, a1)
    d0 = do_down(0, a1)
    s3 = do_sum(3, d0)
    a2 = do_act(2, s3)
    do_hop(1, a2)
    d1 = do_down(1, a2)
    do_hop(2, None)
    a3 = do_act(3, d1)
    d2 = do_down(2, a3)
    do_hop(3, None)
    d3 = do_down(3, d2)
    terms = [v for group in range(parts) for v in shares[group]]
    total, message = total_call(partial[parts - 1][2], stream, terms, dp * mp)
    exchange = lambda v: lax.all_to_all(v, ("dp", "mp"), 0, 0, tiled=True)
    got, branch = lax.optimization_barrier((exchange(message), send(total, home)))
    order = [
        [(q * spread + r) * mp + group * sides + x for group in range(parts) for r in range(spread)]
        for q in range(parts)
        for x in range(sides)
    ]
    logits, pairs = head_call(
        order,
        got,
        terminal_rmsnorm_gain.reshape(mp, block),
        lexicon_projector_weights,
        softness_per_sequence[:, None],
    )
    pairs = exchange(pairs)
    new_hidden = skip_stream_arriving + branch_scale * branch.T.astype(f32)
    largest = jnp.max(pairs[:, 0], axis=0)
    mass = jnp.sum(pairs[:, 1] * jnp.exp(pairs[:, 0] - largest), axis=0)
    logprobs = logits - largest[:, None] - jnp.log(mass)[:, None]
    return (new_hidden, logprobs)


def solution(mesh):
    return jax.shard_map(
        body,
        mesh=mesh,
        in_specs=(
            P("dp", "mp"),
            P("dp", None),
            P("dp", None),
            P("mp"),
            P(),
            P(None, "dp", "mp"),
            P(None, "dp", "mp"),
            P(None, "mp", "dp"),
            P(),
            P(None, ("dp", "mp")),
            P(),
        ),
        out_specs=(P("dp", "mp"), P(None, ("dp", "mp"))),
        check_vma=False,
    )
```

```python
import math

import jax
import jax.numpy as jnp
from jax import lax
from jax.experimental import pallas as pl
from jax.experimental.pallas import tpu as pltpu
from jax.sharding import PartitionSpec as P

WIDTH = 2304
META = 16
LANES = 128
branch_scale = 1.4 / math.sqrt(40.0)
epsilon = 1e-05
f32, bf16 = jnp.float32, jnp.bfloat16

VMEM = pl.BlockSpec(memory_space=pltpu.VMEM)
SMEM = pl.BlockSpec(memory_space=pltpu.SMEM)
ANY = pl.BlockSpec(memory_space=pl.ANY)


def up_to(n, step=LANES):
    return -(-n // step) * step


def params(mib=16):
    return pltpu.CompilerParams(vmem_limit_bytes=mib * 2**20)


def hint(flops, bytes_accessed, scale=0.3):
    return pl.CostEstimate(int(flops * scale), 0, int(bytes_accessed * scale))


def shape(dims, dtype):
    return jax.ShapeDtypeStruct(dims, dtype)


def prep_kernel(tallies, x, gain, routes, out, ends):
    block, tokens = x.shape
    v = x[...]
    wide = up_to(block)
    g = jnp.concatenate([gain[...], jnp.zeros((1, wide - block), f32)], axis=1)
    g = jnp.broadcast_to(g, (LANES, wide)).T[0:block, 0:1]
    out[0:block] = (v * g).astype(bf16)
    sq = jnp.sum(v * v, axis=0, keepdims=True)
    hi = sq.astype(bf16).astype(f32)
    mid = (sq - hi).astype(bf16).astype(f32)
    here = lax.broadcasted_iota(jnp.int32, (1, tokens), 1)
    mark, end = jnp.zeros((1, tokens), f32), jnp.int32(-1)
    for q in range(ends.shape[0]):
        end = end + tallies[0, q]
        mark = jnp.where(here == end, q + 1.0, mark)
    rows = [routes[...].astype(f32), hi, mid, sq - hi - mid, mark]
    rows.append(jnp.zeros((META - 6, tokens), f32))
    out[block:] = jnp.concatenate(rows, axis=0).astype(bf16)
    ends[...] = columns_at(mark, v)[0 : ends.shape[0]]


def columns_at(mark, v):
    row = lax.broadcasted_iota(jnp.int32, (8, mark.shape[1]), 0)
    pick = jnp.where(mark == (row + 1).astype(f32), 1.0, 0.0)
    return lax.dot_general(
        pick, v, (((1,), (1,)), ((), ())), precision=lax.Precision.HIGHEST, preferred_element_type=f32
    )


def whole_spec(v):
    return pl.BlockSpec(v.shape, lambda *_: (0,) * len(v.shape))


def prep_call(x, gain, routes, tallies):
    block, tokens = x.shape
    reqs = tallies.shape[1]
    outs = [shape((block + META, tokens), bf16), shape((reqs, block), f32)]
    return pl.pallas_call(
        prep_kernel,
        grid=(1,),
        in_specs=[SMEM] + [whole_spec(v) for v in (x, gain, routes)],
        out_specs=[whole_spec(v) for v in outs],
        out_shape=outs,
        compiler_params=params(60),
        cost_estimate=hint(4 * tokens * block, 6 * tokens * block),
        name="prep",
    )(tallies, x, gain, routes)


def join_call(blocks):
    rows, tokens = blocks[0].shape

    def join_kernel(*refs):
        for i, ref in enumerate(refs[:-1]):
            refs[-1][i * rows : (i + 1) * rows] = ref[...]

    return pl.pallas_call(
        join_kernel,
        in_specs=[VMEM] * len(blocks),
        out_specs=VMEM,
        out_shape=shape((len(blocks) * rows, tokens), bf16),
        compiler_params=params(),
        cost_estimate=hint(1, 4 * len(blocks) * rows * tokens),
        name="join",
    )(*blocks)


EXTRA = 5


def spread_lanes(v, base):
    lane = lax.broadcasted_iota(jnp.int32, v.shape, 1)
    hi = v.astype(bf16).astype(f32)
    return jnp.where(lane < base, v, jnp.where(lane < base + EXTRA, hi, v - hi)).astype(bf16)


def joined_lanes(v, base):
    lane = lax.broadcasted_iota(jnp.int32, v.shape, 1)
    left, right = pltpu.roll(v, LANES - EXTRA, 1), pltpu.roll(v, EXTRA, 1)
    return v + jnp.where(lane < base, 0.0, jnp.where(lane < base + EXTRA, left, right))


def slot_columns(core, cols):
    first, second = cols[:, 0:1].astype(f32), cols[:, 1:2].astype(f32)
    zero = core == 0
    return jnp.where(zero, first, second), jnp.where(zero, second, first)


def partial_kernel(sides, held, scal, *refs):
    feeds, (wr, wg, wu) = refs[:held], refs[held : held + 3]
    own, give, cols, xs, xt, acc, extra = refs[-7:]
    e = pl.program_id(0)
    core, side = scal[0], scal[1]
    depth, hidden = wg.shape[1:]
    deep, half = up_to(depth), up_to(hidden)
    base = hidden % LANES
    tokens = feeds[0].shape[1]
    block = depth // sides
    last = slice(2 * half - LANES, 2 * half)

    @pl.when(e == 0)
    def _():
        xs[depth:] = jnp.zeros((deep + LANES - depth, xs.shape[1]), bf16)
        for n, ref in enumerate(feeds):
            to = slice(n * tokens, (n + 1) * tokens)
            for i in range(sides):
                at = i * (block + META)
                xs[pl.ds(pl.multiple_of((side ^ i) * block, 16), block), to] = ref[at : at + block]
                xs[deep + i * META : deep + (i + 1) * META, to] = ref[at + block : at + block + META]
        xt[...] = xs[...].T
        more = xt[:, deep:]
        cols[...] = more
        more = more.astype(f32)
        sq = jnp.zeros((more.shape[0], 1), f32)
        for i in range(sides):
            for term in (4, 3, 2):
                sq = sq + more[:, i * META + term : i * META + term + 1]
        router = lax.dot_general(
            xt[:, 0:depth], wr[...], (((1,), (1,)), ((), ())), preferred_element_type=f32
        )
        lane = lax.broadcasted_iota(jnp.int32, router.shape, 1)
        extra[...] = router + jnp.where((lane == base) | (lane == base + EXTRA), sq, 0.0)
        for ref in (own, acc):
            ref[:, half - LANES : half] = jnp.zeros((xt.shape[0], LANES), f32)
            ref[:, last] = jnp.zeros((xt.shape[0], LANES), f32)

    mine, other = slot_columns(core, xt[:, deep : deep + LANES])
    ef = e.astype(f32)
    take = [(v == ef) | (e == 0) for v in (mine, other)]
    for which, w in enumerate((wg, wu)):
        for at in range(0, hidden, 256):
            end = min(hidden, at + 256)
            d = jnp.dot(xt[:, 0:depth], w[0, :, at:end], preferred_element_type=f32)
            to = slice(which * half + at, which * half + end)
            for ref, pick in ((own, take[0]), (acc, take[1])):
                ref[:, to] = jnp.where(pick, d, ref[:, to])

    @pl.when(e == pl.num_programs(0) - 1)
    def _():
        lane = lax.broadcasted_iota(jnp.int32, extra.shape, 1)
        more = extra[...]
        own[:, last] = jnp.where(lane < base, own[:, last], more)
        give[:, 0 : last.start] = acc[:, 0 : last.start].astype(bf16)
        give[:, last] = spread_lanes(jnp.where(lane < base, acc[:, last], more), base)


def partial_call(scal, sides, feeds, wr, wg, wu, deps):
    experts, depth, hidden = wg.shape
    tokens = feeds[0].shape[1] * len(feeds)
    deep, wide = up_to(depth), 2 * up_to(hidden)
    part = pl.BlockSpec((1, depth, hidden), lambda n: (n, 0, 0))
    outs = [shape((tokens, wide), f32), shape((tokens, wide), bf16), shape((tokens, LANES), bf16)]
    return pl.pallas_call(
        lambda *refs: partial_kernel(sides, len(feeds), *refs),
        grid=(experts,),
        in_specs=[SMEM] + [whole_spec(v) for v in feeds] + [whole_spec(wr), part, part] + [ANY] * len(deps),
        out_specs=[whole_spec(v) for v in outs],
        out_shape=outs,
        scratch_shapes=[
            pltpu.VMEM((deep + LANES, tokens), bf16),
            pltpu.VMEM((tokens, deep + LANES), bf16),
            pltpu.VMEM((tokens, wide), f32),
            pltpu.VMEM((tokens, LANES), f32),
        ],
        compiler_params=params(20),
        cost_estimate=hint(
            4 * experts * depth * hidden * tokens, 4 * experts * depth * hidden + 6 * tokens * wide, 4
        ),
        name="gate_up_partial",
    )(scal, *feeds, wr, wg, wu, *deps)


def sum_kernel(base, scal, own, recv, *refs):
    keep, send = refs[-2:]
    y = scal[2]
    th, wide = keep.shape
    main = wide - LANES
    for to, first in ((keep, y), (send, 1 - y)):
        rows = pl.ds(pl.multiple_of(first * th, th), th)
        to[:, 0:main] = (own[rows, 0:main] + recv[rows, 0:main].astype(f32)).astype(to.dtype)
        v = own[rows, main:] + joined_lanes(recv[rows, main:].astype(f32), base)
        to[:, main:] = v if to is keep else spread_lanes(v, base)


def sum_call(scal, base, own, recv, deps):
    tokens, wide = own.shape
    return pl.pallas_call(
        lambda *refs: sum_kernel(base, *refs),
        in_specs=[SMEM, VMEM, VMEM] + [ANY] * len(deps),
        out_specs=[VMEM, VMEM],
        out_shape=[shape((tokens // 2, wide), f32), shape((tokens // 2, wide), bf16)],
        compiler_params=params(),
        cost_estimate=hint(tokens * wide, 9 * tokens * wide),
        name="core_sum",
    )(scal, own, recv, *deps)


def act_kernel(base, scal, keep, recv, cols, *refs):
    act = refs[-1]
    core, y = scal[0], scal[2]
    th, half = act.shape
    main = 2 * half - LANES
    m = keep[:, main:] + joined_lanes(recv[:, main:].astype(f32), base)
    mine, other = slot_columns(core, cols[pl.ds(pl.multiple_of(y * th, th), th)])
    scale = lax.rsqrt(m[:, base : base + 1] / WIDTH + epsilon)
    la = lb = jnp.zeros_like(scale)
    for e in range(4):
        logit = m[:, base + 1 + e : base + 2 + e] * scale
        la = jnp.where(mine == e, logit, la)
        lb = jnp.where(other == e, logit, lb)
    mix = scale / (1.0 + jnp.exp(lb - la))
    g = (keep[:, 0:half] + recv[:, 0:half].astype(f32)) * scale
    u = (keep[:, half:] + recv[:, half:].astype(f32)) * mix
    act[...] = (g / (1.0 + jnp.exp(-g)) * u).astype(bf16)


def act_call(scal, base, keep, recv, cols, deps):
    th, wide = keep.shape
    return pl.pallas_call(
        lambda *refs: act_kernel(base, *refs),
        in_specs=[SMEM] + [VMEM] * 3 + [ANY] * len(deps),
        out_specs=VMEM,
        out_shape=shape((th, wide // 2), bf16),
        compiler_params=params(),
        cost_estimate=hint(6 * th * wide, 7 * th * wide),
        name="act",
    )(scal, keep, recv, cols, *deps)


def down_kernel(sides, scal, a, a_y, b, b_y, cols, wd, *refs):
    outs = refs[-sides - 2 : -2]
    whole, acc = refs[-2:]
    e = pl.program_id(0)
    core, side, y = scal[0], scal[1], scal[2]
    th = a.shape[0]
    width, hidden = wd.shape[1:]
    block = width // sides

    @pl.when(e == 0)
    def _():
        for k, near, far in ((0, a, a_y), (1, b, b_y)):
            whole[k, pl.ds(pl.multiple_of(y * th, th), th)] = near[...]
            whole[k, pl.ds(pl.multiple_of((1 - y) * th, th), th)] = far[...]

    ef = e.astype(f32)
    masks = [jnp.where(v == ef, 1.0, 0.0).astype(bf16) for v in slot_columns(core, cols[...])]
    rows = whole[0, :, 0:hidden] * masks[0] + whole[1, :, 0:hidden] * masks[1]
    d = lax.dot_general(wd[0], rows, (((1,), (1,)), ((), ())), preferred_element_type=f32)

    @pl.when(e == 0)
    def _():
        acc[...] = d

    @pl.when(e > 0)
    def _():
        acc[...] += d

    @pl.when(e == pl.num_programs(0) - 1)
    def _():
        for i in range(sides):
            rows = pl.ds(pl.multiple_of((side ^ i) * block, 16), block)
            outs[i][...] = acc[rows].astype(bf16)


def down_call(scal, sides, pieces, cols, wd, deps):
    experts, width, hidden = wd.shape
    tokens = cols.shape[0]
    outs = [shape((width // sides, tokens), bf16)] * sides
    return pl.pallas_call(
        lambda *refs: down_kernel(sides, *refs),
        grid=(experts,),
        in_specs=[SMEM]
        + [whole_spec(v) for v in pieces]
        + [whole_spec(cols), pl.BlockSpec((1, width, hidden), lambda n: (n, 0, 0))]
        + [ANY] * len(deps),
        out_specs=[whole_spec(v) for v in outs],
        out_shape=outs,
        scratch_shapes=[
            pltpu.VMEM((2, tokens, pieces[0].shape[1]), bf16),
            pltpu.VMEM((width, tokens), f32),
        ],
        compiler_params=params(20),
        cost_estimate=hint(
            2 * experts * width * hidden * tokens, 2 * experts * width * hidden + 2 * width * tokens, 4
        ),
        name="down",
    )(scal, *pieces, cols, wd, *deps)


def total_kernel(cols, stream, *refs):
    parts, (total, message) = refs[:-2], refs[-2:]
    v = parts[0][...].astype(f32)
    for ref in parts[1:]:
        v = v + ref[...].astype(f32)
    total[...] = v.astype(bf16)
    ends = columns_at(cols[...].astype(f32).T[5:6], v)[0 : stream.shape[0]]
    ends = stream[...] + branch_scale * ends
    message[...] = jnp.broadcast_to(ends[None], message.shape)


def total_call(cols, stream, parts, count):
    reqs, block = stream.shape
    tokens = cols.shape[0]
    outs = [shape((block, tokens), bf16), shape((count, reqs, block), f32)]
    return pl.pallas_call(
        total_kernel,
        grid=(1,),
        in_specs=[whole_spec(v) for v in (cols, stream, *parts)],
        out_specs=[whole_spec(v) for v in outs],
        out_shape=outs,
        compiler_params=params(),
        cost_estimate=hint(16 * block * tokens, 14 * block * tokens),
        name="branch_total",
    )(cols, stream, *parts)


def head_kernel(order, got, gain, words, softness, logits, message, wide):
    blocks, block = gain.shape
    rows, columns = logits.shape
    ends, squares = [], 0.0
    for b in range(blocks):
        v = jnp.concatenate([got[at] for at in order[b]], axis=0)
        squares = squares + jnp.sum(v * v, axis=1, keepdims=True)
        ends.append(v)
    scale = lax.rsqrt(squares / WIDTH + epsilon)
    total = jnp.zeros((rows, columns), f32)
    for b in range(blocks):
        feed = (ends[b] * scale * gain[b : b + 1]).astype(bf16)
        total += jnp.dot(feed, words[b * block : (b + 1) * block], preferred_element_type=f32)
    total = total / (WIDTH / 256.0 * softness[...])
    logits[...] = total
    top = jnp.max(total, axis=1, keepdims=True)
    mass = jnp.sum(jnp.exp(total - top), axis=1, keepdims=True)
    wide[...] = jnp.zeros_like(wide)
    lane = lax.broadcasted_iota(jnp.int32, (rows, LANES), 1)
    wide[0:rows] = jnp.where(lane == 0, top, jnp.where(lane == 1, mass, 0.0))
    turned = wide[...].T
    message[...] = jnp.broadcast_to(turned[None, 0:2, 0:rows], message.shape)


def head_call(order, got, gain, words, softness):
    rows, columns = softness.shape[0], words.shape[1]
    return pl.pallas_call(
        lambda *refs: head_kernel(order, *refs),
        in_specs=[VMEM] * 4,
        out_specs=[VMEM, VMEM],
        out_shape=[shape((rows, columns), f32), shape((got.shape[0], 2, rows), f32)],
        scratch_shapes=[pltpu.VMEM((LANES, LANES), f32)],
        compiler_params=params(),
        cost_estimate=hint(2 * rows * WIDTH * columns, 2 * WIDTH * columns),
        name="head",
    )(got, gain, words, softness)


def body(
    skip_stream_arriving,
    chosen_specialists,
    sequence_piece_tallies,
    premix_rmsnorm_gain,
    dispatcher_weights,
    specialist_switch_weights,
    specialist_expand_weights,
    specialist_contract_weights,
    terminal_rmsnorm_gain,
    lexicon_projector_weights,
    softness_per_sequence,
):
    tokens, block = skip_stream_arriving.shape
    dp, mp = lax.axis_size("dp"), lax.axis_size("mp")
    parts = 4
    spread, sides = dp // parts, mp // parts
    assert dp == parts * spread and mp == parts * sides and sides & (sides - 1) == 0
    part = lax.axis_index("dp") // spread
    y, core = part // 2, part % 2
    side = lax.axis_index("mp") % sides

    def send(value, to):
        pairs = []
        for q in range(parts):
            for r in range(spread):
                for z in range(parts):
                    for x in range(sides):
                        q2, z2, x2 = to(q, z, x)
                        source = (q * spread + r) * mp + z * sides + x
                        pairs.append((source, (q2 * spread + r) * mp + z2 * sides + x2))
        return lax.ppermute(value, ("dp", "mp"), pairs)

    other_core = lambda q, z, x: (q ^ 1, z, x)
    other_y = lambda q, z, x: (q ^ 2, z, x)
    home = lambda q, z, x: (z, q, x)

    scal = jnp.stack([core, side, y]).astype(jnp.int32)
    sent, stream = prep_call(
        skip_stream_arriving.T, premix_rmsnorm_gain[None], chosen_specialists.T, sequence_piece_tallies
    )
    wg, wu, wd = specialist_switch_weights, specialist_expand_weights, specialist_contract_weights
    if spread > 1:
        runs = [[q * spread + r for r in range(spread)] for q in range(parts)]
        wg = lax.all_gather(wg, "dp", axis=1, tiled=True, axis_index_groups=runs)
        wu = lax.all_gather(wu, "dp", axis=1, tiled=True, axis_index_groups=runs)
        wd = lax.all_gather(wd, "dp", axis=2, tiled=True, axis_index_groups=runs)
    wd = jnp.swapaxes(wd, 1, 2)
    depth, hidden = wg.shape[1:]
    base = hidden % LANES
    wr = lax.dynamic_slice_in_dim(dispatcher_weights.T, part * depth, depth, axis=1)
    room = lambda at: jnp.pad(wr, ((at, LANES - at - wr.shape[0]), (0, 0)))
    wr = room(base + 1) + room(base + 1 + EXTRA)

    chunks = ((1,), (2,), (3,), (0,))
    first = [send(sent, lambda q, z, x, i=i: (z, (q - 1) % parts, x ^ i)) for i in range(sides)]
    pair = join_call(first)
    feeds = {1: pair}
    step = lambda v: send(v, lambda q, z, x: (q, (z - 1) % parts, x))
    stream = send(stream, home)
    partial, kept, pieces, shares = {}, {}, {}, {}

    def after(v, dep):
        return lax.optimization_barrier((v, dep))[0]

    def do_partial(s, *deps):
        own, give, cols = partial_call(scal, sides, [feeds[g] for g in chunks[s]], wr, wg, wu, deps)
        partial[s] = (own, send(give, other_core), cols)
        return own

    def do_sum(s, *deps):
        own, recv, _ = partial[s]
        keep, give = sum_call(scal, base, own, recv, deps)
        kept[s] = (keep, send(give, other_y))
        return keep

    def do_act(s, *deps):
        a = act_call(scal, base, *kept[s], partial[s][2], deps)
        pieces[s] = (a, send(a, other_y))
        return a

    def do_hop(s, dep):
        a, a_y = pieces[s]
        late = [v if dep is None else after(v, dep) for v in (a, a_y)]
        pieces[s] = (a, a_y, *[send(v, other_core) for v in late])

    def do_down(s, *deps):
        outs = down_call(scal, sides, pieces[s], partial[s][2], wd, deps)
        got = [outs[0]] + [send(outs[i], lambda q, z, x, i=i: (q, z, x ^ i)) for i in range(1, sides)]
        for n, group in enumerate(chunks[s]):
            to = slice(n * tokens, (n + 1) * tokens)
            if group == 0:
                shares[0] = [v[:, to] for v in got]
            else:
                share = sum(v[:, to].astype(f32) for v in got).astype(bf16)
                back = lambda q, z, x, group=group: (q, (z + group) % parts, x)
                shares[group] = [send(share, back)]
        return outs[0]

    feeds[2] = step(feeds[1])
    feeds[3] = step(feeds[2])
    p0 = do_partial(0)
    p1 = do_partial(1, p0)
    s0 = do_sum(0, p1)
    p2 = do_partial(2, s0)
    feeds[0] = step(after(feeds[3], p2))
    s1 = do_sum(1, p2)
    a0 = do_act(0, s1)
    p3 = do_partial(3, a0)
    s2 = do_sum(2, p3)
    do_hop(0, s2)
    a1 = do_act(1, s2)
    d0 = do_down(0, a1)
    s3 = do_sum(3, d0)
    do_hop(1, s3)
    a2 = do_act(2, s3)
    d1 = do_down(1, a2)
    do_hop(2, None)
    d2 = do_down(2, d1)
    a3 = do_act(3, d2)
    do_hop(3, None)
    d3 = do_down(3, a3)
    terms = [v for group in range(parts) for v in shares[group]]
    total, message = total_call(partial[parts - 1][2], stream, terms, dp * mp)
    exchange = lambda v: lax.all_to_all(v, ("dp", "mp"), 0, 0, tiled=True)
    got, branch = lax.optimization_barrier((exchange(message), send(total, home)))
    order = [
        [(q * spread + r) * mp + group * sides + x for group in range(parts) for r in range(spread)]
        for q in range(parts)
        for x in range(sides)
    ]
    logits, pairs = head_call(
        order,
        got,
        terminal_rmsnorm_gain.reshape(mp, block),
        lexicon_projector_weights,
        softness_per_sequence[:, None],
    )
    pairs = exchange(pairs)
    new_hidden = skip_stream_arriving + branch_scale * branch.T.astype(f32)
    largest = jnp.max(pairs[:, 0], axis=0)
    mass = jnp.sum(pairs[:, 1] * jnp.exp(pairs[:, 0] - largest), axis=0)
    logprobs = logits - largest[:, None] - jnp.log(mass)[:, None]
    return (new_hidden, logprobs)


def solution(mesh):
    return jax.shard_map(
        body,
        mesh=mesh,
        in_specs=(
            P("dp", "mp"),
            P("dp", None),
            P("dp", None),
            P("mp"),
            P(),
            P(None, "dp", "mp"),
            P(None, "dp", "mp"),
            P(None, "mp", "dp"),
            P(),
            P(None, ("dp", "mp")),
            P(),
        ),
        out_specs=(P("dp", "mp"), P(None, ("dp", "mp"))),
        check_vma=False,
    )
```

```python
import math

import jax
import jax.numpy as jnp
from jax import lax
from jax.experimental import pallas as pl
from jax.experimental.pallas import tpu as pltpu
from jax.sharding import PartitionSpec as P

WIDTH = 2304
META = 16
LANES = 128
branch_scale = 1.4 / math.sqrt(40.0)
epsilon = 1e-05
f32, bf16 = jnp.float32, jnp.bfloat16

VMEM = pl.BlockSpec(memory_space=pltpu.VMEM)
SMEM = pl.BlockSpec(memory_space=pltpu.SMEM)
ANY = pl.BlockSpec(memory_space=pl.ANY)


def up_to(n, step=LANES):
    return -(-n // step) * step


def params(mib=16):
    return pltpu.CompilerParams(vmem_limit_bytes=mib * 2**20)


def hint(flops, bytes_accessed, scale=0.3):
    return pl.CostEstimate(int(flops * scale), 0, int(bytes_accessed * scale))


def shape(dims, dtype):
    return jax.ShapeDtypeStruct(dims, dtype)


def prep_kernel(tallies, x, gain, routes, out, ends):
    block, tokens = x.shape
    v = x[...]
    wide = up_to(block)
    g = jnp.concatenate([gain[...], jnp.zeros((1, wide - block), f32)], axis=1)
    g = jnp.broadcast_to(g, (LANES, wide)).T[0:block, 0:1]
    out[0:block] = (v * g).astype(bf16)
    sq = jnp.sum(v * v, axis=0, keepdims=True)
    hi = sq.astype(bf16).astype(f32)
    mid = (sq - hi).astype(bf16).astype(f32)
    here = lax.broadcasted_iota(jnp.int32, (1, tokens), 1)
    mark, end = jnp.zeros((1, tokens), f32), jnp.int32(-1)
    for q in range(ends.shape[0]):
        end = end + tallies[0, q]
        mark = jnp.where(here == end, q + 1.0, mark)
    rows = [routes[...].astype(f32), hi, mid, sq - hi - mid, mark]
    rows.append(jnp.zeros((META - 6, tokens), f32))
    out[block:] = jnp.concatenate(rows, axis=0).astype(bf16)
    ends[...] = columns_at(mark, v)[0 : ends.shape[0]]


def columns_at(mark, v):
    row = lax.broadcasted_iota(jnp.int32, (8, mark.shape[1]), 0)
    pick = jnp.where(mark == (row + 1).astype(f32), 1.0, 0.0)
    return lax.dot_general(
        pick, v, (((1,), (1,)), ((), ())), precision=lax.Precision.HIGHEST, preferred_element_type=f32
    )


def whole_spec(v):
    return pl.BlockSpec(v.shape, lambda *_: (0,) * len(v.shape))


def prep_call(x, gain, routes, tallies):
    block, tokens = x.shape
    reqs = tallies.shape[1]
    outs = [shape((block + META, tokens), bf16), shape((reqs, block), f32)]
    return pl.pallas_call(
        prep_kernel,
        grid=(1,),
        in_specs=[SMEM] + [whole_spec(v) for v in (x, gain, routes)],
        out_specs=[whole_spec(v) for v in outs],
        out_shape=outs,
        compiler_params=params(60),
        cost_estimate=hint(4 * tokens * block, 6 * tokens * block),
        name="prep",
    )(tallies, x, gain, routes)


def join_call(blocks):
    rows, tokens = blocks[0].shape

    def join_kernel(*refs):
        for i, ref in enumerate(refs[:-1]):
            refs[-1][i * rows : (i + 1) * rows] = ref[...]

    return pl.pallas_call(
        join_kernel,
        in_specs=[VMEM] * len(blocks),
        out_specs=VMEM,
        out_shape=shape((len(blocks) * rows, tokens), bf16),
        compiler_params=params(),
        cost_estimate=hint(1, 4 * len(blocks) * rows * tokens),
        name="join",
    )(*blocks)


EXTRA = 5


def spread_lanes(v, base):
    lane = lax.broadcasted_iota(jnp.int32, v.shape, 1)
    hi = v.astype(bf16).astype(f32)
    return jnp.where(lane < base, v, jnp.where(lane < base + EXTRA, hi, v - hi)).astype(bf16)


def joined_lanes(v, base):
    lane = lax.broadcasted_iota(jnp.int32, v.shape, 1)
    left, right = pltpu.roll(v, LANES - EXTRA, 1), pltpu.roll(v, EXTRA, 1)
    return v + jnp.where(lane < base, 0.0, jnp.where(lane < base + EXTRA, left, right))


def slot_columns(core, cols):
    first, second = cols[:, 0:1].astype(f32), cols[:, 1:2].astype(f32)
    zero = core == 0
    return jnp.where(zero, first, second), jnp.where(zero, second, first)


def partial_kernel(sides, held, scal, *refs):
    feeds, (wr, wg, wu) = refs[:held], refs[held : held + 3]
    own, give, cols, xs, xt, acc, extra = refs[-7:]
    e = pl.program_id(0)
    core, side = scal[0], scal[1]
    depth, hidden = wg.shape[1:]
    deep, half = up_to(depth), up_to(hidden)
    base = hidden % LANES
    tokens = feeds[0].shape[1]
    block = depth // sides
    last = slice(2 * half - LANES, 2 * half)

    @pl.when(e == 0)
    def _():
        xs[depth:] = jnp.zeros((deep + LANES - depth, xs.shape[1]), bf16)
        for n, ref in enumerate(feeds):
            to = slice(n * tokens, (n + 1) * tokens)
            for i in range(sides):
                at = i * (block + META)
                xs[pl.ds(pl.multiple_of((side ^ i) * block, 16), block), to] = ref[at : at + block]
                xs[deep + i * META : deep + (i + 1) * META, to] = ref[at + block : at + block + META]
        xt[...] = xs[...].T
        more = xt[:, deep:]
        cols[...] = more
        more = more.astype(f32)
        sq = jnp.zeros((more.shape[0], 1), f32)
        for i in range(sides):
            for term in (4, 3, 2):
                sq = sq + more[:, i * META + term : i * META + term + 1]
        router = lax.dot_general(
            xt[:, 0:depth], wr[...], (((1,), (1,)), ((), ())), preferred_element_type=f32
        )
        lane = lax.broadcasted_iota(jnp.int32, router.shape, 1)
        extra[...] = router + jnp.where((lane == base) | (lane == base + EXTRA), sq, 0.0)
        for ref in (own, acc):
            ref[:, half - LANES : half] = jnp.zeros((xt.shape[0], LANES), f32)
            ref[:, last] = jnp.zeros((xt.shape[0], LANES), f32)

    mine, other = slot_columns(core, xt[:, deep : deep + LANES])
    ef = e.astype(f32)
    take = [(v == ef) | (e == 0) for v in (mine, other)]
    for which, w in enumerate((wg, wu)):
        for at in range(0, hidden, 256):
            end = min(hidden, at + 256)
            d = jnp.dot(xt[:, 0:depth], w[0, :, at:end], preferred_element_type=f32)
            to = slice(which * half + at, which * half + end)
            for ref, pick in ((own, take[0]), (acc, take[1])):
                ref[:, to] = jnp.where(pick, d, ref[:, to])

    @pl.when(e == pl.num_programs(0) - 1)
    def _():
        lane = lax.broadcasted_iota(jnp.int32, extra.shape, 1)
        more = extra[...]
        own[:, last] = jnp.where(lane < base, own[:, last], more)
        give[:, 0 : last.start] = acc[:, 0 : last.start].astype(bf16)
        give[:, last] = spread_lanes(jnp.where(lane < base, acc[:, last], more), base)


def partial_call(scal, sides, feeds, wr, wg, wu, deps):
    experts, depth, hidden = wg.shape
    tokens = feeds[0].shape[1] * len(feeds)
    deep, wide = up_to(depth), 2 * up_to(hidden)
    part = pl.BlockSpec((1, depth, hidden), lambda n: (n, 0, 0))
    outs = [shape((tokens, wide), f32), shape((tokens, wide), bf16), shape((tokens, LANES), bf16)]
    return pl.pallas_call(
        lambda *refs: partial_kernel(sides, len(feeds), *refs),
        grid=(experts,),
        in_specs=[SMEM] + [whole_spec(v) for v in feeds] + [whole_spec(wr), part, part] + [ANY] * len(deps),
        out_specs=[whole_spec(v) for v in outs],
        out_shape=outs,
        scratch_shapes=[
            pltpu.VMEM((deep + LANES, tokens), bf16),
            pltpu.VMEM((tokens, deep + LANES), bf16),
            pltpu.VMEM((tokens, wide), f32),
            pltpu.VMEM((tokens, LANES), f32),
        ],
        compiler_params=params(20),
        cost_estimate=hint(
            4 * experts * depth * hidden * tokens, 4 * experts * depth * hidden + 6 * tokens * wide, 4
        ),
        name="gate_up_partial",
    )(scal, *feeds, wr, wg, wu, *deps)


def sum_kernel(base, scal, own, recv, *refs):
    keep, send = refs[-2:]
    y = scal[2]
    th, wide = keep.shape
    main = wide - LANES
    for to, first in ((keep, y), (send, 1 - y)):
        rows = pl.ds(pl.multiple_of(first * th, th), th)
        to[:, 0:main] = (own[rows, 0:main] + recv[rows, 0:main].astype(f32)).astype(to.dtype)
        v = own[rows, main:] + joined_lanes(recv[rows, main:].astype(f32), base)
        to[:, main:] = v if to is keep else spread_lanes(v, base)


def sum_call(scal, base, own, recv, deps):
    tokens, wide = own.shape
    return pl.pallas_call(
        lambda *refs: sum_kernel(base, *refs),
        in_specs=[SMEM, VMEM, VMEM] + [ANY] * len(deps),
        out_specs=[VMEM, VMEM],
        out_shape=[shape((tokens // 2, wide), f32), shape((tokens // 2, wide), bf16)],
        compiler_params=params(),
        cost_estimate=hint(tokens * wide, 9 * tokens * wide),
        name="core_sum",
    )(scal, own, recv, *deps)


def act_kernel(base, scal, keep, recv, cols, *refs):
    act = refs[-1]
    core, y = scal[0], scal[2]
    th, half = act.shape
    main = 2 * half - LANES
    m = keep[:, main:] + joined_lanes(recv[:, main:].astype(f32), base)
    mine, other = slot_columns(core, cols[pl.ds(pl.multiple_of(y * th, th), th)])
    scale = lax.rsqrt(m[:, base : base + 1] / WIDTH + epsilon)
    la = lb = jnp.zeros_like(scale)
    for e in range(4):
        logit = m[:, base + 1 + e : base + 2 + e] * scale
        la = jnp.where(mine == e, logit, la)
        lb = jnp.where(other == e, logit, lb)
    mix = scale / (1.0 + jnp.exp(lb - la))
    g = (keep[:, 0:half] + recv[:, 0:half].astype(f32)) * scale
    u = (keep[:, half:] + recv[:, half:].astype(f32)) * mix
    act[...] = (g / (1.0 + jnp.exp(-g)) * u).astype(bf16)


def act_call(scal, base, keep, recv, cols, deps):
    th, wide = keep.shape
    return pl.pallas_call(
        lambda *refs: act_kernel(base, *refs),
        in_specs=[SMEM] + [VMEM] * 3 + [ANY] * len(deps),
        out_specs=VMEM,
        out_shape=shape((th, wide // 2), bf16),
        compiler_params=params(),
        cost_estimate=hint(6 * th * wide, 7 * th * wide),
        name="act",
    )(scal, keep, recv, cols, *deps)


def down_kernel(sides, scal, a, a_y, b, b_y, cols, wd, *refs):
    outs = refs[-sides - 2 : -2]
    whole, acc = refs[-2:]
    e = pl.program_id(0)
    core, side, y = scal[0], scal[1], scal[2]
    th = a.shape[0]
    width, hidden = wd.shape[1:]
    block = width // sides

    @pl.when(e == 0)
    def _():
        for k, near, far in ((0, a, a_y), (1, b, b_y)):
            whole[k, pl.ds(pl.multiple_of(y * th, th), th)] = near[...]
            whole[k, pl.ds(pl.multiple_of((1 - y) * th, th), th)] = far[...]

    ef = e.astype(f32)
    masks = [jnp.where(v == ef, 1.0, 0.0).astype(bf16) for v in slot_columns(core, cols[...])]
    rows = whole[0, :, 0:hidden] * masks[0] + whole[1, :, 0:hidden] * masks[1]
    d = lax.dot_general(wd[0], rows, (((1,), (1,)), ((), ())), preferred_element_type=f32)

    @pl.when(e == 0)
    def _():
        acc[...] = d

    @pl.when(e > 0)
    def _():
        acc[...] += d

    @pl.when(e == pl.num_programs(0) - 1)
    def _():
        for i in range(sides):
            rows = pl.ds(pl.multiple_of((side ^ i) * block, 16), block)
            outs[i][...] = acc[rows].astype(bf16)


def down_call(scal, sides, pieces, cols, wd, deps):
    experts, width, hidden = wd.shape
    tokens = cols.shape[0]
    outs = [shape((width // sides, tokens), bf16)] * sides
    return pl.pallas_call(
        lambda *refs: down_kernel(sides, *refs),
        grid=(experts,),
        in_specs=[SMEM]
        + [whole_spec(v) for v in pieces]
        + [whole_spec(cols), pl.BlockSpec((1, width, hidden), lambda n: (n, 0, 0))]
        + [ANY] * len(deps),
        out_specs=[whole_spec(v) for v in outs],
        out_shape=outs,
        scratch_shapes=[
            pltpu.VMEM((2, tokens, pieces[0].shape[1]), bf16),
            pltpu.VMEM((width, tokens), f32),
        ],
        compiler_params=params(20),
        cost_estimate=hint(
            2 * experts * width * hidden * tokens, 2 * experts * width * hidden + 2 * width * tokens, 4
        ),
        name="down",
    )(scal, *pieces, cols, wd, *deps)


def total_kernel(cols, stream, *refs):
    parts, (total, message) = refs[:-2], refs[-2:]
    v = parts[0][...].astype(f32)
    for ref in parts[1:]:
        v = v + ref[...].astype(f32)
    total[...] = v.astype(bf16)
    ends = columns_at(cols[...].astype(f32).T[5:6], v)[0 : stream.shape[0]]
    ends = stream[...] + branch_scale * ends
    message[...] = jnp.broadcast_to(ends[None], message.shape)


def total_call(cols, stream, parts, count):
    reqs, block = stream.shape
    tokens = cols.shape[0]
    outs = [shape((block, tokens), bf16), shape((count, reqs, block), f32)]
    return pl.pallas_call(
        total_kernel,
        grid=(1,),
        in_specs=[whole_spec(v) for v in (cols, stream, *parts)],
        out_specs=[whole_spec(v) for v in outs],
        out_shape=outs,
        compiler_params=params(),
        cost_estimate=hint(16 * block * tokens, 14 * block * tokens),
        name="branch_total",
    )(cols, stream, *parts)


def head_kernel(order, got, gain, words, softness, logits, message, wide):
    blocks, block = gain.shape
    rows, columns = logits.shape
    ends, squares = [], 0.0
    for b in range(blocks):
        v = jnp.concatenate([got[at] for at in order[b]], axis=0)
        squares = squares + jnp.sum(v * v, axis=1, keepdims=True)
        ends.append(v)
    scale = lax.rsqrt(squares / WIDTH + epsilon)
    total = jnp.zeros((rows, columns), f32)
    for b in range(blocks):
        feed = (ends[b] * scale * gain[b : b + 1]).astype(bf16)
        total += jnp.dot(feed, words[b * block : (b + 1) * block], preferred_element_type=f32)
    total = total / (WIDTH / 256.0 * softness[...])
    logits[...] = total
    top = jnp.max(total, axis=1, keepdims=True)
    mass = jnp.sum(jnp.exp(total - top), axis=1, keepdims=True)
    wide[...] = jnp.zeros_like(wide)
    lane = lax.broadcasted_iota(jnp.int32, (rows, LANES), 1)
    wide[0:rows] = jnp.where(lane == 0, top, jnp.where(lane == 1, mass, 0.0))
    turned = wide[...].T
    message[...] = jnp.broadcast_to(turned[None, 0:2, 0:rows], message.shape)


def head_call(order, got, gain, words, softness):
    rows, columns = softness.shape[0], words.shape[1]
    return pl.pallas_call(
        lambda *refs: head_kernel(order, *refs),
        in_specs=[VMEM] * 4,
        out_specs=[VMEM, VMEM],
        out_shape=[shape((rows, columns), f32), shape((got.shape[0], 2, rows), f32)],
        scratch_shapes=[pltpu.VMEM((LANES, LANES), f32)],
        compiler_params=params(),
        cost_estimate=hint(2 * rows * WIDTH * columns, 2 * WIDTH * columns),
        name="head",
    )(got, gain, words, softness)


def body(
    skip_stream_arriving,
    chosen_specialists,
    sequence_piece_tallies,
    premix_rmsnorm_gain,
    dispatcher_weights,
    specialist_switch_weights,
    specialist_expand_weights,
    specialist_contract_weights,
    terminal_rmsnorm_gain,
    lexicon_projector_weights,
    softness_per_sequence,
):
    tokens, block = skip_stream_arriving.shape
    dp, mp = lax.axis_size("dp"), lax.axis_size("mp")
    parts = 4
    spread, sides = dp // parts, mp // parts
    assert dp == parts * spread and mp == parts * sides and sides & (sides - 1) == 0
    part = lax.axis_index("dp") // spread
    y, core = part // 2, part % 2
    side = lax.axis_index("mp") % sides

    def send(value, to):
        pairs = []
        for q in range(parts):
            for r in range(spread):
                for z in range(parts):
                    for x in range(sides):
                        q2, z2, x2 = to(q, z, x)
                        source = (q * spread + r) * mp + z * sides + x
                        pairs.append((source, (q2 * spread + r) * mp + z2 * sides + x2))
        return lax.ppermute(value, ("dp", "mp"), pairs)

    other_core = lambda q, z, x: (q ^ 1, z, x)
    other_y = lambda q, z, x: (q ^ 2, z, x)
    home = lambda q, z, x: (z, q, x)

    scal = jnp.stack([core, side, y]).astype(jnp.int32)
    sent, stream = prep_call(
        skip_stream_arriving.T, premix_rmsnorm_gain[None], chosen_specialists.T, sequence_piece_tallies
    )
    wg, wu, wd = specialist_switch_weights, specialist_expand_weights, specialist_contract_weights
    if spread > 1:
        runs = [[q * spread + r for r in range(spread)] for q in range(parts)]
        wg = lax.all_gather(wg, "dp", axis=1, tiled=True, axis_index_groups=runs)
        wu = lax.all_gather(wu, "dp", axis=1, tiled=True, axis_index_groups=runs)
        wd = lax.all_gather(wd, "dp", axis=2, tiled=True, axis_index_groups=runs)
    wd = jnp.swapaxes(wd, 1, 2)
    depth, hidden = wg.shape[1:]
    base = hidden % LANES
    wr = lax.dynamic_slice_in_dim(dispatcher_weights.T, part * depth, depth, axis=1)
    room = lambda at: jnp.pad(wr, ((at, LANES - at - wr.shape[0]), (0, 0)))
    wr = room(base + 1) + room(base + 1 + EXTRA)

    chunks = ((1,), (2,), (3,), (0,))
    first = [send(sent, lambda q, z, x, i=i: (z, (q - 1) % parts, x ^ i)) for i in range(sides)]
    pair = join_call(first)
    feeds = {1: pair}
    step = lambda v: send(v, lambda q, z, x: (q, (z - 1) % parts, x))
    stream = send(stream, home)
    partial, kept, pieces, shares = {}, {}, {}, {}

    def after(v, dep):
        return lax.optimization_barrier((v, dep))[0]

    def do_partial(s, *deps):
        own, give, cols = partial_call(scal, sides, [feeds[g] for g in chunks[s]], wr, wg, wu, deps)
        partial[s] = (own, send(give, other_core), cols)
        return own

    def do_sum(s, *deps):
        own, recv, _ = partial[s]
        keep, give = sum_call(scal, base, own, recv, deps)
        kept[s] = (keep, send(give, other_y))
        return keep

    def do_act(s, *deps):
        a = act_call(scal, base, *kept[s], partial[s][2], deps)
        pieces[s] = (a, send(a, other_y))
        return a

    def do_hop(s, dep):
        a, a_y = pieces[s]
        late = [v if dep is None else after(v, dep) for v in (a, a_y)]
        pieces[s] = (a, a_y, *[send(v, other_core) for v in late])

    def do_down(s, *deps):
        outs = down_call(scal, sides, pieces[s], partial[s][2], wd, deps)
        got = [outs[0]] + [send(outs[i], lambda q, z, x, i=i: (q, z, x ^ i)) for i in range(1, sides)]
        for n, group in enumerate(chunks[s]):
            to = slice(n * tokens, (n + 1) * tokens)
            if group == 0:
                shares[0] = [v[:, to] for v in got]
            else:
                share = sum(v[:, to].astype(f32) for v in got).astype(bf16)
                back = lambda q, z, x, group=group: (q, (z + group) % parts, x)
                shares[group] = [send(share, back)]
        return outs[0]

    feeds[2] = step(feeds[1])
    feeds[3] = step(feeds[2])
    p0 = do_partial(0)
    p1 = do_partial(1, p0)
    s0 = do_sum(0, p1)
    p2 = do_partial(2, s0)
    feeds[0] = step(after(feeds[3], p2))
    s1 = do_sum(1, p2)
    a0 = do_act(0, s1)
    p3 = do_partial(3, a0)
    s2 = do_sum(2, p3)
    do_hop(0, s2)
    a1 = do_act(1, s2)
    d0 = do_down(0, a1)
    s3 = do_sum(3, d0)
    do_hop(1, s3)
    a2 = do_act(2, s3)
    d1 = do_down(1, a2)
    do_hop(2, None)
    d2 = do_down(2, d1)
    a3 = do_act(3, d2)
    do_hop(3, None)
    d3 = do_down(3, a3)
    terms = [v for group in range(parts) for v in shares[group]]
    total, message = total_call(partial[parts - 1][2], stream, terms, dp * mp)
    exchange = lambda v: lax.all_to_all(v, ("dp", "mp"), 0, 0, tiled=True)
    got = exchange(message)
    branch = send(total, home)
    order = [
        [(q * spread + r) * mp + group * sides + x for group in range(parts) for r in range(spread)]
        for q in range(parts)
        for x in range(sides)
    ]
    logits, pairs = head_call(
        order,
        got,
        terminal_rmsnorm_gain.reshape(mp, block),
        lexicon_projector_weights,
        softness_per_sequence[:, None],
    )
    pairs, branch = lax.optimization_barrier((pairs, branch))
    pairs = exchange(pairs)
    new_hidden = skip_stream_arriving + branch_scale * branch.T.astype(f32)
    largest = jnp.max(pairs[:, 0], axis=0)
    mass = jnp.sum(pairs[:, 1] * jnp.exp(pairs[:, 0] - largest), axis=0)
    logprobs = logits - largest[:, None] - jnp.log(mass)[:, None]
    return (new_hidden, logprobs)


def solution(mesh):
    return jax.shard_map(
        body,
        mesh=mesh,
        in_specs=(
            P("dp", "mp"),
            P("dp", None),
            P("dp", None),
            P("mp"),
            P(),
            P(None, "dp", "mp"),
            P(None, "dp", "mp"),
            P(None, "mp", "dp"),
            P(),
            P(None, ("dp", "mp")),
            P(),
        ),
        out_specs=(P("dp", "mp"), P(None, ("dp", "mp"))),
        check_vma=False,
    )
```

```python
import math

import jax
import jax.numpy as jnp
from jax import lax
from jax.experimental import pallas as pl
from jax.experimental.pallas import tpu as pltpu
from jax.sharding import PartitionSpec as P

WIDTH = 2304
META = 16
LANES = 128
branch_scale = 1.4 / math.sqrt(40.0)
epsilon = 1e-05
f32, bf16 = jnp.float32, jnp.bfloat16

VMEM = pl.BlockSpec(memory_space=pltpu.VMEM)
SMEM = pl.BlockSpec(memory_space=pltpu.SMEM)
ANY = pl.BlockSpec(memory_space=pl.ANY)


def up_to(n, step=LANES):
    return -(-n // step) * step


def params(mib=16):
    return pltpu.CompilerParams(vmem_limit_bytes=mib * 2**20)


def hint(flops, bytes_accessed, scale=0.3):
    return pl.CostEstimate(int(flops * scale), 0, int(bytes_accessed * scale))


def shape(dims, dtype):
    return jax.ShapeDtypeStruct(dims, dtype)


def prep_kernel(tallies, x, gain, routes, out, ends):
    block, tokens = x.shape
    v = x[...]
    wide = up_to(block)
    g = jnp.concatenate([gain[...].reshape(1, block), jnp.zeros((1, wide - block), f32)], axis=1)
    g = jnp.broadcast_to(g, (LANES, wide)).T[0:block, 0:1]
    out[0:block] = (v * g).astype(bf16)
    sq = jnp.sum(v * v, axis=0, keepdims=True)
    hi = sq.astype(bf16).astype(f32)
    mid = (sq - hi).astype(bf16).astype(f32)
    here = lax.broadcasted_iota(jnp.int32, (1, tokens), 1)
    mark, end = jnp.zeros((1, tokens), f32), jnp.int32(-1)
    for q in range(ends.shape[0]):
        end = end + tallies[0, q]
        mark = jnp.where(here == end, q + 1.0, mark)
    rows = [routes[...].astype(f32), hi, mid, sq - hi - mid, mark]
    rows.append(jnp.zeros((META - 6, tokens), f32))
    out[block:] = jnp.concatenate(rows, axis=0).astype(bf16)
    ends[...] = columns_at(mark, v)[0 : ends.shape[0]]


def columns_at(mark, v):
    row = lax.broadcasted_iota(jnp.int32, (8, mark.shape[1]), 0)
    pick = jnp.where(mark == (row + 1).astype(f32), 1.0, 0.0)
    return lax.dot_general(
        pick, v, (((1,), (1,)), ((), ())), precision=lax.Precision.HIGHEST, preferred_element_type=f32
    )


def whole_spec(v):
    return pl.BlockSpec(v.shape, lambda *_: (0,) * len(v.shape))


def prep_call(x, gain, routes, tallies):
    block, tokens = x.shape
    reqs = tallies.shape[1]
    outs = [shape((block + META, tokens), bf16), shape((reqs, block), f32)]
    return pl.pallas_call(
        prep_kernel,
        grid=(1,),
        in_specs=[SMEM] + [whole_spec(v) for v in (x, gain, routes)],
        out_specs=[whole_spec(v) for v in outs],
        out_shape=outs,
        compiler_params=params(60),
        cost_estimate=hint(4 * tokens * block, 6 * tokens * block),
        name="prep",
    )(tallies, x, gain, routes)


def join_call(blocks):
    rows, tokens = blocks[0].shape

    def join_kernel(*refs):
        for i, ref in enumerate(refs[:-1]):
            refs[-1][i * rows : (i + 1) * rows] = ref[...]

    return pl.pallas_call(
        join_kernel,
        in_specs=[VMEM] * len(blocks),
        out_specs=VMEM,
        out_shape=shape((len(blocks) * rows, tokens), bf16),
        compiler_params=params(),
        cost_estimate=hint(1, 4 * len(blocks) * rows * tokens),
        name="join",
    )(*blocks)


EXTRA = 5


def spread_lanes(v, base):
    lane = lax.broadcasted_iota(jnp.int32, v.shape, 1)
    hi = v.astype(bf16).astype(f32)
    return jnp.where(lane < base, v, jnp.where(lane < base + EXTRA, hi, v - hi)).astype(bf16)


def joined_lanes(v, base):
    lane = lax.broadcasted_iota(jnp.int32, v.shape, 1)
    left, right = pltpu.roll(v, LANES - EXTRA, 1), pltpu.roll(v, EXTRA, 1)
    return v + jnp.where(lane < base, 0.0, jnp.where(lane < base + EXTRA, left, right))


def slot_columns(core, cols):
    first, second = cols[:, 0:1].astype(f32), cols[:, 1:2].astype(f32)
    zero = core == 0
    return jnp.where(zero, first, second), jnp.where(zero, second, first)


def partial_kernel(sides, held, scal, *refs):
    feeds, (wr, wg, wu) = refs[:held], refs[held : held + 3]
    own, give, cols, xs, xt, acc, extra = refs[-7:]
    e = pl.program_id(0)
    core, side = scal[0], scal[1]
    depth, hidden = wg.shape[1:]
    deep, half = up_to(depth), up_to(hidden)
    base = hidden % LANES
    tokens = feeds[0].shape[1]
    block = depth // sides
    last = slice(2 * half - LANES, 2 * half)

    @pl.when(e == 0)
    def _():
        xs[depth:] = jnp.zeros((deep + LANES - depth, xs.shape[1]), bf16)
        for n, ref in enumerate(feeds):
            to = slice(n * tokens, (n + 1) * tokens)
            for i in range(sides):
                at = i * (block + META)
                xs[pl.ds(pl.multiple_of((side ^ i) * block, 16), block), to] = ref[at : at + block]
                xs[deep + i * META : deep + (i + 1) * META, to] = ref[at + block : at + block + META]
        xt[...] = xs[...].T
        more = xt[:, deep:]
        cols[...] = more
        more = more.astype(f32)
        sq = jnp.zeros((more.shape[0], 1), f32)
        for i in range(sides):
            for term in (4, 3, 2):
                sq = sq + more[:, i * META + term : i * META + term + 1]
        router = lax.dot_general(
            xt[:, 0:depth], wr[...], (((1,), (1,)), ((), ())), preferred_element_type=f32
        )
        lane = lax.broadcasted_iota(jnp.int32, router.shape, 1)
        extra[...] = router + jnp.where((lane == base) | (lane == base + EXTRA), sq, 0.0)
        for ref in (own, acc):
            ref[:, half - LANES : half] = jnp.zeros((xt.shape[0], LANES), f32)
            ref[:, last] = jnp.zeros((xt.shape[0], LANES), f32)

    mine, other = slot_columns(core, xt[:, deep : deep + LANES])
    ef = e.astype(f32)
    take = [(v == ef) | (e == 0) for v in (mine, other)]
    for which, w in enumerate((wg, wu)):
        for at in range(0, hidden, 256):
            end = min(hidden, at + 256)
            d = jnp.dot(xt[:, 0:depth], w[0, :, at:end], preferred_element_type=f32)
            to = slice(which * half + at, which * half + end)
            for ref, pick in ((own, take[0]), (acc, take[1])):
                ref[:, to] = jnp.where(pick, d, ref[:, to])

    @pl.when(e == pl.num_programs(0) - 1)
    def _():
        lane = lax.broadcasted_iota(jnp.int32, extra.shape, 1)
        more = extra[...]
        own[:, last] = jnp.where(lane < base, own[:, last], more)
        give[:, 0 : last.start] = acc[:, 0 : last.start].astype(bf16)
        give[:, last] = spread_lanes(jnp.where(lane < base, acc[:, last], more), base)


def partial_call(scal, sides, feeds, wr, wg, wu, deps):
    experts, depth, hidden = wg.shape
    tokens = feeds[0].shape[1] * len(feeds)
    deep, wide = up_to(depth), 2 * up_to(hidden)
    part = pl.BlockSpec((1, depth, hidden), lambda n: (n, 0, 0))
    outs = [shape((tokens, wide), f32), shape((tokens, wide), bf16), shape((tokens, LANES), bf16)]
    return pl.pallas_call(
        lambda *refs: partial_kernel(sides, len(feeds), *refs),
        grid=(experts,),
        in_specs=[SMEM] + [whole_spec(v) for v in feeds] + [whole_spec(wr), part, part] + [ANY] * len(deps),
        out_specs=[whole_spec(v) for v in outs],
        out_shape=outs,
        scratch_shapes=[
            pltpu.VMEM((deep + LANES, tokens), bf16),
            pltpu.VMEM((tokens, deep + LANES), bf16),
            pltpu.VMEM((tokens, wide), f32),
            pltpu.VMEM((tokens, LANES), f32),
        ],
        compiler_params=params(20),
        cost_estimate=hint(
            4 * experts * depth * hidden * tokens, 4 * experts * depth * hidden + 6 * tokens * wide, 4
        ),
        name="gate_up_partial",
    )(scal, *feeds, wr, wg, wu, *deps)


def sum_kernel(base, scal, own, recv, *refs):
    keep, send = refs[-2:]
    y = scal[2]
    th, wide = keep.shape
    main = wide - LANES
    for to, first in ((keep, y), (send, 1 - y)):
        rows = pl.ds(pl.multiple_of(first * th, th), th)
        to[:, 0:main] = (own[rows, 0:main] + recv[rows, 0:main].astype(f32)).astype(to.dtype)
        v = own[rows, main:] + joined_lanes(recv[rows, main:].astype(f32), base)
        to[:, main:] = v if to is keep else spread_lanes(v, base)


def sum_call(scal, base, own, recv, deps):
    tokens, wide = own.shape
    return pl.pallas_call(
        lambda *refs: sum_kernel(base, *refs),
        in_specs=[SMEM, VMEM, VMEM] + [ANY] * len(deps),
        out_specs=[VMEM, VMEM],
        out_shape=[shape((tokens // 2, wide), f32), shape((tokens // 2, wide), bf16)],
        compiler_params=params(),
        cost_estimate=hint(tokens * wide, 9 * tokens * wide),
        name="core_sum",
    )(scal, own, recv, *deps)


def act_kernel(base, scal, keep, recv, cols, *refs):
    act = refs[-1]
    core, y = scal[0], scal[2]
    th, half = act.shape
    main = 2 * half - LANES
    m = keep[:, main:] + joined_lanes(recv[:, main:].astype(f32), base)
    mine, other = slot_columns(core, cols[pl.ds(pl.multiple_of(y * th, th), th)])
    scale = lax.rsqrt(m[:, base : base + 1] / WIDTH + epsilon)
    la = lb = jnp.zeros_like(scale)
    for e in range(4):
        logit = m[:, base + 1 + e : base + 2 + e] * scale
        la = jnp.where(mine == e, logit, la)
        lb = jnp.where(other == e, logit, lb)
    mix = scale / (1.0 + jnp.exp(lb - la))
    g = (keep[:, 0:half] + recv[:, 0:half].astype(f32)) * scale
    u = (keep[:, half:] + recv[:, half:].astype(f32)) * mix
    act[...] = (g / (1.0 + jnp.exp(-g)) * u).astype(bf16)


def act_call(scal, base, keep, recv, cols, deps):
    th, wide = keep.shape
    return pl.pallas_call(
        lambda *refs: act_kernel(base, *refs),
        in_specs=[SMEM] + [VMEM] * 3 + [ANY] * len(deps),
        out_specs=VMEM,
        out_shape=shape((th, wide // 2), bf16),
        compiler_params=params(),
        cost_estimate=hint(6 * th * wide, 7 * th * wide),
        name="act",
    )(scal, keep, recv, cols, *deps)


def down_kernel(sides, scal, a, a_y, b, b_y, cols, wd, *refs):
    outs = refs[-sides - 2 : -2]
    whole, acc = refs[-2:]
    e = pl.program_id(0)
    core, side, y = scal[0], scal[1], scal[2]
    th = a.shape[0]
    width, hidden = wd.shape[1:]
    block = width // sides

    @pl.when(e == 0)
    def _():
        for k, near, far in ((0, a, a_y), (1, b, b_y)):
            whole[k, pl.ds(pl.multiple_of(y * th, th), th)] = near[...]
            whole[k, pl.ds(pl.multiple_of((1 - y) * th, th), th)] = far[...]

    ef = e.astype(f32)
    masks = [jnp.where(v == ef, 1.0, 0.0).astype(bf16) for v in slot_columns(core, cols[...])]
    rows = whole[0, :, 0:hidden] * masks[0] + whole[1, :, 0:hidden] * masks[1]
    d = lax.dot_general(wd[0], rows, (((1,), (1,)), ((), ())), preferred_element_type=f32)

    @pl.when(e == 0)
    def _():
        acc[...] = d

    @pl.when(e > 0)
    def _():
        acc[...] += d

    @pl.when(e == pl.num_programs(0) - 1)
    def _():
        for i in range(sides):
            rows = pl.ds(pl.multiple_of((side ^ i) * block, 16), block)
            outs[i][...] = acc[rows].astype(bf16)


def down_call(scal, sides, pieces, cols, wd, deps):
    experts, width, hidden = wd.shape
    tokens = cols.shape[0]
    outs = [shape((width // sides, tokens), bf16)] * sides
    return pl.pallas_call(
        lambda *refs: down_kernel(sides, *refs),
        grid=(experts,),
        in_specs=[SMEM]
        + [whole_spec(v) for v in pieces]
        + [whole_spec(cols), pl.BlockSpec((1, width, hidden), lambda n: (n, 0, 0))]
        + [ANY] * len(deps),
        out_specs=[whole_spec(v) for v in outs],
        out_shape=outs,
        scratch_shapes=[
            pltpu.VMEM((2, tokens, pieces[0].shape[1]), bf16),
            pltpu.VMEM((width, tokens), f32),
        ],
        compiler_params=params(20),
        cost_estimate=hint(
            2 * experts * width * hidden * tokens, 2 * experts * width * hidden + 2 * width * tokens, 4
        ),
        name="down",
    )(scal, *pieces, cols, wd, *deps)


def total_kernel(cols, stream, *refs):
    parts, (total, message) = refs[:-2], refs[-2:]
    v = parts[0][...].astype(f32)
    for ref in parts[1:]:
        v = v + ref[...].astype(f32)
    total[...] = v.astype(bf16)
    ends = columns_at(cols[...].astype(f32).T[5:6], v)[0 : stream.shape[0]]
    ends = stream[...] + branch_scale * ends
    message[...] = jnp.broadcast_to(ends[None], message.shape)


def total_call(cols, stream, parts, count):
    reqs, block = stream.shape
    tokens = cols.shape[0]
    outs = [shape((block, tokens), bf16), shape((count, reqs, block), f32)]
    return pl.pallas_call(
        total_kernel,
        grid=(1,),
        in_specs=[whole_spec(v) for v in (cols, stream, *parts)],
        out_specs=[whole_spec(v) for v in outs],
        out_shape=outs,
        compiler_params=params(),
        cost_estimate=hint(16 * block * tokens, 14 * block * tokens),
        name="branch_total",
    )(cols, stream, *parts)


def head_kernel(order, got, gain, words, softness, logits, message, wide):
    blocks, block = gain.shape
    rows, columns = logits.shape
    ends, squares = [], 0.0
    for b in range(blocks):
        v = jnp.concatenate([got[at] for at in order[b]], axis=0)
        squares = squares + jnp.sum(v * v, axis=1, keepdims=True)
        ends.append(v)
    scale = lax.rsqrt(squares / WIDTH + epsilon)
    total = jnp.zeros((rows, columns), f32)
    for b in range(blocks):
        feed = (ends[b] * scale * gain[b : b + 1]).astype(bf16)
        total += jnp.dot(feed, words[b * block : (b + 1) * block], preferred_element_type=f32)
    total = total / (WIDTH / 256.0 * softness[...])
    logits[...] = total
    top = jnp.max(total, axis=1, keepdims=True)
    mass = jnp.sum(jnp.exp(total - top), axis=1, keepdims=True)
    wide[...] = jnp.zeros_like(wide)
    lane = lax.broadcasted_iota(jnp.int32, (rows, LANES), 1)
    wide[0:rows] = jnp.where(lane == 0, top, jnp.where(lane == 1, mass, 0.0))
    turned = wide[...].T
    message[...] = jnp.broadcast_to(turned[None, 0:2, 0:rows], message.shape)


def head_call(order, got, gain, words, softness):
    rows, columns = softness.shape[0], words.shape[1]
    return pl.pallas_call(
        lambda *refs: head_kernel(order, *refs),
        in_specs=[VMEM] * 4,
        out_specs=[VMEM, VMEM],
        out_shape=[shape((rows, columns), f32), shape((got.shape[0], 2, rows), f32)],
        scratch_shapes=[pltpu.VMEM((LANES, LANES), f32)],
        compiler_params=params(),
        cost_estimate=hint(2 * rows * WIDTH * columns, 2 * WIDTH * columns),
        name="head",
    )(got, gain, words, softness)


def body(
    skip_stream_arriving,
    chosen_specialists,
    sequence_piece_tallies,
    premix_rmsnorm_gain,
    dispatcher_weights,
    specialist_switch_weights,
    specialist_expand_weights,
    specialist_contract_weights,
    terminal_rmsnorm_gain,
    lexicon_projector_weights,
    softness_per_sequence,
):
    tokens, block = skip_stream_arriving.shape
    dp, mp = lax.axis_size("dp"), lax.axis_size("mp")
    parts = 4
    spread, sides = dp // parts, mp // parts
    assert dp == parts * spread and mp == parts * sides and sides & (sides - 1) == 0
    part = lax.axis_index("dp") // spread
    y, core = part // 2, part % 2
    side = lax.axis_index("mp") % sides

    def send(value, to):
        pairs = []
        for q in range(parts):
            for r in range(spread):
                for z in range(parts):
                    for x in range(sides):
                        q2, z2, x2 = to(q, z, x)
                        source = (q * spread + r) * mp + z * sides + x
                        pairs.append((source, (q2 * spread + r) * mp + z2 * sides + x2))
        return lax.ppermute(value, ("dp", "mp"), pairs)

    other_core = lambda q, z, x: (q ^ 1, z, x)
    other_y = lambda q, z, x: (q ^ 2, z, x)
    home = lambda q, z, x: (z, q, x)

    scal = jnp.stack([core, side, y]).astype(jnp.int32)
    sent, stream = prep_call(
        skip_stream_arriving.T, premix_rmsnorm_gain, chosen_specialists.T, sequence_piece_tallies
    )
    wg, wu, wd = specialist_switch_weights, specialist_expand_weights, specialist_contract_weights
    if spread > 1:
        runs = [[q * spread + r for r in range(spread)] for q in range(parts)]
        wg = lax.all_gather(wg, "dp", axis=1, tiled=True, axis_index_groups=runs)
        wu = lax.all_gather(wu, "dp", axis=1, tiled=True, axis_index_groups=runs)
        wd = lax.all_gather(wd, "dp", axis=2, tiled=True, axis_index_groups=runs)
    wd = jnp.swapaxes(wd, 1, 2)
    depth, hidden = wg.shape[1:]
    base = hidden % LANES
    wr = lax.dynamic_slice_in_dim(dispatcher_weights.T, part * depth, depth, axis=1)
    room = lambda at: jnp.pad(wr, ((at, LANES - at - wr.shape[0]), (0, 0)))
    wr = room(base + 1) + room(base + 1 + EXTRA)

    chunks = ((1,), (2,), (3,), (0,))
    first = [send(sent, lambda q, z, x, i=i: (z, (q - 1) % parts, x ^ i)) for i in range(sides)]
    pair = join_call(first)
    feeds = {1: pair}
    step = lambda v: send(v, lambda q, z, x: (q, (z - 1) % parts, x))
    stream = send(stream, home)
    partial, kept, pieces, shares = {}, {}, {}, {}

    def after(v, dep):
        return lax.optimization_barrier((v, dep))[0]

    def do_partial(s, *deps):
        own, give, cols = partial_call(scal, sides, [feeds[g] for g in chunks[s]], wr, wg, wu, deps)
        partial[s] = (own, send(give, other_core), cols)
        return own

    def do_sum(s, *deps):
        own, recv, _ = partial[s]
        keep, give = sum_call(scal, base, own, recv, deps)
        kept[s] = (keep, send(give, other_y))
        return keep

    def do_act(s, *deps):
        a = act_call(scal, base, *kept[s], partial[s][2], deps)
        pieces[s] = (a, send(a, other_y))
        return a

    def do_hop(s, dep):
        a, a_y = pieces[s]
        late = [v if dep is None else after(v, dep) for v in (a, a_y)]
        pieces[s] = (a, a_y, *[send(v, other_core) for v in late])

    def do_down(s, *deps):
        outs = down_call(scal, sides, pieces[s], partial[s][2], wd, deps)
        got = [outs[0]] + [send(outs[i], lambda q, z, x, i=i: (q, z, x ^ i)) for i in range(1, sides)]
        for n, group in enumerate(chunks[s]):
            to = slice(n * tokens, (n + 1) * tokens)
            if group == 0:
                shares[0] = [v[:, to] for v in got]
            else:
                share = sum(v[:, to].astype(f32) for v in got).astype(bf16)
                back = lambda q, z, x, group=group: (q, (z + group) % parts, x)
                shares[group] = [send(share, back)]
        return outs[0]

    feeds[2] = step(feeds[1])
    feeds[3] = step(feeds[2])
    p0 = do_partial(0)
    p1 = do_partial(1, p0)
    s0 = do_sum(0, p1)
    p2 = do_partial(2, s0)
    feeds[0] = step(after(feeds[3], p2))
    s1 = do_sum(1, p2)
    a0 = do_act(0, s1)
    p3 = do_partial(3, a0)
    s2 = do_sum(2, p3)
    do_hop(0, s2)
    a1 = do_act(1, s2)
    d0 = do_down(0, a1)
    s3 = do_sum(3, d0)
    do_hop(1, s3)
    a2 = do_act(2, s3)
    d1 = do_down(1, a2)
    do_hop(2, None)
    d2 = do_down(2, d1)
    a3 = do_act(3, d2)
    do_hop(3, None)
    d3 = do_down(3, a3)
    terms = [v for group in range(parts) for v in shares[group]]
    total, message = total_call(partial[parts - 1][2], stream, terms, dp * mp)
    exchange = lambda v: lax.all_to_all(v, ("dp", "mp"), 0, 0, tiled=True)
    got = exchange(message)
    branch = send(total, home)
    order = [
        [(q * spread + r) * mp + group * sides + x for group in range(parts) for r in range(spread)]
        for q in range(parts)
        for x in range(sides)
    ]
    logits, pairs = head_call(
        order,
        got,
        terminal_rmsnorm_gain.reshape(mp, block),
        lexicon_projector_weights,
        softness_per_sequence[:, None],
    )
    pairs, branch = lax.optimization_barrier((pairs, branch))
    pairs = exchange(pairs)
    new_hidden = skip_stream_arriving + branch_scale * branch.T.astype(f32)
    largest = jnp.max(pairs[:, 0], axis=0)
    mass = jnp.sum(pairs[:, 1] * jnp.exp(pairs[:, 0] - largest), axis=0)
    logprobs = logits - largest[:, None] - jnp.log(mass)[:, None]
    return (new_hidden, logprobs)


def solution(mesh):
    return jax.shard_map(
        body,
        mesh=mesh,
        in_specs=(
            P("dp", "mp"),
            P("dp", None),
            P("dp", None),
            P("mp"),
            P(),
            P(None, "dp", "mp"),
            P(None, "dp", "mp"),
            P(None, "mp", "dp"),
            P(),
            P(None, ("dp", "mp")),
            P(),
        ),
        out_specs=(P("dp", "mp"), P(None, ("dp", "mp"))),
        check_vma=False,
    )
```
